32 devices in a mesh: groups: 2 (over y), curve: 4 (over z), sub: 2 (over x), pair: 2 (over core).
Axes of the slice: x: 2, y: 2, z: 4, core: 2. Of those that a mesh axis runs over, the one named last changes fastest.
Arguments:
- state: float32 [16384, 512], P(('groups', 'curve', 'sub', 'pair')), parts along dimension 0, may hold values from -6 to 6
- velocity: float32 [3, 16384], P(None, ('groups', 'curve', 'sub', 'pair')), parts along dimension 1, may hold values from -4 to 4
- levels: int32 [16384], P(('groups', 'curve', 'sub', 'pair')), parts along dimension 0, may hold values from 0 to 3
- neighbours: int32 [6, 16384], P(None, ('groups', 'curve', 'sub', 'pair')), parts along dimension 1, may hold values from -1 to 8191, as said below
- records: int32 [4, 8192], P(None, ('groups', 'curve', 'sub', 'pair')), parts along dimension 1, may hold values from 0 to 511, as said below
- counts: int32 [32, 8], P(('groups', 'curve', 'sub', 'pair')), parts along dimension 0, may hold values from 0 to 32, as said below
- stiffness: bfloat16 [512, 1536], replicated, may hold values from -0.25 to 0.25
- trace_map: bfloat16 [512, 384], replicated, may hold values from -0.25 to 0.25
- lift: bfloat16 [384, 512], replicated, may hold values from -0.75 to 0.75
- projection: bfloat16 [64, 512], replicated, may hold values from -0.75 to 0.75
Outputs:
- stepped: float32 [16384, 512], P(('groups', 'curve', 'sub', 'pair')), parts along dimension 0
The draws below stay inside these ranges and needn't reach their ends.
There are 2 independent parts, one for each index of `groups`. The reference program is written for one: setup_inputs(seed, part) draws one part's arguments, and reference() takes and returns one part's arrays. A program takes and returns all parts, laid end to end along the dimension named above; an argument that names none is the same for every part. Nothing has to cross between parts.
Inputs may be any that keep to these rules, and one draw needn't show every extreme that they name: `neighbours`: A neighbour is -1 or an element of the same partition, one of the last 64 elements of the partition before it, or one of the first 64 elements of the partition after it; both ends are reached. `records`: rows 0 and 3 hold element numbers within a partition, row 1 a face 0 to 5, row 2 a projection id 0 to 7. The columns of partition s are its slots ordered by offset index j, then slot k. counts[s, j] is 0 exactly where s + o_j lies outside 0 to 15, else 1 to 32; some partition receives 32 live records from each of its nearby partitions.
All inputs are finite; a program needn't handle non-finite values.
Results may differ from the reference program's by a relative error of at most 0.0046.
Values may be sent and summed in bfloat16 or wider, within the bound.
No kernel may reach another device: no remote copies, remote signals or barrier semaphores. Data moves between devices by JAX's collectives and lax.ppermute only.
A program may use at most 64 MiB of HBM per device.

```python
import jax
import jax.numpy as jnp
from jax import lax

MODES = 512
FACE_MODES = 64
E_DEV = 512
RIM = 64
REACH = 4
OFFSETS = 8
CAP = 32
PARTITIONS = 16
ELEMENTS = 8192
RECORDS = 4096


def draw_neighbours(key, part):
    key = jax.random.fold_in(key, 11)
    pick_key, edge_key = jax.random.split(key)
    element = jnp.arange(ELEMENTS, dtype=jnp.int32)[None, :]
    faces = jnp.arange(6, dtype=jnp.int32)[:, None]
    owner = element // E_DEV
    within = element % E_DEV
    offset = jax.random.randint(pick_key, (6, ELEMENTS), 0, E_DEV + 2 * RIM, dtype=jnp.int32)
    chosen = owner * E_DEV - RIM + offset
    edge = jax.random.randint(edge_key, (6, ELEMENTS), 0, 4, dtype=jnp.int32) == 0
    keep = (chosen >= 0) & (chosen < ELEMENTS) & jnp.logical_not(edge)
    result = jnp.where(keep, chosen, -1)
    lower_end = (faces == 0) & (within == 0) & (owner > 0)
    upper_end = (faces == 1) & (within == E_DEV - 1) & (owner < PARTITIONS - 1)
    result = jnp.where(lower_end, element - RIM, result)
    result = jnp.where(upper_end, element + RIM, result)
    return result.astype(jnp.int32)


def draw_records(key, part):
    key = jax.random.fold_in(key, 23)
    keys = jax.random.split(key, 4)
    source = jax.random.randint(keys[0], (RECORDS,), 0, E_DEV, dtype=jnp.int32)
    facing = jax.random.randint(keys[1], (RECORDS,), 0, 6, dtype=jnp.int32)
    kind = jax.random.randint(keys[2], (RECORDS,), 0, 8, dtype=jnp.int32)
    target = jax.random.randint(keys[3], (RECORDS,), 0, E_DEV, dtype=jnp.int32)
    return jnp.stack([source, facing, kind, target], axis=0).astype(jnp.int32)


def draw_counts(key, part):
    key = jax.random.fold_in(key, 37)
    keys = jax.random.split(key, 4)
    source = jnp.arange(PARTITIONS, dtype=jnp.int32)[:, None]
    index = jnp.arange(OFFSETS, dtype=jnp.int32)[None, :]
    offset = index - REACH + (index >= REACH).astype(jnp.int32)
    destination = source + offset
    inside = (destination >= 0) & (destination < PARTITIONS)
    busy = jax.random.randint(keys[0], (PARTITIONS, OFFSETS), 0, 2, dtype=jnp.int32) == 0
    heavy = jax.random.randint(keys[1], (PARTITIONS, OFFSETS), CAP // 2, CAP + 1, dtype=jnp.int32)
    light = jax.random.randint(keys[2], (PARTITIONS, OFFSETS), 1, CAP // 2 + 1, dtype=jnp.int32)
    filled = jax.random.randint(keys[3], (), 0, PARTITIONS, dtype=jnp.int32)
    value = jnp.where(destination == filled, CAP, jnp.where(busy, heavy, light))
    return jnp.where(inside, value, 0).astype(jnp.int32)


def plant(array, stream_key, smallest, high):
    longest = array.shape.index(max(array.shape))
    spots = []
    for shift in (0, 1):
        where = [jax.random.randint(jax.random.fold_in(stream_key, axis), (), 0, length) for axis, length in enumerate(array.shape)]
        where[longest] = (where[longest] + shift) % array.shape[longest]
        spots.append(tuple(where))
    return array.at[spots[0]].set(smallest).at[spots[1]].set(high)


def block_levels(own_key, extent, shards, smallest, top_value):
    def one(axis_at, shards_of):
        draws = jax.random.uniform(jax.random.fold_in(jax.random.fold_in(own_key, 6), axis_at), (shards_of,), jnp.float32, smallest / len(shards), top_value / len(shards))
        return jnp.repeat(jnp.exp(draws), extent[axis_at] // shards_of).reshape((-1,) + (1,) * (len(extent) - axis_at - 1))

    level = one(*shards[0])
    for cut in shards[1:]:
        level = level * one(*cut)
    return level


def noise(rng, extent, deviation, bound, cuts=(), held_as=jnp.bfloat16):
    array = deviation * jax.random.normal(rng, extent, jnp.float32)
    if cuts:
        array = array * block_levels(rng, extent, cuts, -0.22, 0.18)
    return jnp.clip(array, -bound, bound).astype(held_as)


def setup_inputs(seed: int = 0, part: int = 0) -> dict:
    streams_of = jax.random.split(jax.random.key(seed), 11)
    own_keys = jax.random.split(jax.random.fold_in(streams_of[10], part), 11)
    state = noise(own_keys[0], (ELEMENTS, MODES), 1.0, 6.0, ((0, 16),), jnp.float32)
    velocity = noise(own_keys[1], (3, ELEMENTS), 1.0, 4.0, ((1, 16),), jnp.float32)
    levels = plant(jax.random.randint(own_keys[2], (ELEMENTS,), 0, 4), jax.random.fold_in(own_keys[2], 1), 0, 3).astype(jnp.int32)
    neighbours = draw_neighbours(jax.random.fold_in(jax.random.fold_in(streams_of[10], part), 71), part)
    records = draw_records(jax.random.fold_in(jax.random.fold_in(streams_of[10], part), 71), part)
    counts = draw_counts(jax.random.fold_in(jax.random.fold_in(streams_of[10], part), 71), part)
    stiffness = noise(streams_of[6], (MODES, 3 * MODES), MODES ** -0.5, 0.25)
    trace_map = noise(streams_of[7], (MODES, 6 * FACE_MODES), MODES ** -0.5, 0.25)
    lift = noise(streams_of[8], (6 * FACE_MODES, MODES), FACE_MODES ** -0.5, 0.75)
    projection = noise(streams_of[9], (FACE_MODES, 8 * FACE_MODES), FACE_MODES ** -0.5, 0.75)
    return {"state": state, "velocity": velocity, "levels": levels, "neighbours": neighbours, "records": records, "counts": counts, "stiffness": stiffness, "trace_map": trace_map, "lift": lift, "projection": projection}


time_step = 0.3


def inflow_speeds(velocity):
    ahead = jnp.maximum(velocity, 0.0)
    behind = jnp.maximum(-velocity, 0.0)
    return jnp.stack([ahead[0], behind[0], ahead[1], behind[1], ahead[2], behind[2]], axis=1)


def tendency(field, velocity, levels, neighbours, records, counts, stiffness, trace_map, lift, projection):
    elements = field.shape[0]
    face_modes = projection.shape[0]
    lowered = field.astype(jnp.bfloat16)
    moved = jnp.dot(lowered, stiffness, preferred_element_type=jnp.float32).reshape(elements, 3, -1)
    volume = velocity[0][:, None] * moved[:, 0] + velocity[1][:, None] * moved[:, 1] + velocity[2][:, None] * moved[:, 2]
    traces = jnp.dot(lowered, trace_map, preferred_element_type=jnp.float32).astype(jnp.bfloat16)
    flat = traces.reshape(elements * 6, face_modes)
    faces = jnp.arange(6, dtype=jnp.int32)[:, None]
    valid = neighbours >= 0
    index = jnp.where(valid, neighbours * 6 + jnp.bitwise_xor(faces, 1), 0).astype(jnp.int32)
    conforming = jnp.where(valid[:, :, None], flat[index].astype(jnp.float32), 0.0)
    conforming = jnp.transpose(conforming, (1, 0, 2))
    slots = CAP * OFFSETS
    slot_ids = jnp.arange(slots, dtype=jnp.int32)
    kinds = jnp.arange(8, dtype=jnp.int32)[None, :]
    offset_index = slot_ids // CAP
    offset_value = offset_index - REACH + (offset_index >= REACH).astype(jnp.int32)

    def one_source(source, total):
        block = lax.dynamic_slice_in_dim(records, (source * slots).astype(jnp.int32), slots, 1)
        allowed = lax.dynamic_slice_in_dim(counts, source.astype(jnp.int32), 1, 0)[0]
        rows = flat[(source * E_DEV + block[0]) * 6 + block[1]]
        every = jnp.dot(rows, projection, preferred_element_type=jnp.float32).reshape(slots, 8, face_modes)
        select = (block[2][:, None] == kinds).astype(jnp.float32)
        piece = jnp.sum(every * select[:, :, None], axis=1).astype(jnp.bfloat16)
        target_part = source + offset_value
        live = (slot_ids % CAP) < allowed[offset_index]
        target = jnp.where(live, (target_part * E_DEV + block[3]) * 6 + jnp.bitwise_xor(block[1], 1), elements * 6).astype(jnp.int32)
        return total.at[target].add(piece.astype(jnp.float32))

    mortar = lax.fori_loop(0, PARTITIONS, one_source, jnp.zeros((elements * 6 + 1, face_modes), jnp.float32))
    mortar = mortar[:-1].reshape(elements, 6, face_modes)
    own = traces.reshape(elements, 6, face_modes).astype(jnp.float32)
    speeds = inflow_speeds(velocity)
    flux = (speeds[:, :, None] * (conforming + mortar - own)).astype(jnp.bfloat16).reshape(elements, -1)
    lifted = jnp.dot(flux, lift, preferred_element_type=jnp.float32)
    scale = jnp.exp2(levels.astype(jnp.float32)) * 0.25
    return scale[:, None] * (volume + lifted)


def reference(state, velocity, levels, neighbours, records, counts, stiffness, trace_map, lift, projection):
    extra = (velocity, levels, neighbours, records, counts, stiffness, trace_map, lift, projection)
    first = state + time_step * tendency(state, *extra)
    second = first + time_step * tendency(first, *extra)
    return 0.5 * state + 0.5 * second
```

```python
import functools

import jax
import jax.numpy as jnp
from jax import lax
from jax.experimental import pallas as pl
from jax.experimental.pallas import tpu as pltpu
from jax.sharding import PartitionSpec as P

time_step = 0.3
bf16 = jnp.bfloat16
f32 = jnp.float32
CURVE = ("curve", "sub", "pair")


def dot(a, b):
    return jnp.dot(a, b, preferred_element_type=f32)


def columns_of(*rows):
    stacked = jnp.concatenate([row.astype(f32) for row in rows], axis=0)
    pad = jnp.zeros((128 - stacked.shape[0], stacked.shape[1]), f32)
    return jnp.concatenate([stacked, pad], axis=0).T


def lanes(shape):
    return lax.broadcasted_iota(jnp.int32, shape, 1)


def rows_of(shape):
    return lax.broadcasted_iota(jnp.int32, shape, 0)


def swapped(tile):
    turned = pltpu.roll(tile.astype(f32), 64, 1)
    low = lanes(turned.shape) < 64
    top = jnp.where(low, turned, 0.0).astype(bf16)
    bottom = jnp.where(low, 0.0, turned).astype(bf16)
    return jnp.concatenate([top, bottom], axis=0)


def hot(column, width):
    rows = column.shape[0]
    picked = column.astype(jnp.int32) == lanes((rows, width))
    return jnp.where(picked, 1.0, 0.0).astype(bf16)


def send(traces, roles, counts, records, projection, traces_out, first_out, own_out, blocks):
    elements, width = traces.shape
    slots = records.shape[1]
    capacity = slots // 8
    rim = elements // 8
    traces_out[...] = traces
    column = columns_of(records[...])
    shape = (slots, 128)
    source = column[:, 0:1]
    face = jnp.broadcast_to(column[:, 1:2], shape).astype(jnp.int32)
    kind = jnp.broadcast_to(column[:, 2:3], shape).astype(jnp.int32)
    target = jnp.broadcast_to(column[:, 3:4], shape).astype(jnp.int32)
    picked = dot(hot(source, elements), traces)
    lane = lanes(shape)
    half = lane // 64
    parts = [
        jnp.where(half + 2 * t == face, picked[:, 128 * t : 128 * t + 128], 0.0).astype(bf16)
        for t in range(width // 128)
    ]
    rows = jnp.concatenate(parts, axis=1)
    every = dot(rows, jnp.concatenate([projection[...]] * (width // 64), axis=0))
    folded = jnp.zeros(shape, f32)
    for t in range(4):
        folded = jnp.where(half + 2 * t == kind, every[:, 128 * t : 128 * t + 128], folded)
    piece = folded + pltpu.roll(folded, 64, 1)
    slot = rows_of(shape)
    allowed = jnp.zeros(shape, jnp.int32)
    for j in range(8):
        allowed = jnp.where(slot // capacity == j, counts[0, j], allowed)
    live = slot % capacity < allowed
    facing = jnp.where(live, jnp.bitwise_xor(face, 1) + 1, 0)
    code = jnp.where(lane == 64, target // 16, jnp.where(lane == 65, target % 16, facing))
    code = jnp.where(lane < 67, code, 0).astype(f32)
    blocks[...] = jnp.where(lane < 64, piece, code).astype(bf16)

    def block(role):
        return blocks[pl.ds(pl.multiple_of(roles[role] * capacity, capacity), capacity), :]

    final_at = pl.multiple_of(roles[8] * rim, rim)
    other_at = pl.multiple_of(roles[9] * rim, rim)
    first_out[0:rim, :] = traces_out[pl.ds(final_at, rim), :]
    first_out[rim : 2 * rim, :] = traces_out[pl.ds(other_at, rim), :]
    at = 2 * rim
    for t in range(3):
        first_out[at : at + capacity, 128 * t : 128 * t + 128] = block(t)
    at += capacity
    first_out[at : at + capacity, 0:128] = block(3)
    first_out[at : at + capacity, 128:] = jnp.zeros((capacity, width - 128), bf16)
    for t in range(4):
        own_out[capacity * t : capacity * t + capacity, :] = block(4 + t)


def start_kernel(roles, counts, state, records, trace_map, projection, traces_out, first_out, own_out, blocks):
    traces = dot(state[...].astype(bf16), trace_map[...]).astype(bf16)
    send(traces, roles, counts, records, projection, traces_out, first_out, own_out, blocks)


def local_kernel(weights, roles, *refs):
    if len(weights) == 3:
        state, field, velocity, levels, neighbours, stiffness, traces, base_out, partial_out = refs
    else:
        field, velocity, levels, neighbours, stiffness, traces, base_out, partial_out = refs
        state = None
    elements, modes = field.shape
    column = columns_of(velocity[...], levels[...], neighbours[...])
    scale = jnp.exp2(column[:, 3:4]) * (0.25 * weights[-1])
    lowered = field[...].astype(bf16)
    step = 256
    for n in range(0, modes, step):
        volume = jnp.zeros((elements, step), f32)
        for d in range(3):
            volume += column[:, d : d + 1] * dot(lowered, stiffness[:, d * modes + n : d * modes + n + step])
        base = weights[-2] * field[:, n : n + step] + scale * volume
        if state is not None:
            base += weights[0] * state[:, n : n + step]
        base_out[:, n : n + step] = base
    start = (roles[10] * elements).astype(f32)
    for t in range(3):
        tile = traces[:, 128 * t : 128 * t + 128]
        picks = [hot(column[:, 4 + 2 * t + i : 5 + 2 * t + i] - start, elements) for i in range(2)]
        near = dot(jnp.concatenate(picks, axis=1), swapped(tile))
        partial_out[:, 128 * t : 128 * t + 128] = near - tile.astype(f32)


def finished(weight, roles, velocity, levels, neighbours, lift, base, partial, got, got_even, got_odd, got_a, got_b, arrived):
    elements = base.shape[0]
    rim = elements // 8
    capacity = arrived.shape[0] // 8
    at = 2 * rim
    column = columns_of(velocity[...], levels[...], neighbours[...])
    arrived[0:capacity, :] = got[at : at + capacity, 0:128]
    for i, ref in enumerate((got_even, got_odd)):
        for k in range(2):
            to = capacity * (1 + 2 * i + k)
            arrived[to : to + capacity, :] = ref[rim : rim + capacity, 128 * k : 128 * k + 128]
    arrived[5 * capacity : 6 * capacity, :] = got_a[0:capacity, :]
    arrived[6 * capacity : 7 * capacity, :] = got_b[0:capacity, :]
    far = jnp.where(roles[12] > 0, got_a[capacity : 2 * capacity, :], got_b[capacity : 2 * capacity, :])
    arrived[7 * capacity :, :] = far
    forward = jnp.where(roles[11] > 0, got_even[0:rim, :], got_odd[0:rim, :])
    window = jnp.concatenate([got[0:rim, :], forward], axis=0)
    pieces = arrived[...]
    shape = (128, 128)
    source_lane = rows_of(shape)
    face_of = jnp.where(source_lane == 66, 1.0, 0.0).astype(bf16)
    face = dot(pieces, face_of).astype(jnp.int32) - 1
    small = (8, 128)
    element_of = jnp.where(lanes(small) == 64, 16.0, jnp.where(lanes(small) == 65, 1.0, 0.0)).astype(bf16)
    target = lax.dot_general(element_of, pieces, (((1,), (1,)), ((), ())), preferred_element_type=f32)[0:1, :]
    slots = pieces.shape[0]
    element_hot = jnp.where(rows_of((elements, slots)) == target.astype(jnp.int32), 1.0, 0.0).astype(bf16)
    half = lanes((slots, 128)) // 64
    plain = jnp.where(half == 0, pieces.astype(f32), 0.0)
    both = plain + pltpu.roll(plain, 64, 1)
    placed = jnp.concatenate([jnp.where(half + 2 * t == face, both, 0.0).astype(bf16) for t in range(3)], axis=1)
    mortar = dot(element_hot, placed)
    start = (roles[10] * elements).astype(f32)
    before = roles[13].astype(f32)
    after = roles[14].astype(f32)
    low = lanes((elements, 128)) < 64
    fluxes = []
    for t in range(3):
        picks = []
        for i in range(2):
            raw = column[:, 4 + 2 * t + i : 5 + 2 * t + i]
            local = raw - start
            index = jnp.where(local < 0, local + before, jnp.where(local >= elements, local - after, -1.0))
            picks.append(hot(jnp.where(raw < 0, -1.0, index), 2 * rim))
        near = dot(jnp.concatenate(picks, axis=1), swapped(window[:, 128 * t : 128 * t + 128]))
        speed = column[:, t : t + 1]
        inflow = jnp.maximum(jnp.where(low, speed, -speed), 0.0)
        total = partial[:, 128 * t : 128 * t + 128] + near + mortar[:, 128 * t : 128 * t + 128]
        fluxes.append((inflow * total).astype(bf16))
    lifted = dot(jnp.concatenate(fluxes, axis=1), lift[...])
    scale = jnp.exp2(column[:, 3:4]) * (0.25 * weight)
    return base[...] + scale * lifted


def middle_kernel(
    roles, counts, velocity, levels, neighbours, lift, base, partial, got, got_even, got_odd, got_a, got_b,
    records, trace_map, projection, field_out, traces_out, first_out, own_out, arrived, blocks
):
    field = finished(
        time_step, roles, velocity, levels, neighbours, lift, base, partial, got, got_even, got_odd, got_a, got_b, arrived
    )
    field_out[...] = field
    traces = dot(field.astype(bf16), trace_map[...]).astype(bf16)
    send(traces, roles, counts, records, projection, traces_out, first_out, own_out, blocks)


def end_kernel(
    roles, velocity, levels, neighbours, lift, base, partial, got, got_even, got_odd, got_a, got_b, field_out, arrived
):
    field_out[...] = finished(
        0.5 * time_step, roles, velocity, levels, neighbours, lift, base, partial, got, got_even, got_odd, got_a, got_b, arrived
    )


def paired(count, step, lower):
    partner = {}
    for s in range(count):
        if lower(s) and s + step < count:
            partner[s] = s + step
            partner[s + step] = s
    rest = [s for s in range(count) if s not in partner]
    for a, b in zip(rest[::2], rest[1::2]):
        partner[a] = b
        partner[b] = a
    return sorted(partner.items())


def call(kernel, out_shape, scratch, scalars, flops, *operands):
    specs = [pl.BlockSpec(memory_space=pltpu.SMEM)] * scalars
    specs += [pl.BlockSpec(memory_space=pltpu.VMEM)] * (len(operands) - scalars)
    read = sum(x.size * x.dtype.itemsize for x in operands)
    return pl.pallas_call(
        kernel,
        out_shape=out_shape,
        in_specs=specs,
        out_specs=[pl.BlockSpec(memory_space=pltpu.VMEM)] * len(out_shape),
        scratch_shapes=scratch,
        compiler_params=pltpu.CompilerParams(vmem_limit_bytes=40 * 1024 * 1024),
        cost_estimate=pl.CostEstimate(flops=flops, bytes_accessed=read, transcendentals=0),
    )(*operands)


def exchange(first, own, chip, core, rim, capacity):
    count = lax.axis_size(CURVE)
    got = lax.ppermute(first, CURVE, paired(count, 1, lambda s: s % 2 == 0))
    forward = got[rim : 2 * rim]
    at = 2 * rim
    up = got[at : at + capacity, 128:256]
    down = got[at : at + capacity, 256:384]
    far = got[at + capacity : at + 2 * capacity, 0:128]
    blank = jnp.zeros_like(up)
    even = chip % 2 == 0
    upper = ((chip // 2) % 2 == 0) == (core == 0)
    mine = [own[capacity * t : capacity * t + capacity] for t in range(4)]

    def near(block, other):
        return jnp.concatenate([forward, jnp.concatenate([block, other, blank], axis=1)], axis=0)

    to_even = near(mine[0], jnp.where(even, up, down))
    to_odd = near(mine[1], jnp.where(even, down, up))
    to_a = jnp.concatenate([mine[2], jnp.where(upper, far, 0)], axis=0)
    to_b = jnp.concatenate([mine[3], jnp.where(upper, 0, far)], axis=0)
    return (
        got,
        lax.ppermute(to_even, CURVE, paired(count, 2, lambda s: (s // 2) % 2 == 0)),
        lax.ppermute(to_odd, CURVE, paired(count, 2, lambda s: (s // 2) % 2 == 1)),
        lax.ppermute(to_a, CURVE, paired(count, 4, lambda s: (s // 4) % 2 == 0)),
        lax.ppermute(to_b, CURVE, paired(count, 4, lambda s: (s // 4) % 2 == 1)),
    )


def body(
    state, velocity, levels, neighbours, records, counts, stiffness, trace_map, lift, projection
):
    elements, modes = state.shape
    width = trace_map.shape[1]
    slots = records.shape[1]
    capacity = slots // counts.shape[1]
    rim = elements // 8
    chip = lax.axis_index(("curve", "sub"))
    core = lax.axis_index("pair")
    position = 2 * chip + core
    even = chip % 2 == 0
    second = (chip // 2) % 2 == 0
    first_core = core == 0

    def pick(which, a, b):
        return jnp.where(which, a, b)

    roles = jnp.stack(
        [
            pick(first_core, 4, 3),
            pick(first_core, 6, 4),
            pick(first_core, 3, 1),
            pick(first_core, 1, 6),
            pick(even, 5, 2),
            pick(even, 2, 5),
            pick(second, 7, 0),
            pick(second, 0, 7),
            pick(first_core, 7, 0),
            pick(first_core, 0, 7),
            position,
            pick(even == first_core, 0, 1),
            pick(second == first_core, 0, 1),
            pick(first_core, 2 * rim, rim),
            pick(first_core, elements, elements - rim),
            0,
        ]
    ).astype(jnp.int32)
    levels = levels.reshape(1, elements)

    def array(shape, dtype):
        return jax.ShapeDtypeStruct(shape, dtype)

    sent = [
        array((elements, width), bf16),
        array((2 * rim + 2 * capacity, width), bf16),
        array((4 * capacity, 128), bf16),
    ]
    whole = array((elements, modes), f32)
    partial_shape = array((elements, width), f32)
    blocks = pltpu.VMEM((slots, 128), bf16)
    arrived = pltpu.VMEM((slots, 128), bf16)

    traces, first, own = call(
        start_kernel, sent, [blocks], 2, 2 * 10**8, roles, counts, state, records, trace_map, projection
    )
    got = exchange(first, own, chip, core, rim, capacity)
    base, partial = call(
        functools.partial(local_kernel, (1.0, time_step)), [whole, partial_shape], [], 1, 3 * 10**9,
        roles, state, velocity, levels, neighbours, stiffness, traces,
    )
    field, traces, first, own = call(
        middle_kernel, [whole] + sent, [arrived, blocks], 2, 10**9,
        roles, counts, velocity, levels, neighbours, lift, base, partial, *got, records, trace_map, projection,
    )
    got = exchange(first, own, chip, core, rim, capacity)
    base, partial = call(
        functools.partial(local_kernel, (0.5, 0.5, 0.5 * time_step)), [whole, partial_shape], [], 1, 3 * 10**9,
        roles, state, field, velocity, levels, neighbours, stiffness, traces,
    )
    return call(
        end_kernel, [whole], [arrived], 1, 10**9,
        roles, velocity, levels, neighbours, lift, base, partial, *got,
    )[0]


def solution(mesh):
    placed = (
        P(("groups", "curve", "sub", "pair"), None),
        P(None, ("groups", "curve", "sub", "pair")),
        P(("groups", "curve", "sub", "pair")),
        P(None, ("groups", "curve", "sub", "pair")),
        P(None, ("groups", "curve", "sub", "pair")),
        P(("groups", "curve", "sub", "pair"), None),
        P(),
        P(),
        P(),
        P(),
    )
    return jax.shard_map(
        body,
        mesh=mesh,
        in_specs=placed,
        out_specs=P(("groups", "curve", "sub", "pair"), None),
        check_vma=False,
    )
```

```python
import jax
import jax.numpy as jnp
from jax import lax
from jax.experimental import pallas as pl
from jax.experimental.pallas import tpu as pltpu
from jax.sharding import PartitionSpec as P

time_step = 0.3
bf16 = jnp.bfloat16
f32 = jnp.float32
CURVE = ("curve", "sub", "pair")


def dot(a, b):
    return jnp.dot(a, b, preferred_element_type=f32)


def transposed(rows):
    pad = jnp.zeros((128 - rows.shape[0], rows.shape[1]), f32)
    return jnp.concatenate([rows, pad], axis=0).T


def lanes(shape):
    return lax.broadcasted_iota(jnp.int32, shape, 1)


def rows_of(shape):
    return lax.broadcasted_iota(jnp.int32, shape, 0)


def swapped(tile):
    turned = pltpu.roll(tile.astype(f32), 64, 1)
    low = lanes(turned.shape) < 64
    top = jnp.where(low, turned, 0.0).astype(bf16)
    bottom = jnp.where(low, 0.0, turned).astype(bf16)
    return jnp.concatenate([top, bottom], axis=0)


def hot(column, width):
    rows = column.shape[0]
    picked = column.astype(jnp.int32) == lanes((rows, width))
    return jnp.where(picked, 1.0, 0.0).astype(bf16)


def place():
    return lax.axis_index("curve") * lax.axis_size("sub") + lax.axis_index("sub"), lax.axis_index("pair")


def record_columns(records, counts):
    slots = records.shape[1]
    capacity = slots // 8
    source, face, kind, target = (records[i : i + 1, :] for i in range(4))
    slot = lanes((1, slots))
    allowed = jnp.zeros((1, slots), jnp.int32)
    for j in range(8):
        inside = (slot >= j * capacity) & (slot < (j + 1) * capacity)
        allowed = jnp.where(inside, counts[:, j : j + 1] + j * capacity, allowed)
    facing = jnp.where(slot < allowed, jnp.bitwise_xor(face, 1) + 1, 0)
    digits = [lax.shift_right_logical(target, 4), jnp.bitwise_and(target, 15), facing]
    gap = jnp.zeros((61, slots), f32)
    rows = [x.astype(f32) for x in (source, face, kind)] + [gap] + [x.astype(f32) for x in digits]
    return transposed(jnp.concatenate(rows, axis=0))


def send(traces, source_hot, column, projection, first_out, own_out, blocks):
    elements, width = traces.shape
    slots = column.shape[0]
    capacity = slots // 8
    rim = elements // 8
    chip, core = place()
    own = lax.rem(chip, 2)
    second = lax.rem(lax.div(chip, 2), 2)
    shape = (slots, 128)
    lane = lanes(shape)
    half = jnp.where(lane < 64, 0.0, 1.0)
    picked = dot(source_hot, traces[...])
    face = column[:, 1:2]
    row = jnp.zeros(shape, f32)
    for t in range(3):
        row = jnp.where(half + 2 * t == face, picked[:, 128 * t : 128 * t + 128], row)
    every = dot(row.astype(bf16), jnp.concatenate([projection[...]] * 2, axis=0))
    kind = column[:, 2:3]
    folded = jnp.zeros(shape, f32)
    for t in range(4):
        folded = jnp.where(half + 2 * t == kind, every[:, 128 * t : 128 * t + 128], folded)
    piece = folded + pltpu.roll(folded, 64, 1)
    blocks[...] = jnp.where(lane < 64, piece, column[...]).astype(bf16)

    def block(index):
        return blocks[pl.ds(pl.multiple_of(index * capacity, capacity), capacity), :]

    def pick(which, a, b):
        return a + which * (b - a)

    final_at = pl.multiple_of(pick(core, elements - rim, 0), rim)
    other_at = pl.multiple_of(pick(core, 0, elements - rim), rim)
    first_out[0:rim, :] = traces[pl.ds(final_at, rim), :]
    first_out[rim : 2 * rim, :] = traces[pl.ds(other_at, rim), :]
    at = 2 * rim
    for t, (a, b) in enumerate(((4, 3), (6, 4), (3, 1))):
        first_out[at : at + capacity, 128 * t : 128 * t + 128] = block(pick(core, a, b))
    at += capacity
    first_out[at : at + capacity, 0:128] = block(pick(core, 1, 6))
    first_out[at : at + capacity, 128:] = jnp.zeros((capacity, width - 128), bf16)
    for t, (which, a, b) in enumerate(((own, 5, 2), (own, 2, 5), (second, 7, 0), (second, 0, 7))):
        own_out[capacity * t : capacity * t + capacity, :] = block(pick(which, a, b))


def start_kernel(
    state_in, trace_map_in, records_in, counts_in, velocity_in, levels_in, neighbours_in, projection_in,
    trace_map, projection, traces, first_out, own_out, source_hot, column, elements_column,
    state, records, counts, velocity, levels, neighbours, blocks, sems
):
    elements = state.shape[0]
    part = elements // 2
    pairs = [(trace_map_in, trace_map)]
    for i in range(2):
        cut = pl.ds(i * part, part)
        pairs.append((state_in.at[cut], state.at[cut]))
    pairs += [(records_in, records), (counts_in, counts), (velocity_in, velocity), (levels_in, levels)]
    pairs += [(neighbours_in, neighbours), (projection_in, projection)]
    copies = [pltpu.make_async_copy(a, b, sems.at[i]) for i, (a, b) in enumerate(pairs)]
    for copy in copies:
        copy.start()
    for copy in copies[3:]:
        copy.wait()
    columns = record_columns(records, counts)
    column[...] = columns
    source_hot[...] = hot(columns[:, 0:1], elements)
    elements_column[...] = element_columns(velocity, levels, neighbours)
    copies[0].wait()
    for i in range(2):
        copies[1 + i].wait()
        cut = slice(i * part, i * part + part)
        traces[cut, :] = dot(state[cut, :].astype(bf16), trace_map[...]).astype(bf16)
    send(traces, source_hot[...], column, projection, first_out, own_out, blocks)


def element_columns(velocity, levels, neighbours):
    elements = velocity.shape[1]
    rim = elements // 8
    chip, core = place()
    raw = neighbours[...].astype(f32)
    local = raw - ((2 * chip + core) * elements).astype(f32)
    before = ((2 - core) * rim).astype(f32)
    after = (elements - core * rim).astype(f32)
    index = jnp.where(local < 0, local + before, jnp.where(local >= elements, local - after, -1.0))
    index = jnp.where(raw < 0, -1.0, index)
    scale = jnp.exp2(levels[...].astype(f32)) * 0.25
    gap = jnp.zeros((4, elements), f32)
    return transposed(jnp.concatenate([velocity[...], scale, gap, local, gap[0:2], index], axis=0))


def volume_term(column, lowered, stiffness, n, step):
    modes = stiffness.shape[0]
    volume = jnp.zeros((lowered.shape[0], step), f32)
    for d in range(3):
        volume += column[:, d : d + 1] * dot(lowered, stiffness[:, d * modes + n : d * modes + n + step])
    return column[:, 3:4] * volume


def own_part(column, traces, partial_out):
    elements = traces.shape[0]
    for t in range(3):
        tile = traces[:, 128 * t : 128 * t + 128]
        at = 8 + 2 * t
        picks = [hot(column[:, at + i : at + i + 1], elements) for i in range(2)]
        near = dot(jnp.concatenate(picks, axis=1), swapped(tile))
        partial_out[:, 128 * t : 128 * t + 128] = near - tile.astype(f32)


def local_kernel(stiffness_in, lift_in, column, state, traces, stiffness, lift, base, partial, inflow, picks, sems):
    elements, modes = state.shape
    rim = elements // 8
    copies = [
        pltpu.make_async_copy(stiffness_in, stiffness, sems.at[0]),
        pltpu.make_async_copy(lift_in, lift, sems.at[1]),
    ]
    for copy in copies:
        copy.start()
    columns = column[...]
    own_part(columns, traces, partial)
    low = lanes((elements, 128)) < 64
    for t in range(3):
        speed = columns[:, t : t + 1]
        inflow[:, 128 * t : 128 * t + 128] = columns[:, 3:4] * jnp.maximum(jnp.where(low, speed, -speed), 0.0)
    for i in range(6):
        picks[:, 2 * rim * i : 2 * rim * i + 2 * rim] = hot(columns[:, 16 + i : 17 + i], 2 * rim)
    lowered = state[...].astype(bf16)
    step = 256
    copies[0].wait()
    for n in range(0, modes, step):
        base[:, n : n + step] = state[:, n : n + step] + time_step * volume_term(columns, lowered, stiffness, n, step)
    copies[1].wait()


def second_local_kernel(column, state, field, stiffness, traces, base, partial):
    modes = state.shape[1]
    columns = column[...]
    lowered = field[...].astype(bf16)
    step = 256
    for n in range(0, modes, step):
        volume = volume_term(columns, lowered, stiffness, n, step)
        base[:, n : n + step] = 0.5 * (state[:, n : n + step] + field[:, n : n + step]) + 0.5 * time_step * volume
    own_part(columns, traces, partial)


def gather_arrivals(got, got_even, got_odd, got_a, got_b, arrived):
    capacity = arrived.shape[0] // 8
    rim = 2 * capacity
    at = 2 * rim
    chip, core = place()
    own = lax.rem(chip, 2)
    second = lax.rem(lax.div(chip, 2), 2)
    arrived[0:capacity, :] = got[at : at + capacity, 0:128]
    for i, ref in enumerate((got_even, got_odd)):
        for k in range(2):
            to = capacity * (1 + 2 * i + k)
            arrived[to : to + capacity, :] = ref[rim : rim + capacity, 128 * k : 128 * k + 128]
    arrived[5 * capacity : 6 * capacity, :] = got_a[0:capacity, :]
    arrived[6 * capacity : 7 * capacity, :] = got_b[0:capacity, :]
    arrived[7 * capacity :, :] = jnp.where(
        second != core, got_a[capacity : 2 * capacity, :], got_b[capacity : 2 * capacity, :]
    )
    forward = jnp.where(own != core, got_even[0:rim, :], got_odd[0:rim, :])
    return jnp.concatenate([got[0:rim, :], forward], axis=0)


def targets(pieces, elements):
    face_of = jnp.where(rows_of((128, 128)) == 66, 1.0, 0.0).astype(bf16)
    face = dot(pieces, face_of) - 1.0
    lane = lanes((8, 128))
    element_of = jnp.where(lane == 64, 16.0, jnp.where(lane == 65, 1.0, 0.0)).astype(bf16)
    target = lax.dot_general(element_of, pieces, (((1,), (1,)), ((), ())), preferred_element_type=f32)[0:1, :]
    match = rows_of((elements, pieces.shape[0])) == target.astype(jnp.int32)
    return face, jnp.where(match, 1.0, 0.0).astype(bf16)


def fluxes(pieces, face, element_hot, window, partial, inflow, picks):
    half = jnp.where(lanes(pieces.shape) < 64, 0.0, 1.0)
    plain = jnp.where(half == 0.0, pieces.astype(f32), 0.0)
    both = plain + pltpu.roll(plain, 64, 1)
    parts = []
    for t in range(3):
        cut = slice(128 * t, 128 * t + 128)
        placed = jnp.where(half + 2 * t == face, both, 0.0).astype(bf16)
        near = dot(picks[:, 256 * t : 256 * t + 256], swapped(window[:, cut]))
        mortar = dot(element_hot, placed)
        parts.append((inflow[:, cut] * (partial[:, cut] + near + mortar)).astype(bf16))
    return jnp.concatenate(parts, axis=1)


def middle_kernel(
    lift, base, partial, inflow, picks, got, got_even, got_odd, got_a, got_b, trace_map, projection, source_hot, column,
    field, traces, first_out, own_out, face_out, element_hot_out, arrived, blocks
):
    elements = base.shape[0]
    window = gather_arrivals(got, got_even, got_odd, got_a, got_b, arrived)
    pieces = arrived[...]
    face, element_hot = targets(pieces, elements)
    face_out[...] = face
    element_hot_out[...] = element_hot
    flux = fluxes(pieces, face, element_hot, window, partial, inflow, picks)
    new = base[...] + time_step * dot(flux, lift[...])
    field[...] = new
    traces[...] = dot(new.astype(bf16), trace_map[...]).astype(bf16)
    send(traces, source_hot[...], column, projection, first_out, own_out, blocks)


def end_kernel(
    lift, base, partial, inflow, picks, got, got_even, got_odd, got_a, got_b, face, element_hot, field, arrived, result, sems
):
    elements = base.shape[0]
    window = gather_arrivals(got, got_even, got_odd, got_a, got_b, arrived)
    flux = fluxes(arrived[...], face[...], element_hot[...], window, partial, inflow, picks)
    part = elements // 2
    copies = []
    for i in range(2):
        cut = slice(i * part, i * part + part)
        result[cut, :] = base[cut, :] + 0.5 * time_step * dot(flux[cut, :], lift[...])
        rows = pl.ds(i * part, part)
        copies.append(pltpu.make_async_copy(result.at[rows], field.at[rows], sems.at[i]))
        copies[i].start()
    for copy in copies:
        copy.wait()


def paired(count, step, lower):
    partner = {}
    for s in range(count):
        if lower(s) and s + step < count:
            partner[s] = s + step
            partner[s + step] = s
    rest = [s for s in range(count) if s not in partner]
    for a, b in zip(rest[::2], rest[1::2]):
        partner[a] = b
        partner[b] = a
    return sorted(partner.items())


def call(kernel, out_shape, scratch, flops, far, near, out_space=pltpu.VMEM):
    operands = [pltpu.with_memory_space_constraint(x, pltpu.HBM) for x in far] + list(near)
    read = sum(x.size * x.dtype.itemsize for x in operands)
    specs = [pl.BlockSpec(memory_space=pl.ANY)] * len(far) + [pl.BlockSpec(memory_space=pltpu.VMEM)] * len(near)
    return pl.pallas_call(
        kernel,
        out_shape=out_shape,
        in_specs=specs,
        out_specs=[pl.BlockSpec(memory_space=out_space)] * len(out_shape),
        scratch_shapes=scratch,
        compiler_params=pltpu.CompilerParams(vmem_limit_bytes=16 * 1024 * 1024),
        cost_estimate=pl.CostEstimate(flops=flops, bytes_accessed=read, transcendentals=0),
    )(*operands)


def exchange(first, own, chip, core, rim, capacity):
    count = lax.axis_size(CURVE)
    got = lax.ppermute(first, CURVE, paired(count, 1, lambda s: s % 2 == 0))
    forward = got[rim : 2 * rim]
    at = 2 * rim
    up = got[at : at + capacity, 128:256]
    down = got[at : at + capacity, 256:384]
    far = got[at + capacity : at + 2 * capacity, 0:128]
    blank = jnp.zeros_like(up)
    even = chip % 2 == 0
    upper = ((chip // 2) % 2 == 0) == (core == 0)
    mine = [own[capacity * t : capacity * t + capacity] for t in range(4)]

    def near(block, other):
        return jnp.concatenate([forward, jnp.concatenate([block, other, blank], axis=1)], axis=0)

    to_even = near(mine[0], jnp.where(even, up, down))
    to_odd = near(mine[1], jnp.where(even, down, up))
    to_a = jnp.concatenate([mine[2], jnp.where(upper, far, 0)], axis=0)
    to_b = jnp.concatenate([mine[3], jnp.where(upper, 0, far)], axis=0)
    return (
        got,
        lax.ppermute(to_even, CURVE, paired(count, 2, lambda s: (s // 2) % 2 == 0)),
        lax.ppermute(to_odd, CURVE, paired(count, 2, lambda s: (s // 2) % 2 == 1)),
        lax.ppermute(to_a, CURVE, paired(count, 4, lambda s: (s // 4) % 2 == 0)),
        lax.ppermute(to_b, CURVE, paired(count, 4, lambda s: (s // 4) % 2 == 1)),
    )


def body(
    state, velocity, levels, neighbours, records, counts, stiffness, trace_map, lift, projection
):
    elements, modes = state.shape
    width = trace_map.shape[1]
    slots = records.shape[1]
    capacity = slots // counts.shape[1]
    rim = elements // 8
    chip, core = place()

    def array(shape, dtype):
        return jax.ShapeDtypeStruct(shape, dtype)

    def like(x):
        return array(x.shape, x.dtype)

    sent = [
        array((elements, width), bf16),
        array((2 * rim + 2 * capacity, width), bf16),
        array((4 * capacity, 128), bf16),
    ]
    whole = array((elements, modes), f32)
    faces = array((elements, width), f32)
    blocks = pltpu.VMEM((slots, 128), bf16)
    column_shape = array((slots, 128), f32)

    levels = levels.reshape(1, elements)
    vmem = pltpu.VMEM
    wide = (elements, 128)
    trace_map, projection, traces, first, own, source_hot, column, element_column = call(
        start_kernel,
        [like(trace_map), like(projection)]
        + sent
        + [array((slots, elements), bf16), column_shape, array(wide, f32)],
        [vmem(x.shape, x.dtype) for x in (state, records, counts, velocity, levels, neighbours)]
        + [blocks, pltpu.SemaphoreType.DMA((9,))],
        2 * 10**8,
        (state, trace_map, records, counts, velocity, levels, neighbours, projection),
        (),
    )
    got = exchange(first, own, chip, core, rim, capacity)
    stiffness, lift, base, partial, inflow, picks = call(
        local_kernel,
        [like(stiffness), like(lift), whole, faces, faces, array((elements, 12 * rim), bf16)],
        [pltpu.SemaphoreType.DMA((2,))],
        3 * 10**9,
        (stiffness, lift),
        (element_column, state, traces),
    )
    field, traces, first, own, face, element_hot = call(
        middle_kernel,
        [whole] + sent + [column_shape, array((elements, slots), bf16)],
        [blocks, blocks],
        10**9,
        (),
        (lift, base, partial, inflow, picks, *got, trace_map, projection, source_hot, column),
    )
    got = exchange(first, own, chip, core, rim, capacity)
    base, partial = call(
        second_local_kernel, [whole, faces], [], 3 * 10**9, (), (element_column, state, field, stiffness, traces)
    )
    return call(
        end_kernel,
        [whole],
        [blocks, vmem((elements, modes), f32), pltpu.SemaphoreType.DMA((2,))],
        10**9,
        (),
        (lift, base, partial, inflow, picks, *got, face, element_hot),
        out_space=pl.ANY,
    )[0]


def solution(mesh):
    placed = (
        P(("groups", "curve", "sub", "pair"), None),
        P(None, ("groups", "curve", "sub", "pair")),
        P(("groups", "curve", "sub", "pair")),
        P(None, ("groups", "curve", "sub", "pair")),
        P(None, ("groups", "curve", "sub", "pair")),
        P(("groups", "curve", "sub", "pair"), None),
        P(),
        P(),
        P(),
        P(),
    )
    return jax.shard_map(
        body,
        mesh=mesh,
        in_specs=placed,
        out_specs=P(("groups", "curve", "sub", "pair"), None),
        check_vma=False,
    )
```

```python
import jax
import jax.numpy as jnp
from jax import lax
from jax.experimental import pallas as pl
from jax.experimental.pallas import tpu as pltpu
from jax.sharding import PartitionSpec as P

time_step = 0.3
bf16 = jnp.bfloat16
f32 = jnp.float32
CURVE = ("curve", "sub", "pair")


def dot(a, b):
    return jnp.dot(a, b, preferred_element_type=f32)


def transposed(rows):
    pad = jnp.zeros((128 - rows.shape[0], rows.shape[1]), f32)
    return jnp.concatenate([rows, pad], axis=0).T


def lanes(shape):
    return lax.broadcasted_iota(jnp.int32, shape, 1)


def rows_of(shape):
    return lax.broadcasted_iota(jnp.int32, shape, 0)


def swapped(tile):
    turned = pltpu.roll(tile.astype(f32), 64, 1)
    low = lanes(turned.shape) < 64
    top = jnp.where(low, turned, 0.0).astype(bf16)
    bottom = jnp.where(low, 0.0, turned).astype(bf16)
    return jnp.concatenate([top, bottom], axis=0)


def hot(column, width):
    rows = column.shape[0]
    picked = column.astype(jnp.int32) == lanes((rows, width))
    return jnp.where(picked, 1.0, 0.0).astype(bf16)


def place():
    return lax.axis_index("curve") * lax.axis_size("sub") + lax.axis_index("sub"), lax.axis_index("pair")


def record_columns(records, counts):
    slots = records.shape[1]
    capacity = slots // 8
    source, face, kind, target = (records[i : i + 1, :] for i in range(4))
    slot = lanes((1, slots))
    allowed = jnp.zeros((1, slots), jnp.int32)
    for j in range(8):
        inside = (slot >= j * capacity) & (slot < (j + 1) * capacity)
        allowed = jnp.where(inside, counts[:, j : j + 1] + j * capacity, allowed)
    facing = jnp.where(slot < allowed, jnp.bitwise_xor(face, 1) + 1, 0)
    digits = [lax.shift_right_logical(target, 4), jnp.bitwise_and(target, 15), facing]
    gap = jnp.zeros((61, slots), f32)
    rows = [x.astype(f32) for x in (source, face, kind)] + [gap] + [x.astype(f32) for x in digits]
    return transposed(jnp.concatenate(rows, axis=0))


def send(traces, source_hot, column, projection, first_out, rim_out, own_out, blocks):
    elements, width = traces.shape
    slots = column.shape[0]
    capacity = slots // 8
    rim = elements // 8
    chip, core = place()
    own = lax.rem(chip, 2)
    second = lax.rem(lax.div(chip, 2), 2)
    shape = (slots, 128)
    lane = lanes(shape)
    half = jnp.where(lane < 64, 0.0, 1.0)
    picked = dot(source_hot, traces[...])
    face = column[:, 1:2]
    row = jnp.zeros(shape, f32)
    for t in range(3):
        row = jnp.where(half + 2 * t == face, picked[:, 128 * t : 128 * t + 128], row)
    every = dot(row.astype(bf16), jnp.concatenate([projection[...]] * 2, axis=0))
    kind = column[:, 2:3]
    folded = jnp.zeros(shape, f32)
    for t in range(4):
        folded = jnp.where(half + 2 * t == kind, every[:, 128 * t : 128 * t + 128], folded)
    piece = folded + pltpu.roll(folded, 64, 1)
    blocks[...] = jnp.where(lane < 64, piece, column[...]).astype(bf16)

    def block(index):
        return blocks[pl.ds(pl.multiple_of(index * capacity, capacity), capacity), :]

    def pick(which, a, b):
        return a + which * (b - a)

    final_at = pl.multiple_of(pick(core, elements - rim, 0), rim)
    other_at = pl.multiple_of(pick(core, 0, elements - rim), rim)
    first_out[0:rim, :] = traces[pl.ds(final_at, rim), :]
    rim_out[...] = traces[pl.ds(other_at, rim), :]
    at = rim
    for t, (a, b) in enumerate(((4, 3), (6, 4), (3, 1))):
        first_out[at : at + capacity, 128 * t : 128 * t + 128] = block(pick(core, a, b))
    at += capacity
    first_out[at : at + capacity, 0:128] = block(pick(core, 1, 6))
    first_out[at : at + capacity, 128:] = jnp.zeros((capacity, width - 128), bf16)
    for t, (which, a, b) in enumerate(((own, 5, 2), (own, 2, 5), (second, 7, 0), (second, 0, 7))):
        own_out[capacity * t : capacity * t + capacity, :] = block(pick(which, a, b))


def start_kernel(
    state_in, trace_map_in, records_in, counts_in, velocity_in, levels_in, neighbours_in, projection_in,
    trace_map, projection, traces, first_out, rim_out, own_out, source_hot, column, elements_column,
    state, records, counts, velocity, levels, neighbours, blocks, sems
):
    elements = state.shape[0]
    part = elements // 2
    pairs = [(trace_map_in, trace_map)]
    for i in range(2):
        cut = pl.ds(i * part, part)
        pairs.append((state_in.at[cut], state.at[cut]))
    pairs += [(records_in, records), (counts_in, counts), (velocity_in, velocity), (levels_in, levels)]
    pairs += [(neighbours_in, neighbours), (projection_in, projection)]
    copies = [pltpu.make_async_copy(a, b, sems.at[i]) for i, (a, b) in enumerate(pairs)]
    for copy in copies:
        copy.start()
    for copy in copies[3:]:
        copy.wait()
    columns = record_columns(records, counts)
    column[...] = columns
    source_hot[...] = hot(columns[:, 0:1], elements)
    elements_column[...] = element_columns(velocity, levels, neighbours)
    copies[0].wait()
    for i in range(2):
        copies[1 + i].wait()
        cut = slice(i * part, i * part + part)
        traces[cut, :] = dot(state[cut, :].astype(bf16), trace_map[...]).astype(bf16)
    send(traces, source_hot[...], column, projection, first_out, rim_out, own_out, blocks)


def element_columns(velocity, levels, neighbours):
    elements = velocity.shape[1]
    rim = elements // 8
    chip, core = place()
    raw = neighbours[...].astype(f32)
    local = raw - ((2 * chip + core) * elements).astype(f32)
    before = ((2 - core) * rim).astype(f32)
    after = (elements - core * rim).astype(f32)
    index = jnp.where(local < 0, local + before, jnp.where(local >= elements, local - after, -1.0))
    index = jnp.where(raw < 0, -1.0, index)
    scale = jnp.exp2(levels[...].astype(f32)) * 0.25
    gap = jnp.zeros((4, elements), f32)
    return transposed(jnp.concatenate([velocity[...], scale, gap, local, gap[0:2], index], axis=0))


def volume_term(column, lowered, stiffness, n, step):
    modes = stiffness.shape[0]
    volume = jnp.zeros((lowered.shape[0], step), f32)
    for d in range(3):
        volume += column[:, d : d + 1] * dot(lowered, stiffness[:, d * modes + n : d * modes + n + step])
    return column[:, 3:4] * volume


def own_part(column, traces, partial_out):
    elements = traces.shape[0]
    for t in range(3):
        tile = traces[:, 128 * t : 128 * t + 128]
        at = 8 + 2 * t
        picks = [hot(column[:, at + i : at + i + 1], elements) for i in range(2)]
        near = dot(jnp.concatenate(picks, axis=1), swapped(tile))
        partial_out[:, 128 * t : 128 * t + 128] = near - tile.astype(f32)


def local_kernel(stiffness_in, lift_in, column, state, traces, stiffness, lift, base, partial, inflow, picks, sems):
    elements, modes = state.shape
    rim = elements // 8
    copies = [
        pltpu.make_async_copy(stiffness_in, stiffness, sems.at[0]),
        pltpu.make_async_copy(lift_in, lift, sems.at[1]),
    ]
    for copy in copies:
        copy.start()
    columns = column[...]
    own_part(columns, traces, partial)
    low = lanes((elements, 128)) < 64
    for t in range(3):
        speed = columns[:, t : t + 1]
        inflow[:, 128 * t : 128 * t + 128] = columns[:, 3:4] * jnp.maximum(jnp.where(low, speed, -speed), 0.0)
    for i in range(6):
        picks[:, 2 * rim * i : 2 * rim * i + 2 * rim] = hot(columns[:, 16 + i : 17 + i], 2 * rim)
    lowered = state[...].astype(bf16)
    step = 256
    copies[0].wait()
    for n in range(0, modes, step):
        base[:, n : n + step] = state[:, n : n + step] + time_step * volume_term(columns, lowered, stiffness, n, step)
    copies[1].wait()


def second_local_kernel(column, state, field, stiffness, traces, base, partial):
    modes = state.shape[1]
    columns = column[...]
    lowered = field[...].astype(bf16)
    step = 256
    for n in range(0, modes, step):
        volume = volume_term(columns, lowered, stiffness, n, step)
        base[:, n : n + step] = 0.5 * (state[:, n : n + step] + field[:, n : n + step]) + 0.5 * time_step * volume
    own_part(columns, traces, partial)


def gather_arrivals(got, got_rim, got_even, got_odd, got_a, got_b, arrived):
    capacity = arrived.shape[0] // 8
    rim = 2 * capacity
    chip, core = place()
    second = lax.rem(lax.div(chip, 2), 2)
    arrived[0:capacity, :] = got[rim : rim + capacity, 0:128]
    for i, ref in enumerate((got_even, got_odd)):
        to = capacity * (1 + 2 * i)
        arrived[to : to + 2 * capacity, :] = ref[...]
    arrived[5 * capacity : 6 * capacity, :] = got_a[0:capacity, :]
    arrived[6 * capacity : 7 * capacity, :] = got_b[0:capacity, :]
    arrived[7 * capacity :, :] = jnp.where(
        second != core, got_a[capacity : 2 * capacity, :], got_b[capacity : 2 * capacity, :]
    )
    return jnp.concatenate([got[0:rim, :], got_rim[...]], axis=0)


def targets(pieces, elements):
    face_of = jnp.where(rows_of((128, 128)) == 66, 1.0, 0.0).astype(bf16)
    face = dot(pieces, face_of) - 1.0
    lane = lanes((8, 128))
    element_of = jnp.where(lane == 64, 16.0, jnp.where(lane == 65, 1.0, 0.0)).astype(bf16)
    target = lax.dot_general(element_of, pieces, (((1,), (1,)), ((), ())), preferred_element_type=f32)[0:1, :]
    match = rows_of((elements, pieces.shape[0])) == target.astype(jnp.int32)
    return face, jnp.where(match, 1.0, 0.0).astype(bf16)


def fluxes(pieces, face, element_hot, window, partial, inflow, picks):
    half = jnp.where(lanes(pieces.shape) < 64, 0.0, 1.0)
    plain = jnp.where(half == 0.0, pieces.astype(f32), 0.0)
    both = plain + pltpu.roll(plain, 64, 1)
    parts = []
    for t in range(3):
        cut = slice(128 * t, 128 * t + 128)
        placed = jnp.where(half + 2 * t == face, both, 0.0).astype(bf16)
        near = dot(picks[:, 256 * t : 256 * t + 256], swapped(window[:, cut]))
        mortar = dot(element_hot, placed)
        parts.append((inflow[:, cut] * (partial[:, cut] + near + mortar)).astype(bf16))
    return jnp.concatenate(parts, axis=1)


def middle_kernel(
    lift, base, partial, inflow, picks, got, got_rim, got_even, got_odd, got_a, got_b, trace_map, projection, source_hot, column,
    field, traces, first_out, rim_out, own_out, face_out, element_hot_out, arrived, blocks
):
    elements = base.shape[0]
    window = gather_arrivals(got, got_rim, got_even, got_odd, got_a, got_b, arrived)
    pieces = arrived[...]
    face, element_hot = targets(pieces, elements)
    face_out[...] = face
    element_hot_out[...] = element_hot
    flux = fluxes(pieces, face, element_hot, window, partial, inflow, picks)
    new = base[...] + time_step * dot(flux, lift[...])
    field[...] = new
    traces[...] = dot(new.astype(bf16), trace_map[...]).astype(bf16)
    send(traces, source_hot[...], column, projection, first_out, rim_out, own_out, blocks)


def end_kernel(
    lift, base, partial, inflow, picks, got, got_rim, got_even, got_odd, got_a, got_b, face, element_hot, field, arrived, result, sems
):
    elements = base.shape[0]
    window = gather_arrivals(got, got_rim, got_even, got_odd, got_a, got_b, arrived)
    flux = fluxes(arrived[...], face[...], element_hot[...], window, partial, inflow, picks)
    part = elements // 2
    copies = []
    for i in range(2):
        cut = slice(i * part, i * part + part)
        result[cut, :] = base[cut, :] + 0.5 * time_step * dot(flux[cut, :], lift[...])
        rows = pl.ds(i * part, part)
        copies.append(pltpu.make_async_copy(result.at[rows], field.at[rows], sems.at[i]))
        copies[i].start()
    for copy in copies:
        copy.wait()


def paired(count, step, lower):
    partner = {}
    for s in range(count):
        if lower(s) and s + step < count:
            partner[s] = s + step
            partner[s + step] = s
    rest = [s for s in range(count) if s not in partner]
    for a, b in zip(rest[::2], rest[1::2]):
        partner[a] = b
        partner[b] = a
    return sorted(partner.items())


def call(kernel, out_shape, scratch, flops, far, near, out_space=pltpu.VMEM):
    operands = [pltpu.with_memory_space_constraint(x, pltpu.HBM) for x in far] + list(near)
    read = sum(x.size * x.dtype.itemsize for x in operands)
    specs = [pl.BlockSpec(memory_space=pl.ANY)] * len(far) + [pl.BlockSpec(memory_space=pltpu.VMEM)] * len(near)
    return pl.pallas_call(
        kernel,
        out_shape=out_shape,
        in_specs=specs,
        out_specs=[pl.BlockSpec(memory_space=out_space)] * len(out_shape),
        scratch_shapes=scratch,
        compiler_params=pltpu.CompilerParams(vmem_limit_bytes=16 * 1024 * 1024),
        cost_estimate=pl.CostEstimate(flops=flops, bytes_accessed=read, transcendentals=0),
    )(*operands)


def exchange(first, rim, own, chip, core):
    count = lax.axis_size(CURVE)
    groups = lax.axis_size("groups")
    capacity = own.shape[0] // 4
    border = [(s, s ^ 1) for s in range(groups) if s ^ 1 < groups]
    to_next = [(g * count + s, g * count + s + 1) for g in range(groups) for s in range(1, count - 1, 2)]
    to_next += [(b, a) for a, b in to_next]
    to_next += [(a * count + s, b * count + s) for a, b in border for s in (0, count - 1)]
    got = lax.ppermute(first, CURVE, paired(count, 1, lambda s: s % 2 == 0))
    got_rim = lax.ppermute(rim, ("groups",) + CURVE, sorted(to_next))
    at = rim.shape[0]
    up = got[at : at + capacity, 128:256]
    down = got[at : at + capacity, 256:384]
    far = got[at + capacity : at + 2 * capacity, 0:128]
    even = chip % 2 == 0
    upper = ((chip // 2) % 2 == 0) == (core == 0)
    others = (jnp.where(even, up, down), jnp.where(even, down, up), jnp.where(upper, far, 0), jnp.where(upper, 0, far))
    swaps = [
        paired(count, 2, lambda s: (s // 2) % 2 == 0),
        paired(count, 2, lambda s: (s // 2) % 2 == 1),
        paired(count, 4, lambda s: (s // 4) % 2 == 0),
        paired(count, 4, lambda s: (s // 4) % 2 == 1),
    ]
    swapped_blocks = []
    for t, (other, pairs) in enumerate(zip(others, swaps)):
        block = jnp.concatenate([own[capacity * t : capacity * t + capacity], other], axis=0)
        swapped_blocks.append(lax.ppermute(block, CURVE, pairs))
    return got, got_rim, *swapped_blocks


def body(
    state, velocity, levels, neighbours, records, counts, stiffness, trace_map, lift, projection
):
    elements, modes = state.shape
    width = trace_map.shape[1]
    slots = records.shape[1]
    capacity = slots // counts.shape[1]
    rim = elements // 8
    chip, core = place()

    def array(shape, dtype):
        return jax.ShapeDtypeStruct(shape, dtype)

    def like(x):
        return array(x.shape, x.dtype)

    sent = [
        array((elements, width), bf16),
        array((rim + 2 * capacity, width), bf16),
        array((rim, width), bf16),
        array((4 * capacity, 128), bf16),
    ]
    whole = array((elements, modes), f32)
    faces = array((elements, width), f32)
    blocks = pltpu.VMEM((slots, 128), bf16)
    column_shape = array((slots, 128), f32)

    levels = levels.reshape(1, elements)
    vmem = pltpu.VMEM
    wide = (elements, 128)
    trace_map, projection, traces, first, rims, own, source_hot, column, element_column = call(
        start_kernel,
        [like(trace_map), like(projection)]
        + sent
        + [array((slots, elements), bf16), column_shape, array(wide, f32)],
        [vmem(x.shape, x.dtype) for x in (state, records, counts, velocity, levels, neighbours)]
        + [blocks, pltpu.SemaphoreType.DMA((9,))],
        2 * 10**8,
        (state, trace_map, records, counts, velocity, levels, neighbours, projection),
        (),
    )
    got = exchange(first, rims, own, chip, core)
    stiffness, lift, base, partial, inflow, picks = call(
        local_kernel,
        [like(stiffness), like(lift), whole, faces, faces, array((elements, 12 * rim), bf16)],
        [pltpu.SemaphoreType.DMA((2,))],
        3 * 10**9,
        (stiffness, lift),
        (element_column, state, traces),
    )
    field, traces, first, rims, own, face, element_hot = call(
        middle_kernel,
        [whole] + sent + [column_shape, array((elements, slots), bf16)],
        [blocks, blocks],
        10**9,
        (),
        (lift, base, partial, inflow, picks, *got, trace_map, projection, source_hot, column),
    )
    got = exchange(first, rims, own, chip, core)
    base, partial = call(
        second_local_kernel, [whole, faces], [], 3 * 10**9, (), (element_column, state, field, stiffness, traces)
    )
    return call(
        end_kernel,
        [whole],
        [blocks, vmem((elements, modes), f32), pltpu.SemaphoreType.DMA((2,))],
        10**9,
        (),
        (lift, base, partial, inflow, picks, *got, face, element_hot),
        out_space=pl.ANY,
    )[0]


def solution(mesh):
    placed = (
        P(("groups", "curve", "sub", "pair"), None),
        P(None, ("groups", "curve", "sub", "pair")),
        P(("groups", "curve", "sub", "pair")),
        P(None, ("groups", "curve", "sub", "pair")),
        P(None, ("groups", "curve", "sub", "pair")),
        P(("groups", "curve", "sub", "pair"), None),
        P(),
        P(),
        P(),
        P(),
    )
    return jax.shard_map(
        body,
        mesh=mesh,
        in_specs=placed,
        out_specs=P(("groups", "curve", "sub", "pair"), None),
        check_vma=False,
    )
```

```python
import jax
import jax.numpy as jnp
from jax import lax
from jax.experimental import pallas as pl
from jax.experimental.pallas import tpu as pltpu
from jax.sharding import PartitionSpec as P

time_step = 0.3
bf16 = jnp.bfloat16
f32 = jnp.float32
CURVE = ("curve", "sub", "pair")


def dot(a, b):
    return jnp.dot(a, b, preferred_element_type=f32)


def transposed(rows):
    pad = jnp.zeros((128 - rows.shape[0], rows.shape[1]), f32)
    return jnp.concatenate([rows, pad], axis=0).T


def lanes(shape):
    return lax.broadcasted_iota(jnp.int32, shape, 1)


def rows_of(shape):
    return lax.broadcasted_iota(jnp.int32, shape, 0)


def swapped(tile):
    turned = pltpu.roll(tile.astype(f32), 64, 1)
    low = lanes(turned.shape) < 64
    top = jnp.where(low, turned, 0.0).astype(bf16)
    bottom = jnp.where(low, 0.0, turned).astype(bf16)
    return jnp.concatenate([top, bottom], axis=0)


def hot(column, width):
    rows = column.shape[0]
    picked = column.astype(jnp.int32) == lanes((rows, width))
    return jnp.where(picked, 1.0, 0.0).astype(bf16)


def place():
    return lax.axis_index("curve") * lax.axis_size("sub") + lax.axis_index("sub"), lax.axis_index("pair")


def record_columns(records, counts):
    slots = records.shape[1]
    capacity = slots // 8
    source, face, kind, target = (records[i : i + 1, :] for i in range(4))
    slot = lanes((1, slots))
    allowed = jnp.zeros((1, slots), jnp.int32)
    for j in range(8):
        inside = (slot >= j * capacity) & (slot < (j + 1) * capacity)
        allowed = jnp.where(inside, counts[:, j : j + 1] + j * capacity, allowed)
    facing = jnp.where(slot < allowed, jnp.bitwise_xor(face, 1) + 1, 0)
    digits = [lax.shift_right_logical(target, 4), jnp.bitwise_and(target, 15), facing]
    gap = jnp.zeros((61, slots), f32)
    rows = [x.astype(f32) for x in (source, face, kind)] + [gap] + [x.astype(f32) for x in digits]
    return transposed(jnp.concatenate(rows, axis=0))


def send(traces, source_hot, column, projection, first_out, own_out, blocks):
    elements, width = traces.shape
    slots = column.shape[0]
    capacity = slots // 8
    rim = elements // 8
    chip, core = place()
    near_up = 1 - jnp.bitwise_xor(core, lax.rem(chip, 2))
    far_up = 1 - jnp.bitwise_xor(core, lax.rem(lax.div(chip, 2), 2))
    shape = (slots, 128)
    lane = lanes(shape)
    half = jnp.where(lane < 64, 0.0, 1.0)
    picked = dot(source_hot, traces[...])
    face = column[:, 1:2]
    row = jnp.zeros(shape, f32)
    for t in range(3):
        row = jnp.where(half + 2 * t == face, picked[:, 128 * t : 128 * t + 128], row)
    every = dot(row.astype(bf16), jnp.concatenate([projection[...]] * 2, axis=0))
    kind = column[:, 2:3]
    folded = jnp.zeros(shape, f32)
    for t in range(4):
        folded = jnp.where(half + 2 * t == kind, every[:, 128 * t : 128 * t + 128], folded)
    piece = folded + pltpu.roll(folded, 64, 1)
    nothing = jnp.zeros((capacity, 128), bf16)
    blocks[0:capacity, :] = nothing
    blocks[capacity : capacity + slots, :] = jnp.where(lane < 64, piece, column[...]).astype(bf16)
    blocks[capacity + slots :, :] = nothing

    def block(index):
        return blocks[pl.ds(pl.multiple_of((index + 1) * capacity, capacity), capacity), :]

    final_at = pl.multiple_of((1 - core) * (elements - rim), rim)
    other_at = pl.multiple_of(core * (elements - rim), rim)
    for t in range(3):
        cut = slice(128 * t, 128 * t + 128)
        first_out[rim * t : rim * t + rim, :] = traces[pl.ds(final_at, rim), cut]
        first_out[rim * (3 + t) : rim * (4 + t), :] = traces[pl.ds(other_at, rim), cut]
    at = 6 * rim
    inside = 4 - core
    here = [2 + 3 * near_up - core, 3 + 3 * near_up - core, 7 * far_up - core, 1 + 7 * far_up - core]
    there = [5 - 3 * near_up - core, 6 - 3 * near_up - core, 7 - 7 * far_up - core, 8 - 7 * far_up - core]
    for i, index in enumerate([inside] + there):
        first_out[at + capacity * i : at + capacity * i + capacity, :] = block(index)
    for i, index in enumerate(here):
        own_out[capacity * i : capacity * i + capacity, :] = block(index)


def start_kernel(
    state_in, trace_map_in, records_in, counts_in, velocity_in, levels_in, neighbours_in, projection_in,
    trace_map, projection, traces, first_out, own_out, source_hot, column, elements_column,
    state, records, counts, velocity, levels, neighbours, blocks, sems
):
    elements = state.shape[0]
    part = elements // 2
    pairs = [(records_in, records), (counts_in, counts), (velocity_in, velocity), (levels_in, levels)]
    pairs += [(neighbours_in, neighbours), (trace_map_in, trace_map)]
    for i in range(2):
        cut = pl.ds(i * part, part)
        pairs.append((state_in.at[cut], state.at[cut]))
    pairs.append((projection_in, projection))
    copies = [pltpu.make_async_copy(a, b, sems.at[i]) for i, (a, b) in enumerate(pairs)]
    for copy in copies:
        copy.start()
    for copy in copies[:5]:
        copy.wait()
    columns = record_columns(records, counts)
    column[...] = columns
    source_hot[...] = hot(columns[:, 0:1], elements)
    elements_column[...] = element_columns(velocity, levels, neighbours)
    copies[5].wait()
    for i in range(2):
        copies[6 + i].wait()
        cut = slice(i * part, i * part + part)
        traces[cut, :] = dot(state[cut, :].astype(bf16), trace_map[...]).astype(bf16)
    copies[8].wait()
    send(traces, source_hot[...], column, projection, first_out, own_out, blocks)


def element_columns(velocity, levels, neighbours):
    elements = velocity.shape[1]
    rim = elements // 8
    chip, core = place()
    raw = neighbours[...].astype(f32)
    local = raw - ((2 * chip + core) * elements).astype(f32)
    before = ((2 - core) * rim).astype(f32)
    after = (elements - core * rim).astype(f32)
    index = jnp.where(local < 0, local + before, jnp.where(local >= elements, local - after, -1.0))
    index = jnp.where(raw < 0, -1.0, index)
    scale = jnp.exp2(levels[...].astype(f32)) * 0.25
    gap = jnp.zeros((4, elements), f32)
    return transposed(jnp.concatenate([velocity[...], scale, gap, local, gap[0:2], index], axis=0))


def volume_term(column, lowered, stiffness, n, step):
    modes = stiffness.shape[0]
    volume = jnp.zeros((lowered.shape[0], step), f32)
    for d in range(3):
        volume += column[:, d : d + 1] * dot(lowered, stiffness[:, d * modes + n : d * modes + n + step])
    return column[:, 3:4] * volume


def own_part(column, traces, partial_out):
    elements = traces.shape[0]
    for t in range(3):
        tile = traces[:, 128 * t : 128 * t + 128]
        at = 8 + 2 * t
        picks = [hot(column[:, at + i : at + i + 1], elements) for i in range(2)]
        near = dot(jnp.concatenate(picks, axis=1), swapped(tile))
        partial_out[:, 128 * t : 128 * t + 128] = near - tile.astype(f32)


def local_kernel(stiffness_in, lift_in, column, state, traces, got, stiffness, lift, base, partial, inflow, picks, token, sems):
    token[...] = got[0:16, :]
    elements, modes = state.shape
    rim = elements // 8
    copies = [
        pltpu.make_async_copy(stiffness_in, stiffness, sems.at[0]),
        pltpu.make_async_copy(lift_in, lift, sems.at[1]),
    ]
    for copy in copies:
        copy.start()
    columns = column[...]
    own_part(columns, traces, partial)
    low = lanes((elements, 128)) < 64
    for t in range(3):
        speed = columns[:, t : t + 1]
        inflow[:, 128 * t : 128 * t + 128] = columns[:, 3:4] * jnp.maximum(jnp.where(low, speed, -speed), 0.0)
    for i in range(6):
        picks[:, 2 * rim * i : 2 * rim * i + 2 * rim] = hot(columns[:, 16 + i : 17 + i], 2 * rim)
    lowered = state[...].astype(bf16)
    step = 256
    copies[0].wait()
    for n in range(0, modes, step):
        base[:, n : n + step] = state[:, n : n + step] + time_step * volume_term(columns, lowered, stiffness, n, step)
    copies[1].wait()


def second_local_kernel(column, state, field, stiffness, traces, got, base, partial, token):
    token[...] = got[0:16, :]
    modes = state.shape[1]
    columns = column[...]
    lowered = field[...].astype(bf16)
    step = 256
    for n in range(0, modes, step):
        volume = volume_term(columns, lowered, stiffness, n, step)
        base[:, n : n + step] = 0.5 * (state[:, n : n + step] + field[:, n : n + step]) + 0.5 * time_step * volume
    own_part(columns, traces, partial)


def gather_arrivals(got, near, far, last, arrived):
    capacity = arrived.shape[0] // 8
    rim = 2 * capacity
    chip, core = place()
    near_up = 1 - jnp.bitwise_xor(core, lax.rem(chip, 2))
    far_up = 1 - jnp.bitwise_xor(core, lax.rem(lax.div(chip, 2), 2))
    at = 3 * rim

    def mine(ref, start):
        return ref[pl.ds(pl.multiple_of(start + core * capacity, capacity), capacity), :]

    parts = [
        got[2 * at : 2 * at + capacity, :],
        mine(near, at),
        mine(near, at + 2 * capacity),
        last[at : at + capacity, :],
        last[at + capacity : at + 2 * capacity, :],
        mine(far, 0),
        last[at + 3 * capacity : at + 4 * capacity, :],
        jnp.where(far_up != core, last[at + 2 * capacity : at + 3 * capacity, :], mine(far, 2 * capacity)),
    ]
    for i, part in enumerate(parts):
        arrived[capacity * i : capacity * i + capacity, :] = part
    window = []
    for t in range(3):
        cut = slice(rim * t, rim * t + rim)
        window.append(jnp.concatenate([got[cut, :], jnp.where(near_up == core, near[cut, :], last[cut, :])], axis=0))
    return window


def targets(pieces, elements):
    face_of = jnp.where(rows_of((128, 128)) == 66, 1.0, 0.0).astype(bf16)
    face = dot(pieces, face_of) - 1.0
    lane = lanes((8, 128))
    element_of = jnp.where(lane == 64, 16.0, jnp.where(lane == 65, 1.0, 0.0)).astype(bf16)
    target = lax.dot_general(element_of, pieces, (((1,), (1,)), ((), ())), preferred_element_type=f32)[0:1, :]
    match = rows_of((elements, pieces.shape[0])) == target.astype(jnp.int32)
    return face, jnp.where(match, 1.0, 0.0).astype(bf16)


def fluxes(pieces, face, element_hot, window, partial, inflow, picks):
    half = jnp.where(lanes(pieces.shape) < 64, 0.0, 1.0)
    plain = jnp.where(half == 0.0, pieces.astype(f32), 0.0)
    both = plain + pltpu.roll(plain, 64, 1)
    parts = []
    for t in range(3):
        cut = slice(128 * t, 128 * t + 128)
        placed = jnp.where(half + 2 * t == face, both, 0.0).astype(bf16)
        near = dot(picks[:, 256 * t : 256 * t + 256], swapped(window[t]))
        mortar = dot(element_hot, placed)
        parts.append((inflow[:, cut] * (partial[:, cut] + near + mortar)).astype(bf16))
    return jnp.concatenate(parts, axis=1)


def middle_kernel(
    lift, base, partial, inflow, picks, got, near, far, last, trace_map, projection, source_hot, column,
    field, traces, first_out, own_out, face_out, element_hot_out, arrived, blocks
):
    elements = base.shape[0]
    window = gather_arrivals(got, near, far, last, arrived)
    pieces = arrived[...]
    face, element_hot = targets(pieces, elements)
    face_out[...] = face
    element_hot_out[...] = element_hot
    flux = fluxes(pieces, face, element_hot, window, partial, inflow, picks)
    new = base[...] + time_step * dot(flux, lift[...])
    field[...] = new
    traces[...] = dot(new.astype(bf16), trace_map[...]).astype(bf16)
    send(traces, source_hot[...], column, projection, first_out, own_out, blocks)


def end_kernel(
    lift, base, partial, inflow, picks, got, near, far, last, face, element_hot, field, arrived, result, sems
):
    elements = base.shape[0]
    window = gather_arrivals(got, near, far, last, arrived)
    flux = fluxes(arrived[...], face[...], element_hot[...], window, partial, inflow, picks)
    part = elements // 2
    copies = []
    for i in range(2):
        cut = slice(i * part, i * part + part)
        result[cut, :] = base[cut, :] + 0.5 * time_step * dot(flux[cut, :], lift[...])
        rows = pl.ds(i * part, part)
        copies.append(pltpu.make_async_copy(result.at[rows], field.at[rows], sems.at[i]))
        copies[i].start()
    for copy in copies:
        copy.wait()


def paired(groups, count, step, lower):
    partner = {}
    for s in range(count):
        if lower(s) and s + step < count:
            partner[s] = s + step
            partner[s + step] = s
    pairs = []
    for g in range(groups):
        for s in range(count):
            if s in partner:
                pairs.append((g * count + s, g * count + partner[s]))
            elif g ^ 1 < groups:
                pairs.append((g * count + s, (g ^ 1) * count + s))
    return pairs


def call(kernel, out_shape, scratch, flops, far, near, out_space=pltpu.VMEM):
    operands = [pltpu.with_memory_space_constraint(x, pltpu.HBM) for x in far] + list(near)
    read = sum(x.size * x.dtype.itemsize for x in operands)
    specs = [pl.BlockSpec(memory_space=pl.ANY)] * len(far) + [pl.BlockSpec(memory_space=pltpu.VMEM)] * len(near)
    return pl.pallas_call(
        kernel,
        out_shape=out_shape,
        in_specs=specs,
        out_specs=[pl.BlockSpec(memory_space=out_space)] * len(out_shape),
        scratch_shapes=scratch,
        compiler_params=pltpu.CompilerParams(vmem_limit_bytes=16 * 1024 * 1024),
        cost_estimate=pl.CostEstimate(flops=flops, bytes_accessed=read, transcendentals=0),
    )(*operands)


def exchange(first, own, chip, core, local):
    axes = ("groups",) + CURVE
    groups, count = lax.axis_size("groups"), lax.axis_size(CURVE)
    cores = paired(groups, count, 1, lambda s: s % 2 == 0)
    chips = paired(groups, count, 2, lambda s: (s // 2) % 2 == s % 2)
    far_chips = paired(groups, count, 4, lambda s: (s // 4) % 2 == s % 2)
    capacity = own.shape[0] // 4
    rim = 6 * capacity
    at = 2 * rim + capacity
    got = lax.ppermute(first, axes, cores)
    own_rim = ((chip % 2) == core) == (core == 1)
    rims = jnp.where(own_rim, first[rim : 2 * rim], got[rim : 2 * rim])
    near = jnp.concatenate([rims, own[: 2 * capacity], got[at : at + 2 * capacity]], axis=0)
    far = jnp.concatenate([own[2 * capacity :], got[at + 2 * capacity : at + 4 * capacity]], axis=0)
    near = lax.ppermute(near, axes, chips)
    far = lax.ppermute(far, axes, far_chips)

    *results, token = local(got)

    def theirs(x):
        return jnp.where(core == 0, x[capacity : 2 * capacity], x[:capacity])

    parts = [near[:rim]]
    parts += [theirs(near[rim : rim + 2 * capacity]), theirs(near[rim + 2 * capacity :])]
    parts += [theirs(far[: 2 * capacity]), theirs(far[2 * capacity :]), token]
    last = lax.ppermute(jnp.concatenate(parts, axis=0), axes, cores)
    return (got, near, far, last), results


def body(
    state, velocity, levels, neighbours, records, counts, stiffness, trace_map, lift, projection
):
    elements, modes = state.shape
    width = trace_map.shape[1]
    slots = records.shape[1]
    capacity = slots // counts.shape[1]
    rim = elements // 8
    chip, core = place()

    def array(shape, dtype):
        return jax.ShapeDtypeStruct(shape, dtype)

    def like(x):
        return array(x.shape, x.dtype)

    sent = [
        array((elements, width), bf16),
        array((6 * rim + 5 * capacity, 128), bf16),
        array((4 * capacity, 128), bf16),
    ]
    whole = array((elements, modes), f32)
    faces = array((elements, width), f32)
    blocks = pltpu.VMEM((slots + 2 * capacity, 128), bf16)
    arrived = pltpu.VMEM((slots, 128), bf16)
    column_shape = array((slots, 128), f32)
    mark = array((16, 128), bf16)

    levels = levels.reshape(1, elements)
    vmem = pltpu.VMEM
    wide = (elements, 128)
    trace_map, projection, traces, first, own, source_hot, column, element_column = call(
        start_kernel,
        [like(trace_map), like(projection)]
        + sent
        + [array((slots, elements), bf16), column_shape, array(wide, f32)],
        [vmem(x.shape, x.dtype) for x in (state, records, counts, velocity, levels, neighbours)]
        + [blocks, pltpu.SemaphoreType.DMA((9,))],
        2 * 10**8,
        (state, trace_map, records, counts, velocity, levels, neighbours, projection),
        (),
    )

    def local(got):
        return call(
            local_kernel,
            [like(stiffness), like(lift), whole, faces, faces, array((elements, 12 * rim), bf16), mark],
            [pltpu.SemaphoreType.DMA((2,))],
            3 * 10**9,
            (stiffness, lift),
            (element_column, state, traces, got),
        )

    got, (near_stiffness, near_lift, base, partial, inflow, picks) = exchange(first, own, chip, core, local)
    field, traces, first, own, face, element_hot = call(
        middle_kernel,
        [whole] + sent + [column_shape, array((elements, slots), bf16)],
        [arrived, blocks],
        10**9,
        (),
        (near_lift, base, partial, inflow, picks, *got, trace_map, projection, source_hot, column),
    )

    def second_local(got):
        return call(
            second_local_kernel,
            [whole, faces, mark],
            [],
            3 * 10**9,
            (),
            (element_column, state, field, near_stiffness, traces, got),
        )

    got, (base, partial) = exchange(first, own, chip, core, second_local)
    return call(
        end_kernel,
        [whole],
        [arrived, vmem((elements, modes), f32), pltpu.SemaphoreType.DMA((2,))],
        10**9,
        (),
        (near_lift, base, partial, inflow, picks, *got, face, element_hot),
        out_space=pl.ANY,
    )[0]


def solution(mesh):
    placed = (
        P(("groups", "curve", "sub", "pair"), None),
        P(None, ("groups", "curve", "sub", "pair")),
        P(("groups", "curve", "sub", "pair")),
        P(None, ("groups", "curve", "sub", "pair")),
        P(None, ("groups", "curve", "sub", "pair")),
        P(("groups", "curve", "sub", "pair"), None),
        P(),
        P(),
        P(),
        P(),
    )
    return jax.shard_map(
        body,
        mesh=mesh,
        in_specs=placed,
        out_specs=P(("groups", "curve", "sub", "pair"), None),
        check_vma=False,
    )
```

```python
import jax
import jax.numpy as jnp
from jax import lax
from jax.experimental import pallas as pl
from jax.experimental.pallas import tpu as pltpu
from jax.sharding import PartitionSpec as P

time_step = 0.3
bf16 = jnp.bfloat16
f32 = jnp.float32
CURVE = ("curve", "sub", "pair")


def dot(a, b):
    return jnp.dot(a, b, preferred_element_type=f32)


def transposed(rows):
    pad = jnp.zeros((128 - rows.shape[0], rows.shape[1]), f32)
    return jnp.concatenate([rows, pad], axis=0).T


def lanes(shape):
    return lax.broadcasted_iota(jnp.int32, shape, 1)


def rows_of(shape):
    return lax.broadcasted_iota(jnp.int32, shape, 0)


def swapped(tile):
    turned = pltpu.roll(tile.astype(f32), 64, 1)
    low = lanes(turned.shape) < 64
    top = jnp.where(low, turned, 0.0).astype(bf16)
    bottom = jnp.where(low, 0.0, turned).astype(bf16)
    return jnp.concatenate([top, bottom], axis=0)


def hot(column, width):
    rows = column.shape[0]
    picked = column.astype(jnp.int32) == lanes((rows, width))
    return jnp.where(picked, 1.0, 0.0).astype(bf16)


def place():
    return lax.axis_index("curve") * lax.axis_size("sub") + lax.axis_index("sub"), lax.axis_index("pair")


def record_columns(records, counts):
    slots = records.shape[1]
    capacity = slots // 8
    source, face, kind, target = (records[i : i + 1, :] for i in range(4))
    slot = lanes((1, slots))
    allowed = jnp.zeros((1, slots), jnp.int32)
    for j in range(8):
        inside = (slot >= j * capacity) & (slot < (j + 1) * capacity)
        allowed = jnp.where(inside, counts[:, j : j + 1] + j * capacity, allowed)
    facing = jnp.where(slot < allowed, jnp.bitwise_xor(face, 1) + 1, 0)
    digits = [lax.shift_right_logical(target, 4), jnp.bitwise_and(target, 15), facing]
    gap = jnp.zeros((61, slots), f32)
    rows = [x.astype(f32) for x in (source, face, kind)] + [gap] + [x.astype(f32) for x in digits]
    return transposed(jnp.concatenate(rows, axis=0))


def send(traces, source_hot, column, projection, first_out, own_out, blocks):
    elements, width = traces.shape
    slots = column.shape[0]
    capacity = slots // 8
    rim = elements // 8
    core = lax.axis_index("pair")
    shape = (slots, 128)
    lane = lanes(shape)
    half = jnp.where(lane < 64, 0.0, 1.0)
    picked = dot(source_hot, traces[...])
    face = column[:, 1:2]
    row = jnp.zeros(shape, f32)
    for t in range(3):
        row = jnp.where(half + 2 * t == face, picked[:, 128 * t : 128 * t + 128], row)
    every = dot(row.astype(bf16), jnp.concatenate([projection[...]] * 2, axis=0))
    kind = column[:, 2:3]
    folded = jnp.zeros(shape, f32)
    for t in range(4):
        folded = jnp.where(half + 2 * t == kind, every[:, 128 * t : 128 * t + 128], folded)
    piece = folded + pltpu.roll(folded, 64, 1)
    blocks[...] = jnp.where(lane < 64, piece, column[...]).astype(bf16)

    def block(at_first, at_second):
        index = at_first + core * (at_second - at_first)
        return blocks[pl.ds(pl.multiple_of(index * capacity, capacity), capacity), :]

    final_at = pl.multiple_of((1 - core) * (elements - rim), rim)
    other_at = pl.multiple_of(core * (elements - rim), rim)
    for t in range(3):
        cut = slice(128 * t, 128 * t + 128)
        rows = slice(rim * t, rim * t + rim)
        first_out[rows, :] = traces[pl.ds(final_at, rim), cut]
        own_out[rows, :] = traces[pl.ds(other_at, rim), cut]
    at = 3 * rim
    there = [(4, 3), (5, 1), (6, 2), (7, 0)]
    here = [(2, 4), (3, 5), (0, 6), (1, 7)]
    for i in range(4):
        rows = slice(at + capacity * i, at + capacity * i + capacity)
        first_out[rows, :] = block(*there[i])
        own_out[rows, :] = block(*here[i])


def start_kernel(
    state_in, trace_map_in, records_in, counts_in, velocity_in, levels_in, neighbours_in, projection_in,
    trace_map, projection, traces, first_out, own_out, source_hot, column, elements_column,
    state, records, counts, velocity, levels, neighbours, blocks, sems
):
    elements = state.shape[0]
    part = elements // 2
    pairs = [(records_in, records), (counts_in, counts), (velocity_in, velocity), (levels_in, levels)]
    pairs += [(neighbours_in, neighbours), (trace_map_in, trace_map)]
    for i in range(2):
        cut = pl.ds(i * part, part)
        pairs.append((state_in.at[cut], state.at[cut]))
    pairs.append((projection_in, projection))
    copies = [pltpu.make_async_copy(a, b, sems.at[i]) for i, (a, b) in enumerate(pairs)]
    for copy in copies:
        copy.start()
    for copy in copies[:5]:
        copy.wait()
    columns = record_columns(records, counts)
    column[...] = columns
    source_hot[...] = hot(columns[:, 0:1], elements)
    elements_column[...] = element_columns(velocity, levels, neighbours)
    copies[5].wait()
    for i in range(2):
        copies[6 + i].wait()
        cut = slice(i * part, i * part + part)
        traces[cut, :] = dot(state[cut, :].astype(bf16), trace_map[...]).astype(bf16)
    copies[8].wait()
    send(traces, source_hot[...], column, projection, first_out, own_out, blocks)


def element_columns(velocity, levels, neighbours):
    elements = velocity.shape[1]
    rim = elements // 8
    chip, core = place()
    raw = neighbours[...].astype(f32)
    local = raw - ((2 * chip + core) * elements).astype(f32)
    before = ((2 - core) * rim).astype(f32)
    after = (elements - core * rim).astype(f32)
    index = jnp.where(local < 0, local + before, jnp.where(local >= elements, local - after, -1.0))
    index = jnp.where(raw < 0, -1.0, index)
    scale = jnp.exp2(levels[...].astype(f32)) * 0.25
    gap = jnp.zeros((4, elements), f32)
    return transposed(jnp.concatenate([velocity[...], scale, gap, local, gap[0:2], index], axis=0))


def volume_term(column, lowered, stiffness, n, step):
    modes = stiffness.shape[0]
    volume = jnp.zeros((lowered.shape[0], step), f32)
    for d in range(3):
        volume += column[:, d : d + 1] * dot(lowered, stiffness[:, d * modes + n : d * modes + n + step])
    return column[:, 3:4] * volume


def own_part(column, traces, partial_out):
    elements = traces.shape[0]
    for t in range(3):
        tile = traces[:, 128 * t : 128 * t + 128]
        at = 8 + 2 * t
        picks = [hot(column[:, at + i : at + i + 1], elements) for i in range(2)]
        near = dot(jnp.concatenate(picks, axis=1), swapped(tile))
        partial_out[:, 128 * t : 128 * t + 128] = near - tile.astype(f32)


def local_kernel(stiffness_in, lift_in, column, state, traces, got, stiffness, lift, base, partial, inflow, picks, token, sems):
    token[...] = got[0:16, :]
    elements, modes = state.shape
    rim = elements // 8
    copies = [
        pltpu.make_async_copy(stiffness_in, stiffness, sems.at[0]),
        pltpu.make_async_copy(lift_in, lift, sems.at[1]),
    ]
    for copy in copies:
        copy.start()
    columns = column[...]
    own_part(columns, traces, partial)
    low = lanes((elements, 128)) < 64
    for t in range(3):
        speed = columns[:, t : t + 1]
        inflow[:, 128 * t : 128 * t + 128] = columns[:, 3:4] * jnp.maximum(jnp.where(low, speed, -speed), 0.0)
    for i in range(6):
        picks[:, 2 * rim * i : 2 * rim * i + 2 * rim] = hot(columns[:, 16 + i : 17 + i], 2 * rim)
    lowered = state[...].astype(bf16)
    step = 256
    copies[0].wait()
    for n in range(0, modes, step):
        base[:, n : n + step] = state[:, n : n + step] + time_step * volume_term(columns, lowered, stiffness, n, step)
    copies[1].wait()


def second_local_kernel(column, state, field, stiffness, traces, got, base, partial, token):
    token[...] = got[0:16, :]
    modes = state.shape[1]
    columns = column[...]
    lowered = field[...].astype(bf16)
    step = 256
    for n in range(0, modes, step):
        volume = volume_term(columns, lowered, stiffness, n, step)
        base[:, n : n + step] = 0.5 * (state[:, n : n + step] + field[:, n : n + step]) + 0.5 * time_step * volume
    own_part(columns, traces, partial)


def gather_arrivals(got, near, far, last, arrived):
    capacity = arrived.shape[0] // 8
    rim = 2 * capacity
    core = lax.axis_index("pair")
    at = 3 * rim

    def mine(ref, start):
        return ref[pl.ds(pl.multiple_of(start + core * capacity, capacity), capacity), :]

    arrived[0:capacity, :] = got[at : at + capacity, :]
    arrived[capacity : 2 * capacity, :] = mine(near, at)
    arrived[2 * capacity : 3 * capacity, :] = mine(near, at + 2 * capacity)
    arrived[3 * capacity : 4 * capacity, :] = mine(far, 0)
    arrived[4 * capacity : 5 * capacity, :] = far[2 * capacity : 3 * capacity, :]
    arrived[5 * capacity :, :] = last[0 : 3 * capacity, :]
    cuts = [slice(rim * t, rim * t + rim) for t in range(3)]
    return [jnp.concatenate([got[cut, :], near[cut, :]], axis=0) for cut in cuts]


def targets(pieces, elements):
    face_of = jnp.where(rows_of((128, 128)) == 66, 1.0, 0.0).astype(bf16)
    face = dot(pieces, face_of) - 1.0
    lane = lanes((8, 128))
    element_of = jnp.where(lane == 64, 16.0, jnp.where(lane == 65, 1.0, 0.0)).astype(bf16)
    target = lax.dot_general(element_of, pieces, (((1,), (1,)), ((), ())), preferred_element_type=f32)[0:1, :]
    match = rows_of((elements, pieces.shape[0])) == target.astype(jnp.int32)
    return face, jnp.where(match, 1.0, 0.0).astype(bf16)


def fluxes(pieces, face, element_hot, window, partial, inflow, picks):
    half = jnp.where(lanes(pieces.shape) < 64, 0.0, 1.0)
    plain = jnp.where(half == 0.0, pieces.astype(f32), 0.0)
    both = plain + pltpu.roll(plain, 64, 1)
    parts = []
    for t in range(3):
        cut = slice(128 * t, 128 * t + 128)
        placed = jnp.where(half + 2 * t == face, both, 0.0).astype(bf16)
        near = dot(picks[:, 256 * t : 256 * t + 256], swapped(window[t]))
        mortar = dot(element_hot, placed)
        parts.append((inflow[:, cut] * (partial[:, cut] + near + mortar)).astype(bf16))
    return jnp.concatenate(parts, axis=1)


def middle_kernel(
    lift, base, partial, inflow, picks, got, near, far, last, trace_map, projection, source_hot, column,
    field, traces, first_out, own_out, face_out, element_hot_out, arrived, blocks
):
    elements = base.shape[0]
    window = gather_arrivals(got, near, far, last, arrived)
    pieces = arrived[...]
    face, element_hot = targets(pieces, elements)
    face_out[...] = face
    element_hot_out[...] = element_hot
    flux = fluxes(pieces, face, element_hot, window, partial, inflow, picks)
    new = base[...] + time_step * dot(flux, lift[...])
    field[...] = new
    traces[...] = dot(new.astype(bf16), trace_map[...]).astype(bf16)
    send(traces, source_hot[...], column, projection, first_out, own_out, blocks)


def end_kernel(
    lift, base, partial, inflow, picks, got, near, far, last, face, element_hot, field, arrived, result, sems
):
    elements = base.shape[0]
    window = gather_arrivals(got, near, far, last, arrived)
    part = elements // 2
    copies = []
    for i in range(2):
        cut = pl.ds(i * part, part)
        flux = fluxes(
            arrived[...], face[...], element_hot[cut, :], window, partial.at[cut], inflow.at[cut], picks.at[cut]
        )
        result[cut, :] = base[cut, :] + 0.5 * time_step * dot(flux, lift[...])
        copies.append(pltpu.make_async_copy(result.at[cut], field.at[cut], sems.at[i]))
        copies[i].start()
    for copy in copies:
        copy.wait()


def paired(groups, count, step, lower):
    partner = {}
    for s in range(count):
        if lower(s) and s + step < count:
            partner[s] = s + step
            partner[s + step] = s
    pairs = []
    for g in range(groups):
        for s in range(count):
            if s in partner:
                pairs.append((g * count + s, g * count + partner[s]))
            elif g ^ 1 < groups:
                pairs.append((g * count + s, (g ^ 1) * count + s))
    return pairs


def call(kernel, out_shape, scratch, flops, far, near, out_space=pltpu.VMEM):
    operands = [pltpu.with_memory_space_constraint(x, pltpu.HBM) for x in far] + list(near)
    read = sum(x.size * x.dtype.itemsize for x in operands)
    specs = [pl.BlockSpec(memory_space=pl.ANY)] * len(far) + [pl.BlockSpec(memory_space=pltpu.VMEM)] * len(near)
    return pl.pallas_call(
        kernel,
        out_shape=out_shape,
        in_specs=specs,
        out_specs=[pl.BlockSpec(memory_space=out_space)] * len(out_shape),
        scratch_shapes=scratch,
        compiler_params=pltpu.CompilerParams(vmem_limit_bytes=16 * 1024 * 1024),
        cost_estimate=pl.CostEstimate(flops=flops, bytes_accessed=read, transcendentals=0),
    )(*operands)


def exchange(first, own, core, capacity, local):
    axes = ("groups",) + CURVE
    groups, count = lax.axis_size("groups"), lax.axis_size(CURVE)
    cores = paired(groups, count, 1, lambda s: s % 2 == 0)
    chips = paired(groups, count, 1, lambda s: s % 2 == 1)
    far_chips = paired(groups, count, 3, lambda s: s % 2 == 1)
    at = own.shape[0] - 4 * capacity
    got = lax.ppermute(first, axes, cores)
    near = jnp.concatenate([own[: at + 2 * capacity], got[at + capacity : at + 3 * capacity]], axis=0)
    far = jnp.concatenate([own[at + 2 * capacity :], got[at + 3 * capacity :]], axis=0)
    near = lax.ppermute(near, axes, chips)
    far = lax.ppermute(far, axes, far_chips)
    *results, token = local(got)

    def theirs(x):
        return jnp.where(core == 0, x[capacity : 2 * capacity], x[:capacity])

    parts = [theirs(near[at : at + 2 * capacity]), theirs(near[at + 2 * capacity :]), theirs(far[: 2 * capacity])]
    last = lax.ppermute(jnp.concatenate(parts + [token], axis=0), axes, cores)
    return (got, near, far, last), results


def body(
    state, velocity, levels, neighbours, records, counts, stiffness, trace_map, lift, projection
):
    elements, modes = state.shape
    width = trace_map.shape[1]
    slots = records.shape[1]
    capacity = slots // counts.shape[1]
    rim = elements // 8
    core = lax.axis_index("pair")

    def array(shape, dtype):
        return jax.ShapeDtypeStruct(shape, dtype)

    def like(x):
        return array(x.shape, x.dtype)

    sent = [
        array((elements, width), bf16),
        array((3 * rim + 4 * capacity, 128), bf16),
        array((3 * rim + 4 * capacity, 128), bf16),
    ]
    whole = array((elements, modes), f32)
    faces = array((elements, width), f32)
    blocks = pltpu.VMEM((slots, 128), bf16)
    column_shape = array((slots, 128), f32)
    mark = array((16, 128), bf16)

    levels = levels.reshape(1, elements)
    vmem = pltpu.VMEM
    wide = (elements, 128)
    trace_map, projection, traces, first, own, source_hot, column, element_column = call(
        start_kernel,
        [like(trace_map), like(projection)]
        + sent
        + [array((slots, elements), bf16), column_shape, array(wide, f32)],
        [vmem(x.shape, x.dtype) for x in (state, records, counts, velocity, levels, neighbours)]
        + [blocks, pltpu.SemaphoreType.DMA((9,))],
        2 * 10**8,
        (state, trace_map, records, counts, velocity, levels, neighbours, projection),
        (),
    )

    def local(got):
        return call(
            local_kernel,
            [like(stiffness), like(lift), whole, faces, faces, array((elements, 12 * rim), bf16), mark],
            [pltpu.SemaphoreType.DMA((2,))],
            3 * 10**9,
            (stiffness, lift),
            (element_column, state, traces, got),
        )

    got, (near_stiffness, near_lift, base, partial, inflow, picks) = exchange(first, own, core, capacity, local)
    field, traces, first, own, face, element_hot = call(
        middle_kernel,
        [whole] + sent + [column_shape, array((elements, slots), bf16)],
        [blocks, blocks],
        10**9,
        (),
        (near_lift, base, partial, inflow, picks, *got, trace_map, projection, source_hot, column),
    )

    def second_local(got):
        return call(
            second_local_kernel,
            [whole, faces, mark],
            [],
            3 * 10**9,
            (),
            (element_column, state, field, near_stiffness, traces, got),
        )

    got, (base, partial) = exchange(first, own, core, capacity, second_local)
    return call(
        end_kernel,
        [whole],
        [blocks, vmem((elements, modes), f32), pltpu.SemaphoreType.DMA((2,))],
        10**9,
        (),
        (near_lift, base, partial, inflow, picks, *got, face, element_hot),
        out_space=pl.ANY,
    )[0]


def solution(mesh):
    placed = (
        P(("groups", "curve", "sub", "pair"), None),
        P(None, ("groups", "curve", "sub", "pair")),
        P(("groups", "curve", "sub", "pair")),
        P(None, ("groups", "curve", "sub", "pair")),
        P(None, ("groups", "curve", "sub", "pair")),
        P(("groups", "curve", "sub", "pair"), None),
        P(),
        P(),
        P(),
        P(),
    )
    return jax.shard_map(
        body,
        mesh=mesh,
        in_specs=placed,
        out_specs=P(("groups", "curve", "sub", "pair"), None),
        check_vma=False,
    )
```

```python
import jax
import jax.numpy as jnp
from jax import lax
from jax.experimental import pallas as pl
from jax.experimental.pallas import tpu as pltpu
from jax.sharding import PartitionSpec as P

time_step = 0.3
bf16 = jnp.bfloat16
f32 = jnp.float32
CURVE = ("curve", "sub", "pair")


def dot(a, b):
    return jnp.dot(a, b, preferred_element_type=f32)


def transposed(rows):
    pad = jnp.zeros((128 - rows.shape[0], rows.shape[1]), f32)
    return jnp.concatenate([rows, pad], axis=0).T


def lanes(shape):
    return lax.broadcasted_iota(jnp.int32, shape, 1)


def rows_of(shape):
    return lax.broadcasted_iota(jnp.int32, shape, 0)


def swapped(tile):
    turned = pltpu.roll(tile.astype(f32), 64, 1)
    low = lanes(turned.shape) < 64
    top = jnp.where(low, turned, 0.0).astype(bf16)
    bottom = jnp.where(low, 0.0, turned).astype(bf16)
    return jnp.concatenate([top, bottom], axis=0)


def hot(column, width):
    rows = column.shape[0]
    picked = column.astype(jnp.int32) == lanes((rows, width))
    return jnp.where(picked, 1.0, 0.0).astype(bf16)


def place():
    return lax.axis_index("curve") * lax.axis_size("sub") + lax.axis_index("sub"), lax.axis_index("pair")


def record_columns(records, counts):
    slots = records.shape[1]
    capacity = slots // 8
    source, face, kind, target = (records[i : i + 1, :] for i in range(4))
    slot = lanes((1, slots))
    allowed = jnp.zeros((1, slots), jnp.int32)
    for j in range(8):
        inside = (slot >= j * capacity) & (slot < (j + 1) * capacity)
        allowed = jnp.where(inside, counts[:, j : j + 1] + j * capacity, allowed)
    facing = jnp.where(slot < allowed, jnp.bitwise_xor(face, 1) + 1, 0)
    digits = [lax.shift_right_logical(target, 4), jnp.bitwise_and(target, 15), facing]
    gap = jnp.zeros((61, slots), f32)
    rows = [x.astype(f32) for x in (source, face, kind)] + [gap] + [x.astype(f32) for x in digits]
    return transposed(jnp.concatenate(rows, axis=0))


def send(traces, source_hot, column, projection, first_out, own_out, blocks):
    elements, width = traces.shape
    slots = column.shape[0]
    capacity = slots // 8
    rim = elements // 8
    core = lax.axis_index("pair")
    shape = (slots, 128)
    lane = lanes(shape)
    half = jnp.where(lane < 64, 0.0, 1.0)
    picked = dot(source_hot, traces[...])
    face = column[:, 1:2]
    row = jnp.zeros(shape, f32)
    for t in range(3):
        row = jnp.where(half + 2 * t == face, picked[:, 128 * t : 128 * t + 128], row)
    every = dot(row.astype(bf16), jnp.concatenate([projection[...]] * 2, axis=0))
    kind = column[:, 2:3]
    folded = jnp.zeros(shape, f32)
    for t in range(4):
        folded = jnp.where(half + 2 * t == kind, every[:, 128 * t : 128 * t + 128], folded)
    piece = folded + pltpu.roll(folded, 64, 1)
    blocks[...] = jnp.where(lane < 64, piece, column[...]).astype(bf16)

    def block(at_first, at_second):
        index = at_first + core * (at_second - at_first)
        return blocks[pl.ds(pl.multiple_of(index * capacity, capacity), capacity), :]

    final_at = pl.multiple_of((1 - core) * (elements - rim), rim)
    other_at = pl.multiple_of(core * (elements - rim), rim)
    for t in range(3):
        cut = slice(128 * t, 128 * t + 128)
        rows = slice(rim * t, rim * t + rim)
        first_out[rows, :] = traces[pl.ds(final_at, rim), cut]
        own_out[rows, :] = traces[pl.ds(other_at, rim), cut]
    at = 3 * rim
    there = [(4, 3), (5, 1), (6, 2), (7, 0)]
    here = [(2, 4), (3, 5), (0, 6), (1, 7)]
    for i in range(4):
        rows = slice(at + capacity * i, at + capacity * i + capacity)
        first_out[rows, :] = block(*there[i])
        own_out[rows, :] = block(*here[i])


def start_kernel(
    state_in, trace_map_in, records_in, counts_in, velocity_in, levels_in, neighbours_in, projection_in,
    state, trace_map, projection, traces, first_out, own_out, source_hot, column, elements_column,
    records, counts, velocity, levels, neighbours, blocks, sems
):
    elements = state.shape[0]
    part = elements // 2
    pairs = [(records_in, records), (counts_in, counts), (velocity_in, velocity), (levels_in, levels)]
    pairs += [(neighbours_in, neighbours), (trace_map_in, trace_map)]
    for i in range(2):
        cut = pl.ds(i * part, part)
        pairs.append((state_in.at[cut], state.at[cut]))
    pairs.append((projection_in, projection))
    copies = [pltpu.make_async_copy(a, b, sems.at[i]) for i, (a, b) in enumerate(pairs)]
    for copy in copies:
        copy.start()
    for copy in copies[:5]:
        copy.wait()
    columns = record_columns(records, counts)
    column[...] = columns
    source_hot[...] = hot(columns[:, 0:1], elements)
    elements_column[...] = element_columns(velocity, levels, neighbours)
    copies[5].wait()
    for i in range(2):
        copies[6 + i].wait()
        cut = slice(i * part, i * part + part)
        traces[cut, :] = dot(state[cut, :].astype(bf16), trace_map[...]).astype(bf16)
    copies[8].wait()
    send(traces, source_hot[...], column, projection, first_out, own_out, blocks)


def element_columns(velocity, levels, neighbours):
    elements = velocity.shape[1]
    rim = elements // 8
    chip, core = place()
    raw = neighbours[...].astype(f32)
    local = raw - ((2 * chip + core) * elements).astype(f32)
    before = ((2 - core) * rim).astype(f32)
    after = (elements - core * rim).astype(f32)
    index = jnp.where(local < 0, local + before, jnp.where(local >= elements, local - after, -1.0))
    index = jnp.where(raw < 0, -1.0, index)
    scale = jnp.exp2(levels[...].astype(f32)) * 0.25
    gap = jnp.zeros((4, elements), f32)
    return transposed(jnp.concatenate([velocity[...], scale, gap, local, gap[0:2], index], axis=0))


def volume_term(column, lowered, stiffness, n, step):
    modes = stiffness.shape[0]
    volume = jnp.zeros((lowered.shape[0], step), f32)
    for d in range(3):
        volume += column[:, d : d + 1] * dot(lowered, stiffness[:, d * modes + n : d * modes + n + step])
    return column[:, 3:4] * volume


def own_part(column, traces, partial_out):
    elements = traces.shape[0]
    for t in range(3):
        tile = traces[:, 128 * t : 128 * t + 128]
        at = 8 + 2 * t
        picks = [hot(column[:, at + i : at + i + 1], elements) for i in range(2)]
        near = dot(jnp.concatenate(picks, axis=1), swapped(tile))
        partial_out[:, 128 * t : 128 * t + 128] = near - tile.astype(f32)


def local_kernel(stiffness_in, lift_in, column, state, traces, got, stiffness, lift, base, partial, inflow, picks, token, sems):
    token[...] = got[0:16, :]
    elements, modes = state.shape
    rim = elements // 8
    copies = [
        pltpu.make_async_copy(stiffness_in, stiffness, sems.at[0]),
        pltpu.make_async_copy(lift_in, lift, sems.at[1]),
    ]
    for copy in copies:
        copy.start()
    columns = column[...]
    own_part(columns, traces, partial)
    low = lanes((elements, 128)) < 64
    for t in range(3):
        speed = columns[:, t : t + 1]
        inflow[:, 128 * t : 128 * t + 128] = columns[:, 3:4] * jnp.maximum(jnp.where(low, speed, -speed), 0.0)
    for i in range(6):
        picks[:, 2 * rim * i : 2 * rim * i + 2 * rim] = hot(columns[:, 16 + i : 17 + i], 2 * rim)
    lowered = state[...].astype(bf16)
    step = 256
    copies[0].wait()
    for n in range(0, modes, step):
        base[:, n : n + step] = state[:, n : n + step] + time_step * volume_term(columns, lowered, stiffness, n, step)
    copies[1].wait()


def second_local_kernel(column, state, field, stiffness, traces, got, base, partial, token):
    token[...] = got[0:16, :]
    modes = state.shape[1]
    columns = column[...]
    lowered = field[...].astype(bf16)
    step = 256
    for n in range(0, modes, step):
        volume = volume_term(columns, lowered, stiffness, n, step)
        base[:, n : n + step] = 0.5 * (state[:, n : n + step] + field[:, n : n + step]) + 0.5 * time_step * volume
    own_part(columns, traces, partial)


def direct_pieces(got, near, far, arrived):
    capacity = arrived.shape[0] // 5
    at = 6 * capacity
    core = lax.axis_index("pair")

    def mine(ref, start):
        return ref[pl.ds(pl.multiple_of(start + core * capacity, capacity), capacity), :]

    blocks = [
        got[at : at + capacity, :],
        mine(near, at),
        mine(near, at + 2 * capacity),
        mine(far, 0),
        far[2 * capacity : 3 * capacity, :],
    ]
    for i, block in enumerate(blocks):
        arrived[capacity * i : capacity * i + capacity, :] = block
    return arrived[...]


def targets(pieces, elements):
    face_of = jnp.where(rows_of((128, 128)) == 66, 1.0, 0.0).astype(bf16)
    face = dot(pieces, face_of) - 1.0
    lane = lanes((8, 128))
    element_of = jnp.where(lane == 64, 16.0, jnp.where(lane == 65, 1.0, 0.0)).astype(bf16)
    target = lax.dot_general(element_of, pieces, (((1,), (1,)), ((), ())), preferred_element_type=f32)[0:1, :]
    match = rows_of((elements, pieces.shape[0])) == target.astype(jnp.int32)
    return face, jnp.where(match, 1.0, 0.0).astype(bf16)


def mortar_term(pieces, face, element_hot, t):
    half = jnp.where(lanes(pieces.shape) < 64, 0.0, 1.0)
    plain = jnp.where(half == 0.0, pieces.astype(f32), 0.0)
    both = plain + pltpu.roll(plain, 64, 1)
    return dot(element_hot, jnp.where(half + 2 * t == face, both, 0.0).astype(bf16))


def add_direct(picks, partial, got, near, pieces, face, element_hot, total):
    rim = picks.shape[1] // 12
    for t in range(3):
        cut = slice(128 * t, 128 * t + 128)
        rows = slice(rim * t, rim * t + rim)
        window = jnp.concatenate([got[rows, :], near[rows, :]], axis=0)
        conforming = dot(picks[:, 4 * rim * t : 4 * rim * t + 4 * rim], swapped(window))
        total[:, cut] = partial[:, cut] + conforming + mortar_term(pieces, face, element_hot, t)


def direct_kernel(picks, partial, got, near, far, last, total, face_out, element_hot_out, arrived):
    pieces = direct_pieces(got, near, far, arrived)
    face, element_hot = targets(pieces, partial.shape[0])
    face_out[...] = face
    element_hot_out[...] = element_hot
    add_direct(picks, partial, got, near, pieces, face, element_hot, total)


def second_direct_kernel(picks, partial, face, element_hot, got, near, far, last, total, arrived):
    pieces = direct_pieces(got, near, far, arrived)
    add_direct(picks, partial, got, near, pieces, face[...], element_hot[...], total)


def fluxes(pieces, face, element_hot, partial, inflow):
    parts = []
    for t in range(3):
        cut = slice(128 * t, 128 * t + 128)
        total = partial[:, cut] + mortar_term(pieces, face, element_hot, t)
        parts.append((inflow[:, cut] * total).astype(bf16))
    return jnp.concatenate(parts, axis=1)


def middle_kernel(
    lift, base, partial, inflow, last, trace_map, projection, source_hot, column,
    field, traces, first_out, own_out, face_out, element_hot_out, blocks
):
    elements = base.shape[0]
    pieces = last[0 : face_out.shape[0], :]
    face, element_hot = targets(pieces, elements)
    face_out[...] = face
    element_hot_out[...] = element_hot
    flux = fluxes(pieces, face, element_hot, partial, inflow)
    new = base[...] + time_step * dot(flux, lift[...])
    field[...] = new
    traces[...] = dot(new.astype(bf16), trace_map[...]).astype(bf16)
    send(traces, source_hot[...], column, projection, first_out, own_out, blocks)


def end_kernel(lift, base, partial, inflow, last, face, element_hot, field, result, sems):
    elements = base.shape[0]
    pieces = last[0 : face.shape[0], :]
    part = elements // 2
    copies = []
    for i in range(2):
        cut = pl.ds(i * part, part)
        flux = fluxes(pieces, face[...], element_hot[cut, :], partial.at[cut], inflow.at[cut])
        result[cut, :] = base[cut, :] + 0.5 * time_step * dot(flux, lift[...])
        copies.append(pltpu.make_async_copy(result.at[cut], field.at[cut], sems.at[i]))
        copies[i].start()
    for copy in copies:
        copy.wait()


def paired(groups, count, step, lower):
    partner = {}
    for s in range(count):
        if lower(s) and s + step < count:
            partner[s] = s + step
            partner[s + step] = s
    pairs = []
    for g in range(groups):
        for s in range(count):
            if s in partner:
                pairs.append((g * count + s, g * count + partner[s]))
            elif g ^ 1 < groups:
                pairs.append((g * count + s, (g ^ 1) * count + s))
    return pairs


def call(kernel, out_shape, scratch, flops, far, near, out_space=pltpu.VMEM):
    operands = [pltpu.with_memory_space_constraint(x, pltpu.HBM) for x in far] + list(near)
    read = sum(x.size * x.dtype.itemsize for x in operands)
    specs = [pl.BlockSpec(memory_space=pl.ANY)] * len(far) + [pl.BlockSpec(memory_space=pltpu.VMEM)] * len(near)
    return pl.pallas_call(
        kernel,
        out_shape=out_shape,
        in_specs=specs,
        out_specs=[pl.BlockSpec(memory_space=out_space)] * len(out_shape),
        scratch_shapes=scratch,
        compiler_params=pltpu.CompilerParams(vmem_limit_bytes=16 * 1024 * 1024),
        cost_estimate=pl.CostEstimate(flops=flops, bytes_accessed=read, transcendentals=0),
    )(*operands)


def exchange(first, own, core, capacity, local, direct):
    axes = ("groups",) + CURVE
    groups, count = lax.axis_size("groups"), lax.axis_size(CURVE)
    cores = paired(groups, count, 1, lambda s: s % 2 == 0)
    chips = paired(groups, count, 1, lambda s: s % 2 == 1)
    far_chips = paired(groups, count, 3, lambda s: s % 2 == 1)
    at = own.shape[0] - 4 * capacity
    got = lax.ppermute(first, axes, cores)
    near = jnp.concatenate([own[: at + 2 * capacity], got[at + capacity : at + 3 * capacity]], axis=0)
    far = jnp.concatenate([own[at + 2 * capacity :], got[at + 3 * capacity :]], axis=0)
    near = lax.ppermute(near, axes, chips)
    far = lax.ppermute(far, axes, far_chips)
    *results, token = local(got)

    def theirs(x):
        return jnp.where(core == 0, x[capacity : 2 * capacity], x[:capacity])

    parts = [theirs(near[at : at + 2 * capacity]), theirs(near[at + 2 * capacity :]), theirs(far[: 2 * capacity])]
    last = jnp.concatenate(parts + [token], axis=0)
    totals = direct(results, got, near, far, last)
    return lax.ppermute(last, axes, cores), totals, results


def body(
    state, velocity, levels, neighbours, records, counts, stiffness, trace_map, lift, projection
):
    elements, modes = state.shape
    width = trace_map.shape[1]
    slots = records.shape[1]
    capacity = slots // counts.shape[1]
    rim = elements // 8
    core = lax.axis_index("pair")

    def array(shape, dtype):
        return jax.ShapeDtypeStruct(shape, dtype)

    def like(x):
        return array(x.shape, x.dtype)

    sent = [
        array((elements, width), bf16),
        array((3 * rim + 4 * capacity, 128), bf16),
        array((3 * rim + 4 * capacity, 128), bf16),
    ]
    whole = array((elements, modes), f32)
    faces = array((elements, width), f32)
    blocks = pltpu.VMEM((slots, 128), bf16)
    column_shape = array((slots, 128), f32)
    mark = array((16, 128), bf16)

    levels = levels.reshape(1, elements)
    vmem = pltpu.VMEM
    wide = (elements, 128)
    near_state, trace_map, projection, traces, first, own, source_hot, column, element_column = call(
        start_kernel,
        [like(state), like(trace_map), like(projection)]
        + sent
        + [array((slots, elements), bf16), column_shape, array(wide, f32)],
        [vmem(x.shape, x.dtype) for x in (records, counts, velocity, levels, neighbours)]
        + [blocks, pltpu.SemaphoreType.DMA((9,))],
        2 * 10**8,
        (state, trace_map, records, counts, velocity, levels, neighbours, projection),
        (),
    )

    def local(got):
        return call(
            local_kernel,
            [like(stiffness), like(lift), whole, faces, faces, array((elements, 12 * rim), bf16), mark],
            [pltpu.SemaphoreType.DMA((2,))],
            3 * 10**9,
            (stiffness, lift),
            (element_column, near_state, traces, got),
        )

    def direct(results, *arrived):
        return call(
            direct_kernel,
            [faces, array((5 * capacity, 128), f32), array((elements, 5 * capacity), bf16)],
            [vmem((5 * capacity, 128), bf16)],
            10**9,
            (),
            (results[5], results[3], *arrived),
        )

    last, (partial, *direct_targets), (near_stiffness, near_lift, base, _, inflow, picks) = exchange(
        first, own, core, capacity, local, direct
    )
    field, traces, first, own, face, element_hot = call(
        middle_kernel,
        [whole] + sent + [array((3 * capacity, 128), f32), array((elements, 3 * capacity), bf16)],
        [blocks],
        10**9,
        (),
        (near_lift, base, partial, inflow, last, trace_map, projection, source_hot, column),
    )

    def second_local(got):
        return call(
            second_local_kernel,
            [whole, faces, mark],
            [],
            3 * 10**9,
            (),
            (element_column, state, field, near_stiffness, traces, got),
        )

    def second_direct(results, *arrived):
        return call(
            second_direct_kernel,
            [faces],
            [vmem((5 * capacity, 128), bf16)],
            10**9,
            (),
            (picks, results[1], *direct_targets, *arrived),
        )

    last, (partial,), (base, _) = exchange(first, own, core, capacity, second_local, second_direct)
    return call(
        end_kernel,
        [whole],
        [vmem((elements, modes), f32), pltpu.SemaphoreType.DMA((2,))],
        10**9,
        (),
        (near_lift, base, partial, inflow, last, face, element_hot),
        out_space=pl.ANY,
    )[0]


def solution(mesh):
    placed = (
        P(("groups", "curve", "sub", "pair"), None),
        P(None, ("groups", "curve", "sub", "pair")),
        P(("groups", "curve", "sub", "pair")),
        P(None, ("groups", "curve", "sub", "pair")),
        P(None, ("groups", "curve", "sub", "pair")),
        P(("groups", "curve", "sub", "pair"), None),
        P(),
        P(),
        P(),
        P(),
    )
    return jax.shard_map(
        body,
        mesh=mesh,
        in_specs=placed,
        out_specs=P(("groups", "curve", "sub", "pair"), None),
        check_vma=False,
    )
```

```python
import jax
import jax.numpy as jnp
from jax import lax
from jax.experimental import pallas as pl
from jax.experimental.pallas import tpu as pltpu
from jax.sharding import PartitionSpec as P

time_step = 0.3
bf16 = jnp.bfloat16
f32 = jnp.float32
CURVE = ("curve", "sub", "pair")


def dot(a, b):
    return jnp.dot(a, b, preferred_element_type=f32)


def transposed(rows):
    pad = jnp.zeros((128 - rows.shape[0], rows.shape[1]), f32)
    return jnp.concatenate([rows, pad], axis=0).T


def lanes(shape):
    return lax.broadcasted_iota(jnp.int32, shape, 1)


def rows_of(shape):
    return lax.broadcasted_iota(jnp.int32, shape, 0)


def swapped(tile):
    turned = pltpu.roll(tile.astype(f32), 64, 1)
    low = lanes(turned.shape) < 64
    top = jnp.where(low, turned, 0.0).astype(bf16)
    bottom = jnp.where(low, 0.0, turned).astype(bf16)
    return jnp.concatenate([top, bottom], axis=0)


def hot(column, width):
    rows = column.shape[0]
    picked = column.astype(jnp.int32) == lanes((rows, width))
    return jnp.where(picked, 1.0, 0.0).astype(bf16)


def place():
    return lax.axis_index("curve") * lax.axis_size("sub") + lax.axis_index("sub"), lax.axis_index("pair")


def record_columns(records, counts):
    slots = records.shape[1]
    capacity = slots // 8
    source, face, kind, target = (records[i : i + 1, :] for i in range(4))
    slot = lanes((1, slots))
    allowed = jnp.zeros((1, slots), jnp.int32)
    for j in range(8):
        inside = (slot >= j * capacity) & (slot < (j + 1) * capacity)
        allowed = jnp.where(inside, counts[:, j : j + 1] + j * capacity, allowed)
    facing = jnp.where(slot < allowed, jnp.bitwise_xor(face, 1) + 1, 0)
    digits = [lax.shift_right_logical(target, 4), jnp.bitwise_and(target, 15), facing]
    gap = jnp.zeros((61, slots), f32)
    rows = [x.astype(f32) for x in (source, face, kind)] + [gap] + [x.astype(f32) for x in digits]
    return transposed(jnp.concatenate(rows, axis=0))


def send(traces, source_hot, column, projection, first_out, own_out, blocks):
    elements, width = traces.shape
    slots = column.shape[0]
    capacity = slots // 8
    rim = elements // 8
    core = lax.axis_index("pair")
    shape = (slots, 128)
    lane = lanes(shape)
    half = jnp.where(lane < 64, 0.0, 1.0)
    picked = dot(source_hot, traces[...])
    face = column[:, 1:2]
    row = jnp.zeros(shape, f32)
    for t in range(3):
        row = jnp.where(half + 2 * t == face, picked[:, 128 * t : 128 * t + 128], row)
    every = dot(row.astype(bf16), jnp.concatenate([projection[...]] * 2, axis=0))
    kind = column[:, 2:3]
    folded = jnp.zeros(shape, f32)
    for t in range(4):
        folded = jnp.where(half + 2 * t == kind, every[:, 128 * t : 128 * t + 128], folded)
    piece = folded + pltpu.roll(folded, 64, 1)
    blocks[...] = jnp.where(lane < 64, piece, column[...]).astype(bf16)

    def block(at_first, at_second):
        index = at_first + core * (at_second - at_first)
        return blocks[pl.ds(pl.multiple_of(index * capacity, capacity), capacity), :]

    final_at = pl.multiple_of((1 - core) * (elements - rim), rim)
    other_at = pl.multiple_of(core * (elements - rim), rim)
    for t in range(3):
        cut = slice(128 * t, 128 * t + 128)
        rows = slice(rim * t, rim * t + rim)
        first_out[rows, :] = traces[pl.ds(final_at, rim), cut]
        own_out[rows, :] = traces[pl.ds(other_at, rim), cut]
    at = 3 * rim
    there = [(4, 3), (5, 1), (6, 2), (7, 0)]
    here = [(2, 4), (3, 5), (0, 6), (1, 7)]
    for i in range(4):
        rows = slice(at + capacity * i, at + capacity * i + capacity)
        first_out[rows, :] = block(*there[i])
        own_out[rows, :] = block(*here[i])


def start_kernel(
    state_in, trace_map_in, records_in, counts_in, velocity_in, levels_in, neighbours_in, projection_in,
    state, trace_map, projection, traces, first_out, own_out, source_hot, column, elements_column,
    records, counts, velocity, levels, neighbours, blocks, sems
):
    elements = state.shape[0]
    part = elements // 2
    pairs = [(records_in, records), (counts_in, counts), (velocity_in, velocity), (levels_in, levels)]
    pairs += [(neighbours_in, neighbours), (trace_map_in, trace_map)]
    for i in range(2):
        cut = pl.ds(i * part, part)
        pairs.append((state_in.at[cut], state.at[cut]))
    pairs.append((projection_in, projection))
    copies = [pltpu.make_async_copy(a, b, sems.at[i]) for i, (a, b) in enumerate(pairs)]
    for copy in copies:
        copy.start()
    for copy in copies[:5]:
        copy.wait()
    columns = record_columns(records, counts)
    column[...] = columns
    source_hot[...] = hot(columns[:, 0:1], elements)
    elements_column[...] = element_columns(velocity, levels, neighbours)
    copies[5].wait()
    for i in range(2):
        copies[6 + i].wait()
        cut = slice(i * part, i * part + part)
        traces[cut, :] = dot(state[cut, :].astype(bf16), trace_map[...]).astype(bf16)
    copies[8].wait()
    send(traces, source_hot[...], column, projection, first_out, own_out, blocks)


def element_columns(velocity, levels, neighbours):
    elements = velocity.shape[1]
    rim = elements // 8
    chip, core = place()
    raw = neighbours[...].astype(f32)
    local = raw - ((2 * chip + core) * elements).astype(f32)
    before = ((2 - core) * rim).astype(f32)
    after = (elements - core * rim).astype(f32)
    index = jnp.where(local < 0, local + before, jnp.where(local >= elements, local - after, -1.0))
    index = jnp.where(raw < 0, -1.0, index)
    scale = jnp.exp2(levels[...].astype(f32)) * 0.25
    gap = jnp.zeros((4, elements), f32)
    return transposed(jnp.concatenate([velocity[...], scale, gap, local, gap[0:2], index], axis=0))


def volume_term(column, lowered, stiffness, n, step):
    modes = stiffness.shape[0]
    volume = jnp.zeros((lowered.shape[0], step), f32)
    for d in range(3):
        volume += column[:, d : d + 1] * dot(lowered, stiffness[:, d * modes + n : d * modes + n + step])
    return column[:, 3:4] * volume


def own_part(column, traces, partial_out):
    elements = traces.shape[0]
    for t in range(3):
        tile = traces[:, 128 * t : 128 * t + 128]
        at = 8 + 2 * t
        picks = [hot(column[:, at + i : at + i + 1], elements) for i in range(2)]
        near = dot(jnp.concatenate(picks, axis=1), swapped(tile))
        partial_out[:, 128 * t : 128 * t + 128] = near - tile.astype(f32)


def local_kernel(stiffness_in, lift_in, column, state, traces, got, stiffness, lift, base, partial, inflow, picks, token, sems):
    token[...] = got[0:16, :]
    elements, modes = state.shape
    rim = elements // 8
    copies = [
        pltpu.make_async_copy(stiffness_in, stiffness, sems.at[0]),
        pltpu.make_async_copy(lift_in, lift, sems.at[1]),
    ]
    for copy in copies:
        copy.start()
    columns = column[...]
    own_part(columns, traces, partial)
    low = lanes((elements, 128)) < 64
    for t in range(3):
        speed = columns[:, t : t + 1]
        inflow[:, 128 * t : 128 * t + 128] = columns[:, 3:4] * jnp.maximum(jnp.where(low, speed, -speed), 0.0)
    for i in range(6):
        picks[:, 2 * rim * i : 2 * rim * i + 2 * rim] = hot(columns[:, 16 + i : 17 + i], 2 * rim)
    lowered = state[...].astype(bf16)
    step = 256
    copies[0].wait()
    for n in range(0, modes, step):
        base[:, n : n + step] = state[:, n : n + step] + time_step * volume_term(columns, lowered, stiffness, n, step)
    copies[1].wait()


def second_local_kernel(column, state, field, stiffness, traces, got, base, partial, token):
    token[...] = got[0:16, :]
    modes = state.shape[1]
    columns = column[...]
    lowered = field[...].astype(bf16)
    step = 256
    for n in range(0, modes, step):
        volume = volume_term(columns, lowered, stiffness, n, step)
        base[:, n : n + step] = 0.5 * (state[:, n : n + step] + field[:, n : n + step]) + 0.5 * time_step * volume
    own_part(columns, traces, partial)


def direct_pieces(got, near, far, arrived):
    capacity = arrived.shape[0] // 5
    at = 6 * capacity
    core = lax.axis_index("pair")

    def mine(ref, start):
        return ref[pl.ds(pl.multiple_of(start + core * capacity, capacity), capacity), :]

    blocks = [
        got[at : at + capacity, :],
        mine(near, at),
        mine(near, at + 2 * capacity),
        mine(far, 0),
        far[2 * capacity : 3 * capacity, :],
    ]
    for i, block in enumerate(blocks):
        arrived[capacity * i : capacity * i + capacity, :] = block
    return arrived[...]


def targets(pieces, elements):
    face_of = jnp.where(rows_of((128, 128)) == 66, 1.0, 0.0).astype(bf16)
    face = dot(pieces, face_of) - 1.0
    lane = lanes((8, 128))
    element_of = jnp.where(lane == 64, 16.0, jnp.where(lane == 65, 1.0, 0.0)).astype(bf16)
    target = lax.dot_general(element_of, pieces, (((1,), (1,)), ((), ())), preferred_element_type=f32)[0:1, :]
    match = rows_of((elements, pieces.shape[0])) == target.astype(jnp.int32)
    return face, jnp.where(match, 1.0, 0.0).astype(bf16)


def mortar_term(pieces, face, element_hot, t):
    half = jnp.where(lanes(pieces.shape) < 64, 0.0, 1.0)
    plain = jnp.where(half == 0.0, pieces.astype(f32), 0.0)
    both = plain + pltpu.roll(plain, 64, 1)
    return dot(element_hot, jnp.where(half + 2 * t == face, both, 0.0).astype(bf16))


def add_direct(picks, partial, got, near, pieces, face, element_hot, total):
    rim = picks.shape[1] // 12
    for t in range(3):
        cut = slice(128 * t, 128 * t + 128)
        rows = slice(rim * t, rim * t + rim)
        window = jnp.concatenate([got[rows, :], near[rows, :]], axis=0)
        conforming = dot(picks[:, 4 * rim * t : 4 * rim * t + 4 * rim], swapped(window))
        total[:, cut] = partial[:, cut] + conforming + mortar_term(pieces, face, element_hot, t)


def direct_kernel(picks, partial, got, near, far, last, total, face_out, element_hot_out, arrived):
    pieces = direct_pieces(got, near, far, arrived)
    face, element_hot = targets(pieces, partial.shape[0])
    face_out[...] = face
    element_hot_out[...] = element_hot
    add_direct(picks, partial, got, near, pieces, face, element_hot, total)


def second_direct_kernel(picks, partial, face, element_hot, got, near, far, last, total, arrived):
    pieces = direct_pieces(got, near, far, arrived)
    add_direct(picks, partial, got, near, pieces, face[...], element_hot[...], total)


def fluxes(pieces, face, element_hot, partial, inflow):
    parts = []
    for t in range(3):
        cut = slice(128 * t, 128 * t + 128)
        total = partial[:, cut] + mortar_term(pieces, face, element_hot, t)
        parts.append((inflow[:, cut] * total).astype(bf16))
    return jnp.concatenate(parts, axis=1)


def middle_kernel(
    lift, base, partial, inflow, last, trace_map, projection, source_hot, column,
    field, traces, first_out, own_out, face_out, element_hot_out, blocks
):
    elements = base.shape[0]
    pieces = last[0 : face_out.shape[0], :]
    face, element_hot = targets(pieces, elements)
    face_out[...] = face
    element_hot_out[...] = element_hot
    flux = fluxes(pieces, face, element_hot, partial, inflow)
    new = base[...] + time_step * dot(flux, lift[...])
    field[...] = new
    traces[...] = dot(new.astype(bf16), trace_map[...]).astype(bf16)
    send(traces, source_hot[...], column, projection, first_out, own_out, blocks)


def end_kernel(lift, base, partial, inflow, last, face, element_hot, field, result, sems):
    elements = base.shape[0]
    flux = fluxes(last[0 : face.shape[0], :], face[...], element_hot[...], partial, inflow)
    part = elements // 4
    copies = []
    for i in range(4):
        cut = slice(part * i, part * i + part)
        result[cut, :] = base[cut, :] + 0.5 * time_step * dot(flux[cut, :], lift[...])
        rows = pl.ds(part * i, part)
        copies.append(pltpu.make_async_copy(result.at[rows], field.at[rows], sems.at[i]))
        copies[i].start()
    for copy in copies:
        copy.wait()


def paired(groups, count, step, lower):
    partner = {}
    for s in range(count):
        if lower(s) and s + step < count:
            partner[s] = s + step
            partner[s + step] = s
    pairs = []
    for g in range(groups):
        for s in range(count):
            if s in partner:
                pairs.append((g * count + s, g * count + partner[s]))
            elif g ^ 1 < groups:
                pairs.append((g * count + s, (g ^ 1) * count + s))
    return pairs


def call(kernel, out_shape, scratch, flops, far, near, out_space=pltpu.VMEM):
    operands = [pltpu.with_memory_space_constraint(x, pltpu.HBM) for x in far] + list(near)
    read = sum(x.size * x.dtype.itemsize for x in operands) if flops > 10**8 else 10**5
    specs = [pl.BlockSpec(memory_space=pl.ANY)] * len(far) + [pl.BlockSpec(memory_space=pltpu.VMEM)] * len(near)
    return pl.pallas_call(
        kernel,
        out_shape=out_shape,
        in_specs=specs,
        out_specs=[pl.BlockSpec(memory_space=out_space)] * len(out_shape),
        scratch_shapes=scratch,
        compiler_params=pltpu.CompilerParams(vmem_limit_bytes=16 * 1024 * 1024),
        cost_estimate=pl.CostEstimate(flops=flops, bytes_accessed=read, transcendentals=0),
    )(*operands)


def exchange(first, own, core, capacity, local, direct):
    axes = ("groups",) + CURVE
    groups, count = lax.axis_size("groups"), lax.axis_size(CURVE)
    cores = paired(groups, count, 1, lambda s: s % 2 == 0)
    chips = paired(groups, count, 1, lambda s: s % 2 == 1)
    far_chips = paired(groups, count, 3, lambda s: s % 2 == 1)
    at = own.shape[0] - 4 * capacity
    got = lax.ppermute(first, axes, cores)
    near = jnp.concatenate([own[: at + 2 * capacity], got[at + capacity : at + 3 * capacity]], axis=0)
    far = jnp.concatenate([own[at + 2 * capacity :], got[at + 3 * capacity :]], axis=0)
    near = lax.ppermute(near, axes, chips)
    far = lax.ppermute(far, axes, far_chips)
    *results, token = local(got)

    def theirs(x):
        return jnp.where(core == 0, x[capacity : 2 * capacity], x[:capacity])

    parts = [theirs(near[at : at + 2 * capacity]), theirs(near[at + 2 * capacity :]), theirs(far[: 2 * capacity]), theirs(far[capacity:])]
    last = jnp.concatenate(parts + [token], axis=0)
    totals = direct(results, got, near, far, last)
    return lax.ppermute(last, axes, cores), totals, results


def body(
    state, velocity, levels, neighbours, records, counts, stiffness, trace_map, lift, projection
):
    elements, modes = state.shape
    width = trace_map.shape[1]
    slots = records.shape[1]
    capacity = slots // counts.shape[1]
    rim = elements // 8
    core = lax.axis_index("pair")

    def array(shape, dtype):
        return jax.ShapeDtypeStruct(shape, dtype)

    def like(x):
        return array(x.shape, x.dtype)

    sent = [
        array((elements, width), bf16),
        array((3 * rim + 4 * capacity, 128), bf16),
        array((3 * rim + 4 * capacity, 128), bf16),
    ]
    whole = array((elements, modes), f32)
    faces = array((elements, width), f32)
    blocks = pltpu.VMEM((slots, 128), bf16)
    column_shape = array((slots, 128), f32)
    mark = array((16, 128), bf16)

    levels = levels.reshape(1, elements)
    vmem = pltpu.VMEM
    wide = (elements, 128)
    near_state, trace_map, projection, traces, first, own, source_hot, column, element_column = call(
        start_kernel,
        [like(state), like(trace_map), like(projection)]
        + sent
        + [array((slots, elements), bf16), column_shape, array(wide, f32)],
        [vmem(x.shape, x.dtype) for x in (records, counts, velocity, levels, neighbours)]
        + [blocks, pltpu.SemaphoreType.DMA((9,))],
        2 * 10**8,
        (state, trace_map, records, counts, velocity, levels, neighbours, projection),
        (),
    )

    def local(got):
        return call(
            local_kernel,
            [like(stiffness), like(lift), whole, faces, faces, array((elements, 12 * rim), bf16), mark],
            [pltpu.SemaphoreType.DMA((2,))],
            10**8,
            (stiffness, lift),
            (element_column, near_state, traces, got),
        )

    def direct(results, *arrived):
        return call(
            direct_kernel,
            [faces, array((5 * capacity, 128), f32), array((elements, 5 * capacity), bf16)],
            [vmem((5 * capacity, 128), bf16)],
            10**9,
            (),
            (results[5], results[3], *arrived),
        )

    last, (partial, *direct_targets), (near_stiffness, near_lift, base, _, inflow, picks) = exchange(
        first, own, core, capacity, local, direct
    )
    field, traces, first, own, face, element_hot = call(
        middle_kernel,
        [whole] + sent + [array((3 * capacity, 128), f32), array((elements, 3 * capacity), bf16)],
        [blocks],
        10**9,
        (),
        (near_lift, base, partial, inflow, last, trace_map, projection, source_hot, column),
    )

    def second_local(got):
        return call(
            second_local_kernel,
            [whole, faces, mark],
            [],
            10**8,
            (),
            (element_column, state, field, near_stiffness, traces, got),
        )

    def second_direct(results, *arrived):
        return call(
            second_direct_kernel,
            [faces],
            [vmem((5 * capacity, 128), bf16)],
            10**9,
            (),
            (picks, results[1], *direct_targets, *arrived),
        )

    last, (partial,), (base, _) = exchange(first, own, core, capacity, second_local, second_direct)
    return call(
        end_kernel,
        [whole],
        [vmem((elements, modes), f32), pltpu.SemaphoreType.DMA((4,))],
        10**9,
        (),
        (near_lift, base, partial, inflow, last, face, element_hot),
        out_space=pl.ANY,
    )[0]


def solution(mesh):
    placed = (
        P(("groups", "curve", "sub", "pair"), None),
        P(None, ("groups", "curve", "sub", "pair")),
        P(("groups", "curve", "sub", "pair")),
        P(None, ("groups", "curve", "sub", "pair")),
        P(None, ("groups", "curve", "sub", "pair")),
        P(("groups", "curve", "sub", "pair"), None),
        P(),
        P(),
        P(),
        P(),
    )
    return jax.shard_map(
        body,
        mesh=mesh,
        in_specs=placed,
        out_specs=P(("groups", "curve", "sub", "pair"), None),
        check_vma=False,
    )
```

```python
import jax
import jax.numpy as jnp
from jax import lax
from jax.experimental import pallas as pl
from jax.experimental.pallas import tpu as pltpu
from jax.sharding import PartitionSpec as P

time_step = 0.3
bf16 = jnp.bfloat16
f32 = jnp.float32
CURVE = ("curve", "sub", "pair")


def dot(a, b):
    return jnp.dot(a, b, preferred_element_type=f32)


def transposed(rows):
    pad = jnp.zeros((128 - rows.shape[0], rows.shape[1]), f32)
    return jnp.concatenate([rows, pad], axis=0).T


def lanes(shape):
    return lax.broadcasted_iota(jnp.int32, shape, 1)


def rows_of(shape):
    return lax.broadcasted_iota(jnp.int32, shape, 0)


def swapped(tile):
    turned = pltpu.roll(tile.astype(f32), 64, 1)
    low = lanes(turned.shape) < 64
    top = jnp.where(low, turned, 0.0).astype(bf16)
    bottom = jnp.where(low, 0.0, turned).astype(bf16)
    return jnp.concatenate([top, bottom], axis=0)


def hot(column, width):
    rows = column.shape[0]
    picked = column.astype(jnp.int32) == lanes((rows, width))
    return jnp.where(picked, 1.0, 0.0).astype(bf16)


def place():
    return lax.axis_index("curve") * lax.axis_size("sub") + lax.axis_index("sub"), lax.axis_index("pair")


def record_columns(records, counts):
    slots = records.shape[1]
    capacity = slots // 8
    source, face, kind, target = (records[i : i + 1, :] for i in range(4))
    slot = lanes((1, slots))
    allowed = jnp.zeros((1, slots), jnp.int32)
    for j in range(8):
        inside = (slot >= j * capacity) & (slot < (j + 1) * capacity)
        allowed = jnp.where(inside, counts[:, j : j + 1] + j * capacity, allowed)
    facing = jnp.where(slot < allowed, jnp.bitwise_xor(face, 1) + 1, 0)
    digits = [lax.shift_right_logical(target, 4), jnp.bitwise_and(target, 15), facing]
    gap = jnp.zeros((61, slots), f32)
    rows = [x.astype(f32) for x in (source, face, kind)] + [gap] + [x.astype(f32) for x in digits]
    return transposed(jnp.concatenate(rows, axis=0))


def send(traces, source_hot, column, projection, first_out, rim_out, own_out, blocks, with_codes):
    elements, width = traces.shape
    slots = column.shape[0]
    capacity = slots // 8
    rim = elements // 8
    core = lax.axis_index("pair")
    shape = (slots, 128)
    lane = lanes(shape)
    half = jnp.where(lane < 64, 0.0, 1.0)
    picked = dot(source_hot, traces[...])
    face = column[:, 1:2]
    row = jnp.zeros(shape, f32)
    for t in range(3):
        row = jnp.where(half + 2 * t == face, picked[:, 128 * t : 128 * t + 128], row)
    every = dot(row.astype(bf16), jnp.concatenate([projection[...]] * 2, axis=0))
    kind = column[:, 2:3]
    folded = jnp.zeros(shape, f32)
    for t in range(4):
        folded = jnp.where(half + 2 * t == kind, every[:, 128 * t : 128 * t + 128], folded)
    piece = folded + pltpu.roll(folded, 64, 1)
    if with_codes:
        piece = jnp.where(lane < 64, piece, column[...])
    blocks[...] = piece.astype(bf16)

    def block(at_first, at_second):
        index = at_first + core * (at_second - at_first)
        return blocks[pl.ds(pl.multiple_of(index * capacity, capacity), capacity), :]

    final_at = pl.multiple_of((1 - core) * (elements - rim), rim)
    other_at = pl.multiple_of(core * (elements - rim), rim)
    for t in range(3):
        cut = slice(128 * t, 128 * t + 128)
        rows = slice(rim * t, rim * t + rim)
        first_out[rows, :] = traces[pl.ds(final_at, rim), cut]
        rim_out[rows, :] = traces[pl.ds(other_at, rim), cut]
    at = 3 * rim
    there = [(4, 3), (5, 1), (6, 2), (7, 0)]
    here = [(2, 4), (3, 5), (0, 6), (1, 7)]
    if with_codes:
        for i in range(4):
            rows = slice(at + capacity * i, at + capacity * i + capacity)
            first_out[rows, :] = block(*there[i])
            own_out[rows, :] = block(*here[i])
        return
    low = lanes((capacity, 128)) < 64

    def pair(a, b):
        return jnp.where(low, block(*a), block(*b))

    first_out[at : at + capacity, :] = pair(there[0], there[3])
    first_out[at + capacity :, :] = pair(there[1], there[2])
    own_out[0:capacity, :] = pair(here[0], here[1])
    own_out[capacity:, :] = pair(here[2], here[3])


def start_kernel(
    state_in, trace_map_in, records_in, counts_in, velocity_in, levels_in, neighbours_in, projection_in,
    state, trace_map, projection, traces, first_out, own_out, source_hot, column, elements_column,
    records, counts, velocity, levels, neighbours, blocks, sems
):
    elements = state.shape[0]
    part = elements // 2
    pairs = [(records_in, records), (counts_in, counts), (velocity_in, velocity), (levels_in, levels)]
    pairs += [(neighbours_in, neighbours), (trace_map_in, trace_map)]
    for i in range(2):
        cut = pl.ds(i * part, part)
        pairs.append((state_in.at[cut], state.at[cut]))
    pairs.append((projection_in, projection))
    copies = [pltpu.make_async_copy(a, b, sems.at[i]) for i, (a, b) in enumerate(pairs)]
    for copy in copies:
        copy.start()
    for copy in copies[:5]:
        copy.wait()
    columns = record_columns(records, counts)
    column[...] = columns
    source_hot[...] = hot(columns[:, 0:1], elements)
    elements_column[...] = element_columns(velocity, levels, neighbours)
    copies[5].wait()
    for i in range(2):
        copies[6 + i].wait()
        cut = slice(i * part, i * part + part)
        traces[cut, :] = dot(state[cut, :].astype(bf16), trace_map[...]).astype(bf16)
    copies[8].wait()
    send(traces, source_hot[...], column, projection, first_out, own_out, own_out, blocks, True)


def element_columns(velocity, levels, neighbours):
    elements = velocity.shape[1]
    rim = elements // 8
    chip, core = place()
    raw = neighbours[...].astype(f32)
    local = raw - ((2 * chip + core) * elements).astype(f32)
    before = ((2 - core) * rim).astype(f32)
    after = (elements - core * rim).astype(f32)
    index = jnp.where(local < 0, local + before, jnp.where(local >= elements, local - after, -1.0))
    index = jnp.where(raw < 0, -1.0, index)
    scale = jnp.exp2(levels[...].astype(f32)) * 0.25
    gap = jnp.zeros((4, elements), f32)
    return transposed(jnp.concatenate([velocity[...], scale, gap, local, gap[0:2], index], axis=0))


def volume_term(column, lowered, stiffness, n, step):
    modes = stiffness.shape[0]
    volume = jnp.zeros((lowered.shape[0], step), f32)
    for d in range(3):
        volume += column[:, d : d + 1] * dot(lowered, stiffness[:, d * modes + n : d * modes + n + step])
    return column[:, 3:4] * volume


def own_part(column, traces, partial_out):
    elements = traces.shape[0]
    for t in range(3):
        tile = traces[:, 128 * t : 128 * t + 128]
        at = 8 + 2 * t
        picks = [hot(column[:, at + i : at + i + 1], elements) for i in range(2)]
        near = dot(jnp.concatenate(picks, axis=1), swapped(tile))
        partial_out[:, 128 * t : 128 * t + 128] = near - tile.astype(f32)


def own_kernel(column, traces, partial):
    own_part(column[...], traces, partial)


def local_kernel(stiffness_in, lift_in, column, state, got, stiffness, lift, base, inflow, picks, token, sems):
    token[...] = got[0:16, :]
    elements, modes = state.shape
    rim = elements // 8
    copies = [
        pltpu.make_async_copy(stiffness_in, stiffness, sems.at[0]),
        pltpu.make_async_copy(lift_in, lift, sems.at[1]),
    ]
    for copy in copies:
        copy.start()
    columns = column[...]
    low = lanes((elements, 128)) < 64
    for t in range(3):
        speed = columns[:, t : t + 1]
        inflow[:, 128 * t : 128 * t + 128] = columns[:, 3:4] * jnp.maximum(jnp.where(low, speed, -speed), 0.0)
    for i in range(6):
        picks[:, 2 * rim * i : 2 * rim * i + 2 * rim] = hot(columns[:, 16 + i : 17 + i], 2 * rim)
    lowered = state[...].astype(bf16)
    step = 256
    copies[0].wait()
    for n in range(0, modes, step):
        base[:, n : n + step] = state[:, n : n + step] + time_step * volume_term(columns, lowered, stiffness, n, step)
    copies[1].wait()


def second_local_kernel(column, state, field, stiffness, traces, got, base, partial, token):
    token[...] = got[0:16, :]
    modes = state.shape[1]
    columns = column[...]
    lowered = field[...].astype(bf16)
    step = 256
    for n in range(0, modes, step):
        volume = volume_term(columns, lowered, stiffness, n, step)
        base[:, n : n + step] = 0.5 * (state[:, n : n + step] + field[:, n : n + step]) + 0.5 * time_step * volume
    own_part(columns, traces, partial)


def direct_pieces(got, near, far, arrived):
    capacity = arrived.shape[0] // 5
    at = 6 * capacity
    core = lax.axis_index("pair")

    def mine(ref, start):
        return ref[pl.ds(pl.multiple_of(start + core * capacity, capacity), capacity), :]

    blocks = [
        got[at : at + capacity, :],
        mine(near, at),
        mine(near, at + 2 * capacity),
        mine(far, 0),
        far[2 * capacity : 3 * capacity, :],
    ]
    for i, block in enumerate(blocks):
        arrived[capacity * i : capacity * i + capacity, :] = block
    return arrived[...]


def in_both(pieces, which):
    half = jnp.where(lanes(pieces.shape) < 64, 0, 1)
    kept = jnp.where(half == which, pieces.astype(f32), 0.0)
    return kept + pltpu.roll(kept, 64, 1)


def direct_pairs(got, near, far, arrived):
    capacity = arrived.shape[0] // 5
    at = 6 * capacity
    core = lax.axis_index("pair")
    blocks = [
        (got[at : at + capacity, :], 0),
        (near[0:capacity, :], core),
        (near[capacity : 2 * capacity, :], core),
        (far[0:capacity, :], core),
        (far[capacity : 2 * capacity, :], 1),
    ]
    for i, (block, which) in enumerate(blocks):
        arrived[capacity * i : capacity * i + capacity, :] = in_both(block, which)
    return arrived[...]


def targets(pieces, elements):
    face_of = jnp.where(rows_of((128, 128)) == 66, 1.0, 0.0).astype(bf16)
    face = dot(pieces, face_of) - 1.0
    lane = lanes((8, 128))
    element_of = jnp.where(lane == 64, 16.0, jnp.where(lane == 65, 1.0, 0.0)).astype(bf16)
    target = lax.dot_general(element_of, pieces, (((1,), (1,)), ((), ())), preferred_element_type=f32)[0:1, :]
    match = rows_of((elements, pieces.shape[0])) == target.astype(jnp.int32)
    return face, jnp.where(match, 1.0, 0.0).astype(bf16)


def mortar_term(both, face, element_hot, t):
    half = jnp.where(lanes(both.shape) < 64, 0.0, 1.0)
    return dot(element_hot, jnp.where(half + 2 * t == face, both, 0.0).astype(bf16))


def add_direct(picks, partial, got, near, both, face, element_hot, total):
    rim = picks.shape[1] // 12
    for t in range(3):
        cut = slice(128 * t, 128 * t + 128)
        rows = slice(rim * t, rim * t + rim)
        window = jnp.concatenate([got[rows, :], near[rows, :]], axis=0)
        conforming = dot(picks[:, 4 * rim * t : 4 * rim * t + 4 * rim], swapped(window))
        total[:, cut] = partial[:, cut] + conforming + mortar_term(both, face, element_hot, t)


def direct_kernel(picks, partial, got, near, far, last, total, face_out, element_hot_out, arrived):
    pieces = direct_pieces(got, near, far, arrived)
    face, element_hot = targets(pieces, partial.shape[0])
    face_out[...] = face
    element_hot_out[...] = element_hot
    add_direct(picks, partial, got, near, in_both(pieces, 0), face, element_hot, total)


def second_direct_kernel(picks, partial, face, element_hot, got, rim, near, far, last, total, arrived):
    both = direct_pairs(got, near, far, arrived)
    add_direct(picks, partial, got, rim, both, face[...], element_hot[...], total)


def fluxes(both, face, element_hot, partial, inflow):
    parts = []
    for t in range(3):
        cut = slice(128 * t, 128 * t + 128)
        total = partial[:, cut] + mortar_term(both, face, element_hot, t)
        parts.append((inflow[:, cut] * total).astype(bf16))
    return jnp.concatenate(parts, axis=1)


def middle_kernel(
    lift, base, partial, inflow, last, trace_map, projection, source_hot, column,
    field, traces, first_out, rim_out, own_out, face_out, element_hot_out, blocks
):
    elements = base.shape[0]
    pieces = last[0 : face_out.shape[0], :]
    face, element_hot = targets(pieces, elements)
    face_out[...] = face
    element_hot_out[...] = element_hot
    flux = fluxes(in_both(pieces, 0), face, element_hot, partial, inflow)
    new = base[...] + time_step * dot(flux, lift[...])
    field[...] = new
    traces[...] = dot(new.astype(bf16), trace_map[...]).astype(bf16)
    send(traces, source_hot[...], column, projection, first_out, rim_out, own_out, blocks, False)


def end_kernel(lift, base, partial, inflow, last, face, element_hot, field, result, sems):
    elements = base.shape[0]
    capacity = face.shape[0] // 3
    core = lax.axis_index("pair")
    far = last[pl.ds(pl.multiple_of((3 - core) * capacity, capacity), capacity), :]
    both = in_both(jnp.concatenate([last[0 : 2 * capacity, :], far], axis=0), core)
    flux = fluxes(both, face[...], element_hot[...], partial, inflow)
    part = elements // 4
    copies = []
    for i in range(4):
        cut = slice(part * i, part * i + part)
        result[cut, :] = base[cut, :] + 0.5 * time_step * dot(flux[cut, :], lift[...])
        rows = pl.ds(part * i, part)
        copies.append(pltpu.make_async_copy(result.at[rows], field.at[rows], sems.at[i]))
        copies[i].start()
    for copy in copies:
        copy.wait()


def paired(groups, count, step, lower):
    partner = {}
    for s in range(count):
        if lower(s) and s + step < count:
            partner[s] = s + step
            partner[s + step] = s
    pairs = []
    for g in range(groups):
        for s in range(count):
            if s in partner:
                pairs.append((g * count + s, g * count + partner[s]))
            elif g ^ 1 < groups:
                pairs.append((g * count + s, (g ^ 1) * count + s))
    return pairs


def call(kernel, out_shape, scratch, flops, far, near, out_space=pltpu.VMEM):
    operands = [pltpu.with_memory_space_constraint(x, pltpu.HBM) for x in far] + list(near)
    read = sum(x.size * x.dtype.itemsize for x in operands) if flops > 10**8 else 10**5
    specs = [pl.BlockSpec(memory_space=pl.ANY)] * len(far) + [pl.BlockSpec(memory_space=pltpu.VMEM)] * len(near)
    return pl.pallas_call(
        kernel,
        out_shape=out_shape,
        in_specs=specs,
        out_specs=[pl.BlockSpec(memory_space=out_space)] * len(out_shape),
        scratch_shapes=scratch,
        compiler_params=pltpu.CompilerParams(vmem_limit_bytes=16 * 1024 * 1024),
        cost_estimate=pl.CostEstimate(flops=flops, bytes_accessed=read, transcendentals=0),
    )(*operands)


def exchange(first, rim, own, core, capacity, local, direct):
    axes = ("groups",) + CURVE
    groups, count = lax.axis_size("groups"), lax.axis_size(CURVE)
    cores = paired(groups, count, 1, lambda s: s % 2 == 0)
    chips = paired(groups, count, 1, lambda s: s % 2 == 1)
    far_chips = paired(groups, count, 3, lambda s: s % 2 == 1)
    got = lax.ppermute(first, axes, cores)
    with_codes = rim is None
    at = own.shape[0] - 4 * capacity if with_codes else 0

    def either(x, at_first, at_second):
        return jnp.where(core == 0, x[at_first : at_first + capacity], x[at_second : at_second + capacity])

    if with_codes:
        near = jnp.concatenate([own[: at + 2 * capacity], got[at + capacity : at + 3 * capacity]], axis=0)
        far = jnp.concatenate([own[at + 2 * capacity :], got[at + 3 * capacity :]], axis=0)
    else:
        rim = lax.ppermute(rim, axes, chips)
        theirs = got.shape[0] - 2 * capacity
        near = jnp.concatenate([own[:capacity], got[theirs + capacity :]], axis=0)
        far = jnp.concatenate([own[capacity:], got[theirs : theirs + capacity]], axis=0)
    near = lax.ppermute(near, axes, chips)
    far = lax.ppermute(far, axes, far_chips)
    *results, token = local(got)
    if with_codes:
        parts = [either(near, at + capacity, at + 2 * capacity), either(near, at + 3 * capacity, at)]
        parts += [either(far, capacity, 0), either(far, 0, capacity)]
    else:
        parts = [either(near, at, at + capacity), either(near, at + capacity, at)]
        parts += [either(far, 0, capacity), either(far, capacity, 0)]
    last = jnp.concatenate(parts + [token], axis=0)
    arrived = (got, near, far) if with_codes else (got, rim, near, far)
    totals = direct(results, *arrived, last)
    return lax.ppermute(last, axes, cores), totals, results


def body(
    state, velocity, levels, neighbours, records, counts, stiffness, trace_map, lift, projection
):
    elements, modes = state.shape
    width = trace_map.shape[1]
    slots = records.shape[1]
    capacity = slots // counts.shape[1]
    rim = elements // 8
    core = lax.axis_index("pair")

    def array(shape, dtype):
        return jax.ShapeDtypeStruct(shape, dtype)

    def like(x):
        return array(x.shape, x.dtype)

    message = array((3 * rim + 4 * capacity, 128), bf16)
    sent = [array((elements, width), bf16), message, message]
    second_sent = [
        array((elements, width), bf16),
        array((3 * rim + 2 * capacity, 128), bf16),
        array((3 * rim, 128), bf16),
        array((2 * capacity, 128), bf16),
    ]
    whole = array((elements, modes), f32)
    faces = array((elements, width), f32)
    blocks = pltpu.VMEM((slots, 128), bf16)
    column_shape = array((slots, 128), f32)
    mark = array((16, 128), bf16)

    levels = levels.reshape(1, elements)
    vmem = pltpu.VMEM
    wide = (elements, 128)
    near_state, trace_map, projection, traces, first, own, source_hot, column, element_column = call(
        start_kernel,
        [like(state), like(trace_map), like(projection)]
        + sent
        + [array((slots, elements), bf16), column_shape, array(wide, f32)],
        [vmem(x.shape, x.dtype) for x in (records, counts, velocity, levels, neighbours)]
        + [blocks, pltpu.SemaphoreType.DMA((9,))],
        2 * 10**8,
        (state, trace_map, records, counts, velocity, levels, neighbours, projection),
        (),
    )

    partial = call(own_kernel, [faces], [], 10**8, (), (element_column, traces))[0]

    def local(got):
        return call(
            local_kernel,
            [like(stiffness), like(lift), whole, faces, array((elements, 12 * rim), bf16), mark],
            [pltpu.SemaphoreType.DMA((2,))],
            10**8,
            (stiffness, lift),
            (element_column, near_state, got),
        )

    def direct(results, *arrived):
        return call(
            direct_kernel,
            [faces, array((5 * capacity, 128), f32), array((elements, 5 * capacity), bf16)],
            [vmem((5 * capacity, 128), bf16)],
            10**9,
            (),
            (results[4], partial, *arrived),
        )

    last, (partial, *direct_targets), (stiffness, lift, base, inflow, picks) = exchange(
        first, None, own, core, capacity, local, direct
    )
    field, traces, first, rims, own, face, element_hot = call(
        middle_kernel,
        [whole] + second_sent + [array((3 * capacity, 128), f32), array((elements, 3 * capacity), bf16)],
        [blocks],
        10**9,
        (),
        (lift, base, partial, inflow, last, trace_map, projection, source_hot, column),
    )

    def second_local(got):
        return call(
            second_local_kernel,
            [whole, faces, mark],
            [],
            10**8,
            (),
            (element_column, state, field, stiffness, traces, got),
        )

    def second_direct(results, *arrived):
        return call(
            second_direct_kernel,
            [faces],
            [vmem((5 * capacity, 128), f32)],
            10**9,
            (),
            (picks, results[1], *direct_targets, *arrived),
        )

    last, (partial,), (base, _) = exchange(
        first, rims, own, core, capacity, second_local, second_direct
    )
    return call(
        end_kernel,
        [whole],
        [vmem((elements, modes), f32), pltpu.SemaphoreType.DMA((4,))],
        10**9,
        (),
        (lift, base, partial, inflow, last, face, element_hot),
        out_space=pl.ANY,
    )[0]


def solution(mesh):
    placed = (
        P(("groups", "curve", "sub", "pair"), None),
        P(None, ("groups", "curve", "sub", "pair")),
        P(("groups", "curve", "sub", "pair")),
        P(None, ("groups", "curve", "sub", "pair")),
        P(None, ("groups", "curve", "sub", "pair")),
        P(("groups", "curve", "sub", "pair"), None),
        P(),
        P(),
        P(),
        P(),
    )
    return jax.shard_map(
        body,
        mesh=mesh,
        in_specs=placed,
        out_specs=P(("groups", "curve", "sub", "pair"), None),
        check_vma=False,
    )
```

```python
import jax
import jax.numpy as jnp
from jax import lax
from jax.experimental import pallas as pl
from jax.experimental.pallas import tpu as pltpu
from jax.sharding import PartitionSpec as P

time_step = 0.3
bf16 = jnp.bfloat16
f32 = jnp.float32
CURVE = ("curve", "sub", "pair")


def dot(a, b):
    return jnp.dot(a, b, preferred_element_type=f32)


def transposed(rows):
    pad = jnp.zeros((128 - rows.shape[0], rows.shape[1]), f32)
    return jnp.concatenate([rows, pad], axis=0).T


def lanes(shape):
    return lax.broadcasted_iota(jnp.int32, shape, 1)


def rows_of(shape):
    return lax.broadcasted_iota(jnp.int32, shape, 0)


def swapped(tile):
    turned = pltpu.roll(tile.astype(f32), 64, 1)
    low = lanes(turned.shape) < 64
    top = jnp.where(low, turned, 0.0).astype(bf16)
    bottom = jnp.where(low, 0.0, turned).astype(bf16)
    return jnp.concatenate([top, bottom], axis=0)


def hot(column, width):
    rows = column.shape[0]
    picked = column.astype(jnp.int32) == lanes((rows, width))
    return jnp.where(picked, 1.0, 0.0).astype(bf16)


def place():
    return lax.axis_index("curve") * lax.axis_size("sub") + lax.axis_index("sub"), lax.axis_index("pair")


def record_columns(records, counts):
    slots = records.shape[1]
    capacity = slots // 8
    source, face, kind, target = (records[i : i + 1, :] for i in range(4))
    slot = lanes((1, slots))
    allowed = jnp.zeros((1, slots), jnp.int32)
    for j in range(8):
        inside = (slot >= j * capacity) & (slot < (j + 1) * capacity)
        allowed = jnp.where(inside, counts[:, j : j + 1] + j * capacity, allowed)
    facing = jnp.where(slot < allowed, jnp.bitwise_xor(face, 1) + 1, 0)
    digits = [lax.shift_right_logical(target, 4), jnp.bitwise_and(target, 15), facing]
    gap = jnp.zeros((61, slots), f32)
    rows = [x.astype(f32) for x in (source, face, kind)] + [gap] + [x.astype(f32) for x in digits]
    return transposed(jnp.concatenate(rows, axis=0))


def send(traces, source_hot, column, projection, first_out, rim_out, own_out, blocks, with_codes):
    elements, width = traces.shape
    slots = column.shape[0]
    capacity = slots // 8
    rim = elements // 8
    core = lax.axis_index("pair")
    shape = (slots, 128)
    lane = lanes(shape)
    half = jnp.where(lane < 64, 0.0, 1.0)
    picked = dot(source_hot, traces[...])
    face = column[:, 1:2]
    row = jnp.zeros(shape, f32)
    for t in range(3):
        row = jnp.where(half + 2 * t == face, picked[:, 128 * t : 128 * t + 128], row)
    every = dot(row.astype(bf16), jnp.concatenate([projection[...]] * 2, axis=0))
    kind = column[:, 2:3]
    folded = jnp.zeros(shape, f32)
    for t in range(4):
        folded = jnp.where(half + 2 * t == kind, every[:, 128 * t : 128 * t + 128], folded)
    piece = folded + pltpu.roll(folded, 64, 1)
    if with_codes:
        piece = jnp.where(lane < 64, piece, column[...])
    blocks[...] = piece.astype(bf16)

    def block(at_first, at_second):
        index = at_first + core * (at_second - at_first)
        return blocks[pl.ds(pl.multiple_of(index * capacity, capacity), capacity), :]

    final_at = pl.multiple_of((1 - core) * (elements - rim), rim)
    other_at = pl.multiple_of(core * (elements - rim), rim)
    for t in range(3):
        cut = slice(128 * t, 128 * t + 128)
        rows = slice(rim * t, rim * t + rim)
        first_out[rows, :] = traces[pl.ds(final_at, rim), cut]
        rim_out[rows, :] = traces[pl.ds(other_at, rim), cut]
    at = 3 * rim
    there = [(4, 3), (5, 1), (6, 2), (7, 0)]
    here = [(2, 4), (3, 5), (0, 6), (1, 7)]
    if with_codes:
        for i in range(4):
            rows = slice(at + capacity * i, at + capacity * i + capacity)
            first_out[rows, :] = block(*there[i])
            own_out[rows, :] = block(*here[i])
        return
    low = lanes((capacity, 128)) < 64

    def pair(a, b):
        return jnp.where(low, block(*a), block(*b))

    first_out[at : at + capacity, :] = pair(there[0], there[3])
    first_out[at + capacity :, :] = pair(there[1], there[2])
    own_out[0:capacity, :] = pair(here[0], here[1])
    own_out[capacity:, :] = pair(here[2], here[3])


def start_kernel(
    state_in, trace_map_in, records_in, counts_in, velocity_in, levels_in, neighbours_in, projection_in,
    state, trace_map, projection, traces, first_out, own_out, source_hot, column, elements_column,
    records, counts, velocity, levels, neighbours, blocks, sems
):
    elements = state.shape[0]
    part = elements // 2
    pairs = [(records_in, records), (counts_in, counts), (velocity_in, velocity), (levels_in, levels)]
    pairs += [(neighbours_in, neighbours), (trace_map_in, trace_map)]
    for i in range(2):
        cut = pl.ds(i * part, part)
        pairs.append((state_in.at[cut], state.at[cut]))
    pairs.append((projection_in, projection))
    copies = [pltpu.make_async_copy(a, b, sems.at[i]) for i, (a, b) in enumerate(pairs)]
    for copy in copies:
        copy.start()
    for copy in copies[:5]:
        copy.wait()
    columns = record_columns(records, counts)
    column[...] = columns
    source_hot[...] = hot(columns[:, 0:1], elements)
    elements_column[...] = element_columns(velocity, levels, neighbours)
    copies[5].wait()
    for i in range(2):
        copies[6 + i].wait()
        cut = slice(i * part, i * part + part)
        traces[cut, :] = dot(state[cut, :].astype(bf16), trace_map[...]).astype(bf16)
    copies[8].wait()
    send(traces, source_hot[...], column, projection, first_out, own_out, own_out, blocks, True)


def element_columns(velocity, levels, neighbours):
    elements = velocity.shape[1]
    rim = elements // 8
    chip, core = place()
    raw = neighbours[...].astype(f32)
    local = raw - ((2 * chip + core) * elements).astype(f32)
    before = ((2 - core) * rim).astype(f32)
    after = (elements - core * rim).astype(f32)
    index = jnp.where(local < 0, local + before, jnp.where(local >= elements, local - after, -1.0))
    index = jnp.where(raw < 0, -1.0, index)
    scale = jnp.exp2(levels[...].astype(f32)) * 0.25
    gap = jnp.zeros((4, elements), f32)
    return transposed(jnp.concatenate([velocity[...], scale, gap, local, gap[0:2], index], axis=0))


def volume_term(column, lowered, stiffness, n, step):
    modes = stiffness.shape[0]
    volume = jnp.zeros((lowered.shape[0], step), f32)
    for d in range(3):
        volume += column[:, d : d + 1] * dot(lowered, stiffness[:, d * modes + n : d * modes + n + step])
    return column[:, 3:4] * volume


def own_part(column, traces, partial_out):
    elements = traces.shape[0]
    for t in range(3):
        tile = traces[:, 128 * t : 128 * t + 128]
        at = 8 + 2 * t
        picks = [hot(column[:, at + i : at + i + 1], elements) for i in range(2)]
        near = dot(jnp.concatenate(picks, axis=1), swapped(tile))
        partial_out[:, 128 * t : 128 * t + 128] = near - tile.astype(f32)


def columns_kernel(column, inflow, picks):
    elements = column.shape[0]
    rim = elements // 8
    columns = column[...]
    low = lanes((elements, 128)) < 64
    for t in range(3):
        speed = columns[:, t : t + 1]
        inflow[:, 128 * t : 128 * t + 128] = columns[:, 3:4] * jnp.maximum(jnp.where(low, speed, -speed), 0.0)
    for i in range(6):
        picks[:, 2 * rim * i : 2 * rim * i + 2 * rim] = hot(columns[:, 16 + i : 17 + i], 2 * rim)


def local_kernel(stiffness_in, lift_in, column, state, traces, got, stiffness, lift, base, partial, token, sems):
    token[...] = got[0:16, :]
    modes = state.shape[1]
    copies = [
        pltpu.make_async_copy(stiffness_in, stiffness, sems.at[0]),
        pltpu.make_async_copy(lift_in, lift, sems.at[1]),
    ]
    for copy in copies:
        copy.start()
    columns = column[...]
    own_part(columns, traces, partial)
    lowered = state[...].astype(bf16)
    step = 256
    copies[0].wait()
    for n in range(0, modes, step):
        base[:, n : n + step] = state[:, n : n + step] + time_step * volume_term(columns, lowered, stiffness, n, step)
    copies[1].wait()


def second_local_kernel(column, state, field, stiffness, traces, got, base, partial, token):
    token[...] = got[0:16, :]
    modes = state.shape[1]
    columns = column[...]
    lowered = field[...].astype(bf16)
    step = 256
    for n in range(0, modes, step):
        volume = volume_term(columns, lowered, stiffness, n, step)
        base[:, n : n + step] = 0.5 * (state[:, n : n + step] + field[:, n : n + step]) + 0.5 * time_step * volume
    own_part(columns, traces, partial)


def direct_pieces(got, near, far, arrived):
    capacity = arrived.shape[0] // 5
    at = 6 * capacity
    core = lax.axis_index("pair")

    def mine(ref, start):
        return ref[pl.ds(pl.multiple_of(start + core * capacity, capacity), capacity), :]

    blocks = [
        got[at : at + capacity, :],
        mine(near, at),
        mine(near, at + 2 * capacity),
        mine(far, 0),
        far[2 * capacity : 3 * capacity, :],
    ]
    for i, block in enumerate(blocks):
        arrived[capacity * i : capacity * i + capacity, :] = block
    return arrived[...]


def in_both(pieces, which):
    half = jnp.where(lanes(pieces.shape) < 64, 0, 1)
    kept = jnp.where(half == which, pieces.astype(f32), 0.0)
    return kept + pltpu.roll(kept, 64, 1)


def direct_pairs(got, near, far, arrived):
    capacity = arrived.shape[0] // 5
    at = 6 * capacity
    core = lax.axis_index("pair")
    blocks = [
        (got[at : at + capacity, :], 0),
        (near[0:capacity, :], core),
        (near[capacity : 2 * capacity, :], core),
        (far[0:capacity, :], core),
        (far[capacity : 2 * capacity, :], 1),
    ]
    for i, (block, which) in enumerate(blocks):
        arrived[capacity * i : capacity * i + capacity, :] = in_both(block, which)
    return arrived[...]


def targets(pieces, elements):
    face_of = jnp.where(rows_of((128, 128)) == 66, 1.0, 0.0).astype(bf16)
    face = dot(pieces, face_of) - 1.0
    lane = lanes((8, 128))
    element_of = jnp.where(lane == 64, 16.0, jnp.where(lane == 65, 1.0, 0.0)).astype(bf16)
    target = lax.dot_general(element_of, pieces, (((1,), (1,)), ((), ())), preferred_element_type=f32)[0:1, :]
    match = rows_of((elements, pieces.shape[0])) == target.astype(jnp.int32)
    return face, jnp.where(match, 1.0, 0.0).astype(bf16)


def mortar_sum(both, face, element_hot):
    half = jnp.where(lanes(both.shape) < 64, 0.0, 1.0)
    placed = [jnp.where(half + 2 * t == face, both, 0.0).astype(bf16) for t in range(3)]
    return dot(element_hot, jnp.concatenate(placed, axis=1))


def add_direct(picks, partial, got, near, both, face, element_hot, total):
    rim = picks.shape[1] // 12
    mortar = mortar_sum(both, face, element_hot)
    for t in range(3):
        cut = slice(128 * t, 128 * t + 128)
        rows = slice(rim * t, rim * t + rim)
        window = jnp.concatenate([got[rows, :], near[rows, :]], axis=0)
        conforming = dot(picks[:, 4 * rim * t : 4 * rim * t + 4 * rim], swapped(window))
        total[:, cut] = partial[:, cut] + conforming + mortar[:, cut]


def direct_kernel(picks, partial, got, near, far, last, total, face_out, element_hot_out, arrived):
    pieces = direct_pieces(got, near, far, arrived)
    face, element_hot = targets(pieces, partial.shape[0])
    face_out[...] = face
    element_hot_out[...] = element_hot
    add_direct(picks, partial, got, near, in_both(pieces, 0), face, element_hot, total)


def second_direct_kernel(picks, partial, face, element_hot, got, rim, near, far, last, total, arrived):
    both = direct_pairs(got, near, far, arrived)
    add_direct(picks, partial, got, rim, both, face[...], element_hot[...], total)


def fluxes(both, face, element_hot, partial, inflow):
    return (inflow[...] * (partial[...] + mortar_sum(both, face, element_hot))).astype(bf16)


def middle_kernel(
    lift, base, partial, inflow, last, trace_map, projection, source_hot, column,
    field, traces, first_out, rim_out, own_out, face_out, element_hot_out, blocks
):
    elements = base.shape[0]
    pieces = last[0 : face_out.shape[0], :]
    face, element_hot = targets(pieces, elements)
    face_out[...] = face
    element_hot_out[...] = element_hot
    flux = fluxes(in_both(pieces, 0), face, element_hot, partial, inflow)
    new = base[...] + time_step * dot(flux, lift[...])
    field[...] = new
    traces[...] = dot(new.astype(bf16), trace_map[...]).astype(bf16)
    send(traces, source_hot[...], column, projection, first_out, rim_out, own_out, blocks, False)


def end_kernel(lift, base, partial, inflow, last, face, element_hot, field, result, sems):
    elements = base.shape[0]
    capacity = face.shape[0] // 3
    core = lax.axis_index("pair")
    far = last[pl.ds(pl.multiple_of((3 - core) * capacity, capacity), capacity), :]
    both = in_both(jnp.concatenate([last[0 : 2 * capacity, :], far], axis=0), core)
    flux = fluxes(both, face[...], element_hot[...], partial, inflow)
    part = elements // 4
    copies = []
    for i in range(4):
        cut = slice(part * i, part * i + part)
        result[cut, :] = base[cut, :] + 0.5 * time_step * dot(flux[cut, :], lift[...])
        rows = pl.ds(part * i, part)
        copies.append(pltpu.make_async_copy(result.at[rows], field.at[rows], sems.at[i]))
        copies[i].start()
    for copy in copies:
        copy.wait()


def paired(groups, count, step, lower):
    partner = {}
    for s in range(count):
        if lower(s) and s + step < count:
            partner[s] = s + step
            partner[s + step] = s
    pairs = []
    for g in range(groups):
        for s in range(count):
            if s in partner:
                pairs.append((g * count + s, g * count + partner[s]))
            elif g ^ 1 < groups:
                pairs.append((g * count + s, (g ^ 1) * count + s))
    return pairs


def call(kernel, out_shape, scratch, flops, far, near, out_space=pltpu.VMEM):
    operands = [pltpu.with_memory_space_constraint(x, pltpu.HBM) for x in far] + list(near)
    read = sum(x.size * x.dtype.itemsize for x in operands) if flops > 10**8 else 10**5
    specs = [pl.BlockSpec(memory_space=pl.ANY)] * len(far) + [pl.BlockSpec(memory_space=pltpu.VMEM)] * len(near)
    return pl.pallas_call(
        kernel,
        out_shape=out_shape,
        in_specs=specs,
        out_specs=[pl.BlockSpec(memory_space=out_space)] * len(out_shape),
        scratch_shapes=scratch,
        compiler_params=pltpu.CompilerParams(vmem_limit_bytes=16 * 1024 * 1024),
        cost_estimate=pl.CostEstimate(flops=flops, bytes_accessed=read, transcendentals=0),
    )(*operands)


def exchange(first, rim, own, core, capacity, local, direct):
    axes = ("groups",) + CURVE
    groups, count = lax.axis_size("groups"), lax.axis_size(CURVE)
    cores = paired(groups, count, 1, lambda s: s % 2 == 0)
    chips = paired(groups, count, 1, lambda s: s % 2 == 1)
    far_chips = paired(groups, count, 3, lambda s: s % 2 == 1)
    got = lax.ppermute(first, axes, cores)
    with_codes = rim is None
    at = own.shape[0] - 4 * capacity if with_codes else 0

    def either(x, at_first, at_second):
        return jnp.where(core == 0, x[at_first : at_first + capacity], x[at_second : at_second + capacity])

    if with_codes:
        near = jnp.concatenate([own[: at + 2 * capacity], got[at + capacity : at + 3 * capacity]], axis=0)
        far = jnp.concatenate([own[at + 2 * capacity :], got[at + 3 * capacity :]], axis=0)
    else:
        rim = lax.ppermute(rim, axes, chips)
        theirs = got.shape[0] - 2 * capacity
        near = jnp.concatenate([own[:capacity], got[theirs + capacity :]], axis=0)
        far = jnp.concatenate([own[capacity:], got[theirs : theirs + capacity]], axis=0)
    near = lax.ppermute(near, axes, chips)
    far = lax.ppermute(far, axes, far_chips)
    *results, token = local(got)
    if with_codes:
        parts = [either(near, at + capacity, at + 2 * capacity), either(near, at + 3 * capacity, at)]
        parts += [either(far, capacity, 0), either(far, 0, capacity)]
    else:
        parts = [either(near, at, at + capacity), either(near, at + capacity, at)]
        parts += [either(far, 0, capacity), either(far, capacity, 0)]
    last = jnp.concatenate(parts + [token], axis=0)
    arrived = (got, near, far) if with_codes else (got, rim, near, far)
    totals = direct(results, *arrived, last)
    return lax.ppermute(last, axes, cores), totals, results


def body(
    state, velocity, levels, neighbours, records, counts, stiffness, trace_map, lift, projection
):
    elements, modes = state.shape
    width = trace_map.shape[1]
    slots = records.shape[1]
    capacity = slots // counts.shape[1]
    rim = elements // 8
    core = lax.axis_index("pair")

    def array(shape, dtype):
        return jax.ShapeDtypeStruct(shape, dtype)

    def like(x):
        return array(x.shape, x.dtype)

    message = array((3 * rim + 4 * capacity, 128), bf16)
    sent = [array((elements, width), bf16), message, message]
    second_sent = [
        array((elements, width), bf16),
        array((3 * rim + 2 * capacity, 128), bf16),
        array((3 * rim, 128), bf16),
        array((2 * capacity, 128), bf16),
    ]
    whole = array((elements, modes), f32)
    faces = array((elements, width), f32)
    blocks = pltpu.VMEM((slots, 128), bf16)
    column_shape = array((slots, 128), f32)
    mark = array((16, 128), bf16)

    levels = levels.reshape(1, elements)
    vmem = pltpu.VMEM
    wide = (elements, 128)
    near_state, trace_map, projection, traces, first, own, source_hot, column, element_column = call(
        start_kernel,
        [like(state), like(trace_map), like(projection)]
        + sent
        + [array((slots, elements), bf16), column_shape, array(wide, f32)],
        [vmem(x.shape, x.dtype) for x in (records, counts, velocity, levels, neighbours)]
        + [blocks, pltpu.SemaphoreType.DMA((9,))],
        2 * 10**8,
        (state, trace_map, records, counts, velocity, levels, neighbours, projection),
        (),
    )

    picks = array((elements, 12 * rim), bf16)
    inflow, picks = call(columns_kernel, [faces, picks], [], 10**8, (), (element_column,))

    def local(got):
        return call(
            local_kernel,
            [like(stiffness), like(lift), whole, faces, mark],
            [pltpu.SemaphoreType.DMA((2,))],
            10**8,
            (stiffness, lift),
            (element_column, near_state, traces, got),
        )

    def direct(results, *arrived):
        return call(
            direct_kernel,
            [faces, array((5 * capacity, 128), f32), array((elements, 5 * capacity), bf16)],
            [vmem((5 * capacity, 128), bf16)],
            10**9,
            (),
            (picks, results[3], *arrived),
        )

    last, (partial, *direct_targets), (stiffness, lift, base, _) = exchange(
        first, None, own, core, capacity, local, direct
    )
    field, traces, first, rims, own, face, element_hot = call(
        middle_kernel,
        [whole] + second_sent + [array((3 * capacity, 128), f32), array((elements, 3 * capacity), bf16)],
        [blocks],
        10**9,
        (),
        (lift, base, partial, inflow, last, trace_map, projection, source_hot, column),
    )

    def second_local(got):
        return call(
            second_local_kernel,
            [whole, faces, mark],
            [],
            10**8,
            (),
            (element_column, state, field, stiffness, traces, got),
        )

    def second_direct(results, *arrived):
        return call(
            second_direct_kernel,
            [faces],
            [vmem((5 * capacity, 128), f32)],
            10**9,
            (),
            (picks, results[1], *direct_targets, *arrived),
        )

    last, (partial,), (base, _) = exchange(
        first, rims, own, core, capacity, second_local, second_direct
    )
    return call(
        end_kernel,
        [whole],
        [vmem((elements, modes), f32), pltpu.SemaphoreType.DMA((4,))],
        10**9,
        (),
        (lift, base, partial, inflow, last, face, element_hot),
        out_space=pl.ANY,
    )[0]


def solution(mesh):
    placed = (
        P(("groups", "curve", "sub", "pair"), None),
        P(None, ("groups", "curve", "sub", "pair")),
        P(("groups", "curve", "sub", "pair")),
        P(None, ("groups", "curve", "sub", "pair")),
        P(None, ("groups", "curve", "sub", "pair")),
        P(("groups", "curve", "sub", "pair"), None),
        P(),
        P(),
        P(),
        P(),
    )
    return jax.shard_map(
        body,
        mesh=mesh,
        in_specs=placed,
        out_specs=P(("groups", "curve", "sub", "pair"), None),
        check_vma=False,
    )
```

```python
import jax
import jax.numpy as jnp
from jax import lax
from jax.experimental import pallas as pl
from jax.experimental.pallas import tpu as pltpu
from jax.sharding import PartitionSpec as P

time_step = 0.3
bf16 = jnp.bfloat16
f32 = jnp.float32
CURVE = ("curve", "sub", "pair")


def dot(a, b):
    return jnp.dot(a, b, preferred_element_type=f32)


def transposed(rows):
    pad = jnp.zeros((128 - rows.shape[0], rows.shape[1]), f32)
    return jnp.concatenate([rows, pad], axis=0).T


def lanes(shape):
    return lax.broadcasted_iota(jnp.int32, shape, 1)


def rows_of(shape):
    return lax.broadcasted_iota(jnp.int32, shape, 0)


def swapped(tile):
    turned = pltpu.roll(tile.astype(f32), 64, 1)
    low = lanes(turned.shape) < 64
    top = jnp.where(low, turned, 0.0).astype(bf16)
    bottom = jnp.where(low, 0.0, turned).astype(bf16)
    return jnp.concatenate([top, bottom], axis=0)


def hot(column, width):
    rows = column.shape[0]
    picked = column.astype(jnp.int32) == lanes((rows, width))
    return jnp.where(picked, 1.0, 0.0).astype(bf16)


def place():
    return lax.axis_index("curve") * lax.axis_size("sub") + lax.axis_index("sub"), lax.axis_index("pair")


def record_columns(records, counts):
    slots = records.shape[1]
    capacity = slots // 8
    source, face, kind, target = (records[i : i + 1, :] for i in range(4))
    slot = lanes((1, slots))
    allowed = jnp.zeros((1, slots), jnp.int32)
    for j in range(8):
        inside = (slot >= j * capacity) & (slot < (j + 1) * capacity)
        allowed = jnp.where(inside, counts[:, j : j + 1] + j * capacity, allowed)
    facing = jnp.where(slot < allowed, jnp.bitwise_xor(face, 1) + 1, 0)
    digits = [lax.shift_right_logical(target, 4), jnp.bitwise_and(target, 15), facing]
    gap = jnp.zeros((61, slots), f32)
    rows = [x.astype(f32) for x in (source, face, kind)] + [gap] + [x.astype(f32) for x in digits]
    return transposed(jnp.concatenate(rows, axis=0))


def send(traces, source_hot, column, projection, first_out, rim_out, own_out, blocks, with_codes):
    elements, width = traces.shape
    slots = column.shape[0]
    capacity = slots // 8
    rim = elements // 8
    core = lax.axis_index("pair")
    shape = (slots, 128)
    lane = lanes(shape)
    half = jnp.where(lane < 64, 0.0, 1.0)
    picked = dot(source_hot, traces[...])
    face = column[:, 1:2]
    row = jnp.zeros(shape, f32)
    for t in range(3):
        row = jnp.where(half + 2 * t == face, picked[:, 128 * t : 128 * t + 128], row)
    every = dot(row.astype(bf16), jnp.concatenate([projection[...]] * 2, axis=0))
    kind = column[:, 2:3]
    folded = jnp.zeros(shape, f32)
    for t in range(4):
        folded = jnp.where(half + 2 * t == kind, every[:, 128 * t : 128 * t + 128], folded)
    piece = folded + pltpu.roll(folded, 64, 1)
    if with_codes:
        piece = jnp.where(lane < 64, piece, column[...])
    blocks[...] = piece.astype(bf16)

    def block(at_first, at_second):
        index = at_first + core * (at_second - at_first)
        return blocks[pl.ds(pl.multiple_of(index * capacity, capacity), capacity), :]

    final_at = pl.multiple_of((1 - core) * (elements - rim), rim)
    other_at = pl.multiple_of(core * (elements - rim), rim)
    for t in range(3):
        cut = slice(128 * t, 128 * t + 128)
        rows = slice(rim * t, rim * t + rim)
        first_out[rows, :] = traces[pl.ds(final_at, rim), cut]
        rim_out[rows, :] = traces[pl.ds(other_at, rim), cut]
    at = 3 * rim
    there = [(4, 3), (5, 1), (6, 2), (7, 0)]
    here = [(2, 4), (3, 5), (0, 6), (1, 7)]
    if with_codes:
        for i in range(4):
            rows = slice(at + capacity * i, at + capacity * i + capacity)
            first_out[rows, :] = block(*there[i])
            own_out[rows, :] = block(*here[i])
        return
    low = lanes((capacity, 128)) < 64

    def pair(a, b):
        return jnp.where(low, block(*a), block(*b))

    first_out[at : at + capacity, :] = pair(there[0], there[3])
    first_out[at + capacity :, :] = pair(there[1], there[2])
    own_out[0:capacity, :] = pair(here[0], here[1])
    own_out[capacity:, :] = pair(here[2], here[3])


def start_kernel(
    state_in, trace_map_in, records_in, counts_in, velocity_in, levels_in, neighbours_in, projection_in,
    state, trace_map, projection, traces, first_out, own_out, source_hot, column, elements_column,
    records, counts, velocity, levels, neighbours, blocks, sems
):
    elements = state.shape[0]
    part = elements // 2
    pairs = [(records_in, records), (counts_in, counts), (velocity_in, velocity), (levels_in, levels)]
    pairs += [(neighbours_in, neighbours), (trace_map_in, trace_map)]
    for i in range(2):
        cut = pl.ds(i * part, part)
        pairs.append((state_in.at[cut], state.at[cut]))
    pairs.append((projection_in, projection))
    copies = [pltpu.make_async_copy(a, b, sems.at[i]) for i, (a, b) in enumerate(pairs)]
    for copy in copies:
        copy.start()
    for copy in copies[:5]:
        copy.wait()
    columns = record_columns(records, counts)
    column[...] = columns
    source_hot[...] = hot(columns[:, 0:1], elements)
    elements_column[...] = element_columns(velocity, levels, neighbours)
    copies[5].wait()
    for i in range(2):
        copies[6 + i].wait()
        cut = slice(i * part, i * part + part)
        traces[cut, :] = dot(state[cut, :].astype(bf16), trace_map[...]).astype(bf16)
    copies[8].wait()
    send(traces, source_hot[...], column, projection, first_out, own_out, own_out, blocks, True)


def element_columns(velocity, levels, neighbours):
    elements = velocity.shape[1]
    rim = elements // 8
    chip, core = place()
    raw = neighbours[...].astype(f32)
    local = raw - ((2 * chip + core) * elements).astype(f32)
    before = ((2 - core) * rim).astype(f32)
    after = (elements - core * rim).astype(f32)
    index = jnp.where(local < 0, local + before, jnp.where(local >= elements, local - after, -1.0))
    index = jnp.where(raw < 0, -1.0, index)
    scale = jnp.exp2(levels[...].astype(f32)) * 0.25
    gap = jnp.zeros((4, elements), f32)
    return transposed(jnp.concatenate([velocity[...], scale, gap, local, gap[0:2], index], axis=0))


def volume_term(column, lowered, stiffness, n, step):
    modes = stiffness.shape[0]
    volume = jnp.zeros((lowered.shape[0], step), f32)
    for d in range(3):
        volume += column[:, d : d + 1] * dot(lowered, stiffness[:, d * modes + n : d * modes + n + step])
    return column[:, 3:4] * volume


def own_part(column, traces, partial_out):
    elements = traces.shape[0]
    for t in range(3):
        tile = traces[:, 128 * t : 128 * t + 128]
        at = 8 + 2 * t
        picks = [hot(column[:, at + i : at + i + 1], elements) for i in range(2)]
        near = dot(jnp.concatenate(picks, axis=1), swapped(tile))
        partial_out[:, 128 * t : 128 * t + 128] = near - tile.astype(f32)


def own_kernel(column, traces, partial):
    own_part(column[...], traces, partial)


def local_kernel(stiffness_in, lift_in, column, state, got, stiffness, lift, base, inflow, picks, token, sems):
    token[...] = got[0:16, :]
    elements, modes = state.shape
    rim = elements // 8
    copies = [
        pltpu.make_async_copy(stiffness_in, stiffness, sems.at[0]),
        pltpu.make_async_copy(lift_in, lift, sems.at[1]),
    ]
    copies[0].start()
    columns = column[...]
    low = lanes((elements, 128)) < 64
    for t in range(3):
        speed = columns[:, t : t + 1]
        inflow[:, 128 * t : 128 * t + 128] = columns[:, 3:4] * jnp.maximum(jnp.where(low, speed, -speed), 0.0)
    for i in range(6):
        picks[:, 2 * rim * i : 2 * rim * i + 2 * rim] = hot(columns[:, 16 + i : 17 + i], 2 * rim)
    lowered = state[...].astype(bf16)
    step = 256
    copies[0].wait()
    copies[1].start()
    for n in range(0, modes, step):
        base[:, n : n + step] = state[:, n : n + step] + time_step * volume_term(columns, lowered, stiffness, n, step)
    copies[1].wait()


def second_local_kernel(column, state, field, stiffness, traces, got, base, partial, token):
    token[...] = got[0:16, :]
    modes = state.shape[1]
    columns = column[...]
    lowered = field[...].astype(bf16)
    step = 256
    for n in range(0, modes, step):
        volume = volume_term(columns, lowered, stiffness, n, step)
        base[:, n : n + step] = 0.5 * (state[:, n : n + step] + field[:, n : n + step]) + 0.5 * time_step * volume
    own_part(columns, traces, partial)


def direct_pieces(got, near, far, arrived):
    capacity = arrived.shape[0] // 5
    at = 6 * capacity
    core = lax.axis_index("pair")

    def mine(ref, start):
        return ref[pl.ds(pl.multiple_of(start + core * capacity, capacity), capacity), :]

    blocks = [
        got[at : at + capacity, :],
        mine(near, at),
        mine(near, at + 2 * capacity),
        mine(far, 0),
        far[2 * capacity : 3 * capacity, :],
    ]
    for i, block in enumerate(blocks):
        arrived[capacity * i : capacity * i + capacity, :] = block
    return arrived[...]


def in_both(pieces, which):
    half = jnp.where(lanes(pieces.shape) < 64, 0, 1)
    kept = jnp.where(half == which, pieces.astype(f32), 0.0)
    return kept + pltpu.roll(kept, 64, 1)


def direct_pairs(got, near, far, arrived):
    capacity = arrived.shape[0] // 5
    at = 6 * capacity
    core = lax.axis_index("pair")
    blocks = [
        (got[at : at + capacity, :], 0),
        (near[0:capacity, :], core),
        (near[capacity : 2 * capacity, :], core),
        (far[0:capacity, :], core),
        (far[capacity : 2 * capacity, :], 1),
    ]
    for i, (block, which) in enumerate(blocks):
        arrived[capacity * i : capacity * i + capacity, :] = in_both(block, which)
    return arrived[...]


def targets(pieces, elements):
    face_of = jnp.where(rows_of((128, 128)) == 66, 1.0, 0.0).astype(bf16)
    face = dot(pieces, face_of) - 1.0
    lane = lanes((8, 128))
    element_of = jnp.where(lane == 64, 16.0, jnp.where(lane == 65, 1.0, 0.0)).astype(bf16)
    target = lax.dot_general(element_of, pieces, (((1,), (1,)), ((), ())), preferred_element_type=f32)[0:1, :]
    match = rows_of((elements, pieces.shape[0])) == target.astype(jnp.int32)
    return face, jnp.where(match, 1.0, 0.0).astype(bf16)


def mortar_sum(both, face, element_hot):
    half = jnp.where(lanes(both.shape) < 64, 0.0, 1.0)
    placed = [jnp.where(half + 2 * t == face, both, 0.0).astype(bf16) for t in range(3)]
    return dot(element_hot, jnp.concatenate(placed, axis=1))


def add_direct(picks, partial, got, near, both, face, element_hot, total):
    rim = picks.shape[1] // 12
    mortar = mortar_sum(both, face, element_hot)
    for t in range(3):
        cut = slice(128 * t, 128 * t + 128)
        rows = slice(rim * t, rim * t + rim)
        window = jnp.concatenate([got[rows, :], near[rows, :]], axis=0)
        conforming = dot(picks[:, 4 * rim * t : 4 * rim * t + 4 * rim], swapped(window))
        total[:, cut] = partial[:, cut] + conforming + mortar[:, cut]


def direct_kernel(picks, partial, got, near, far, last, total, face_out, element_hot_out, arrived):
    pieces = direct_pieces(got, near, far, arrived)
    face, element_hot = targets(pieces, partial.shape[0])
    face_out[...] = face
    element_hot_out[...] = element_hot
    add_direct(picks, partial, got, near, in_both(pieces, 0), face, element_hot, total)


def second_direct_kernel(picks, partial, face, element_hot, got, rim, near, far, last, total, arrived):
    both = direct_pairs(got, near, far, arrived)
    add_direct(picks, partial, got, rim, both, face[...], element_hot[...], total)


def fluxes(both, face, element_hot, partial, inflow):
    return (inflow[...] * (partial[...] + mortar_sum(both, face, element_hot))).astype(bf16)


def middle_kernel(
    lift, base, partial, inflow, last, trace_map, projection, source_hot, column,
    field, traces, first_out, rim_out, own_out, face_out, element_hot_out, blocks
):
    elements = base.shape[0]
    pieces = last[0 : face_out.shape[0], :]
    face, element_hot = targets(pieces, elements)
    face_out[...] = face
    element_hot_out[...] = element_hot
    flux = fluxes(in_both(pieces, 0), face, element_hot, partial, inflow)
    new = base[...] + time_step * dot(flux, lift[...])
    field[...] = new
    traces[...] = dot(new.astype(bf16), trace_map[...]).astype(bf16)
    send(traces, source_hot[...], column, projection, first_out, rim_out, own_out, blocks, False)


def end_kernel(lift, base, partial, inflow, last, face, element_hot, field, result, sems):
    elements = base.shape[0]
    capacity = face.shape[0] // 3
    core = lax.axis_index("pair")
    far = last[pl.ds(pl.multiple_of((3 - core) * capacity, capacity), capacity), :]
    both = in_both(jnp.concatenate([last[0 : 2 * capacity, :], far], axis=0), core)
    flux = fluxes(both, face[...], element_hot[...], partial, inflow)
    part = elements // 4
    copies = []
    for i in range(4):
        cut = slice(part * i, part * i + part)
        result[cut, :] = base[cut, :] + 0.5 * time_step * dot(flux[cut, :], lift[...])
        rows = pl.ds(part * i, part)
        copies.append(pltpu.make_async_copy(result.at[rows], field.at[rows], sems.at[i]))
        copies[i].start()
    for copy in copies:
        copy.wait()


def paired(groups, count, step, lower):
    partner = {}
    for s in range(count):
        if lower(s) and s + step < count:
            partner[s] = s + step
            partner[s + step] = s
    pairs = []
    for g in range(groups):
        for s in range(count):
            if s in partner:
                pairs.append((g * count + s, g * count + partner[s]))
            elif g ^ 1 < groups:
                pairs.append((g * count + s, (g ^ 1) * count + s))
    return pairs


def call(kernel, out_shape, scratch, flops, far, near, out_space=pltpu.VMEM):
    operands = [pltpu.with_memory_space_constraint(x, pltpu.HBM) for x in far] + list(near)
    read = sum(x.size * x.dtype.itemsize for x in operands) if flops > 10**8 else 10**5
    specs = [pl.BlockSpec(memory_space=pl.ANY)] * len(far) + [pl.BlockSpec(memory_space=pltpu.VMEM)] * len(near)
    return pl.pallas_call(
        kernel,
        out_shape=out_shape,
        in_specs=specs,
        out_specs=[pl.BlockSpec(memory_space=out_space)] * len(out_shape),
        scratch_shapes=scratch,
        compiler_params=pltpu.CompilerParams(vmem_limit_bytes=16 * 1024 * 1024),
        cost_estimate=pl.CostEstimate(flops=flops, bytes_accessed=read, transcendentals=0),
    )(*operands)


def exchange(first, rim, own, core, capacity, local, direct):
    axes = ("groups",) + CURVE
    groups, count = lax.axis_size("groups"), lax.axis_size(CURVE)
    cores = paired(groups, count, 1, lambda s: s % 2 == 0)
    chips = paired(groups, count, 1, lambda s: s % 2 == 1)
    far_chips = paired(groups, count, 3, lambda s: s % 2 == 1)
    got = lax.ppermute(first, axes, cores)
    with_codes = rim is None
    at = own.shape[0] - 4 * capacity if with_codes else 0

    def either(x, at_first, at_second):
        return jnp.where(core == 0, x[at_first : at_first + capacity], x[at_second : at_second + capacity])

    if with_codes:
        near = jnp.concatenate([own[: at + 2 * capacity], got[at + capacity : at + 3 * capacity]], axis=0)
        far = jnp.concatenate([own[at + 2 * capacity :], got[at + 3 * capacity :]], axis=0)
    else:
        rim = lax.ppermute(rim, axes, chips)
        theirs = got.shape[0] - 2 * capacity
        near = jnp.concatenate([own[:capacity], got[theirs + capacity :]], axis=0)
        far = jnp.concatenate([own[capacity:], got[theirs : theirs + capacity]], axis=0)
    near = lax.ppermute(near, axes, chips)
    far = lax.ppermute(far, axes, far_chips)
    *results, token = local(got)
    if with_codes:
        parts = [either(near, at + capacity, at + 2 * capacity), either(near, at + 3 * capacity, at)]
        parts += [either(far, capacity, 0), either(far, 0, capacity)]
    else:
        parts = [either(near, at, at + capacity), either(near, at + capacity, at)]
        parts += [either(far, 0, capacity), either(far, capacity, 0)]
    last = jnp.concatenate(parts + [token], axis=0)
    arrived = (got, near, far) if with_codes else (got, rim, near, far)
    totals = direct(results, *arrived, last)
    return lax.ppermute(last, axes, cores), totals, results


def body(
    state, velocity, levels, neighbours, records, counts, stiffness, trace_map, lift, projection
):
    elements, modes = state.shape
    width = trace_map.shape[1]
    slots = records.shape[1]
    capacity = slots // counts.shape[1]
    rim = elements // 8
    core = lax.axis_index("pair")

    def array(shape, dtype):
        return jax.ShapeDtypeStruct(shape, dtype)

    def like(x):
        return array(x.shape, x.dtype)

    message = array((3 * rim + 4 * capacity, 128), bf16)
    sent = [array((elements, width), bf16), message, message]
    second_sent = [
        array((elements, width), bf16),
        array((3 * rim + 2 * capacity, 128), bf16),
        array((3 * rim, 128), bf16),
        array((2 * capacity, 128), bf16),
    ]
    whole = array((elements, modes), f32)
    faces = array((elements, width), f32)
    blocks = pltpu.VMEM((slots, 128), bf16)
    column_shape = array((slots, 128), f32)
    mark = array((16, 128), bf16)

    levels = levels.reshape(1, elements)
    vmem = pltpu.VMEM
    wide = (elements, 128)
    near_state, trace_map, projection, traces, first, own, source_hot, column, element_column = call(
        start_kernel,
        [like(state), like(trace_map), like(projection)]
        + sent
        + [array((slots, elements), bf16), column_shape, array(wide, f32)],
        [vmem(x.shape, x.dtype) for x in (records, counts, velocity, levels, neighbours)]
        + [blocks, pltpu.SemaphoreType.DMA((9,))],
        2 * 10**8,
        (state, trace_map, records, counts, velocity, levels, neighbours, projection),
        (),
    )

    partial = call(own_kernel, [faces], [], 10**8, (), (element_column, traces))[0]

    def local(got):
        return call(
            local_kernel,
            [like(stiffness), like(lift), whole, faces, array((elements, 12 * rim), bf16), mark],
            [pltpu.SemaphoreType.DMA((2,))],
            10**8,
            (stiffness, lift),
            (element_column, near_state, got),
        )

    def direct(results, *arrived):
        return call(
            direct_kernel,
            [faces, array((5 * capacity, 128), f32), array((elements, 5 * capacity), bf16)],
            [vmem((5 * capacity, 128), bf16)],
            10**9,
            (),
            (results[4], partial, *arrived),
        )

    last, (partial, *direct_targets), (stiffness, lift, base, inflow, picks) = exchange(
        first, None, own, core, capacity, local, direct
    )
    field, traces, first, rims, own, face, element_hot = call(
        middle_kernel,
        [whole] + second_sent + [array((3 * capacity, 128), f32), array((elements, 3 * capacity), bf16)],
        [blocks],
        10**9,
        (),
        (lift, base, partial, inflow, last, trace_map, projection, source_hot, column),
    )

    def second_local(got):
        return call(
            second_local_kernel,
            [whole, faces, mark],
            [],
            10**8,
            (),
            (element_column, state, field, stiffness, traces, got),
        )

    def second_direct(results, *arrived):
        return call(
            second_direct_kernel,
            [faces],
            [vmem((5 * capacity, 128), f32)],
            10**9,
            (),
            (picks, results[1], *direct_targets, *arrived),
        )

    last, (partial,), (base, _) = exchange(
        first, rims, own, core, capacity, second_local, second_direct
    )
    return call(
        end_kernel,
        [whole],
        [vmem((elements, modes), f32), pltpu.SemaphoreType.DMA((4,))],
        10**9,
        (),
        (lift, base, partial, inflow, last, face, element_hot),
        out_space=pl.ANY,
    )[0]


def solution(mesh):
    placed = (
        P(("groups", "curve", "sub", "pair"), None),
        P(None, ("groups", "curve", "sub", "pair")),
        P(("groups", "curve", "sub", "pair")),
        P(None, ("groups", "curve", "sub", "pair")),
        P(None, ("groups", "curve", "sub", "pair")),
        P(("groups", "curve", "sub", "pair"), None),
        P(),
        P(),
        P(),
        P(),
    )
    return jax.shard_map(
        body,
        mesh=mesh,
        in_specs=placed,
        out_specs=P(("groups", "curve", "sub", "pair"), None),
        check_vma=False,
    )
```

```python
import jax
import jax.numpy as jnp
from jax import lax
from jax.experimental import pallas as pl
from jax.experimental.pallas import tpu as pltpu
from jax.sharding import PartitionSpec as P

time_step = 0.3
bf16 = jnp.bfloat16
f32 = jnp.float32
CURVE = ("curve", "sub", "pair")


def dot(a, b):
    return jnp.dot(a, b, preferred_element_type=f32)


def transposed(rows):
    pad = jnp.zeros((128 - rows.shape[0], rows.shape[1]), f32)
    return jnp.concatenate([rows, pad], axis=0).T


def lanes(shape):
    return lax.broadcasted_iota(jnp.int32, shape, 1)


def rows_of(shape):
    return lax.broadcasted_iota(jnp.int32, shape, 0)


def swapped(tile):
    turned = pltpu.roll(tile.astype(f32), 64, 1)
    low = lanes(turned.shape) < 64
    top = jnp.where(low, turned, 0.0).astype(bf16)
    bottom = jnp.where(low, 0.0, turned).astype(bf16)
    return jnp.concatenate([top, bottom], axis=0)


def hot(column, width):
    rows = column.shape[0]
    picked = column.astype(jnp.int32) == lanes((rows, width))
    return jnp.where(picked, 1.0, 0.0).astype(bf16)


def place():
    return lax.axis_index("curve") * lax.axis_size("sub") + lax.axis_index("sub"), lax.axis_index("pair")


def record_columns(records, counts):
    slots = records.shape[1]
    capacity = slots // 8
    source, face, kind, target = (records[i : i + 1, :] for i in range(4))
    slot = lanes((1, slots))
    allowed = jnp.zeros((1, slots), jnp.int32)
    for j in range(8):
        inside = (slot >= j * capacity) & (slot < (j + 1) * capacity)
        allowed = jnp.where(inside, counts[:, j : j + 1] + j * capacity, allowed)
    facing = jnp.where(slot < allowed, jnp.bitwise_xor(face, 1) + 1, 0)
    digits = [lax.shift_right_logical(target, 4), jnp.bitwise_and(target, 15), facing]
    gap = jnp.zeros((61, slots), f32)
    rows = [x.astype(f32) for x in (source, face, kind)] + [gap] + [x.astype(f32) for x in digits]
    return transposed(jnp.concatenate(rows, axis=0))


def send(traces, source_hot, column, projection, first_out, rim_out, own_out, blocks, with_codes):
    elements, width = traces.shape
    slots = column.shape[0]
    capacity = slots // 8
    rim = elements // 8
    core = lax.axis_index("pair")
    shape = (slots, 128)
    lane = lanes(shape)
    half = jnp.where(lane < 64, 0.0, 1.0)
    picked = dot(source_hot, traces[...])
    face = column[:, 1:2]
    row = jnp.zeros(shape, f32)
    for t in range(3):
        row = jnp.where(half + 2 * t == face, picked[:, 128 * t : 128 * t + 128], row)
    every = dot(row.astype(bf16), jnp.concatenate([projection[...]] * 2, axis=0))
    kind = column[:, 2:3]
    folded = jnp.zeros(shape, f32)
    for t in range(4):
        folded = jnp.where(half + 2 * t == kind, every[:, 128 * t : 128 * t + 128], folded)
    piece = folded + pltpu.roll(folded, 64, 1)
    if with_codes:
        piece = jnp.where(lane < 64, piece, column[...])
    blocks[...] = piece.astype(bf16)

    def block(at_first, at_second):
        index = at_first + core * (at_second - at_first)
        return blocks[pl.ds(pl.multiple_of(index * capacity, capacity), capacity), :]

    final_at = pl.multiple_of((1 - core) * (elements - rim), rim)
    other_at = pl.multiple_of(core * (elements - rim), rim)
    for t in range(3):
        cut = slice(128 * t, 128 * t + 128)
        rows = slice(rim * t, rim * t + rim)
        first_out[rows, :] = traces[pl.ds(final_at, rim), cut]
        rim_out[rows, :] = traces[pl.ds(other_at, rim), cut]
    at = 3 * rim
    there = [(4, 3), (5, 1), (6, 2), (7, 0)]
    here = [(2, 4), (3, 5), (0, 6), (1, 7)]
    if with_codes:
        for i in range(4):
            rows = slice(at + capacity * i, at + capacity * i + capacity)
            first_out[rows, :] = block(*there[i])
            own_out[rows, :] = block(*here[i])
        return
    low = lanes((capacity, 128)) < 64

    def pair(a, b):
        return jnp.where(low, block(*a), block(*b))

    first_out[at : at + capacity, :] = pair(there[0], there[3])
    first_out[at + capacity :, :] = pair(there[1], there[2])
    own_out[0:capacity, :] = pair(here[0], here[1])
    own_out[capacity:, :] = pair(here[2], here[3])


def start_kernel(
    state_in, trace_map_in, records_in, counts_in, velocity_in, levels_in, neighbours_in, projection_in,
    state, trace_map, projection, traces, first_out, own_out, source_hot, column, elements_column,
    records, counts, velocity, levels, neighbours, blocks, sems
):
    elements = state.shape[0]
    part = elements // 2
    pairs = [(records_in, records), (counts_in, counts), (velocity_in, velocity), (levels_in, levels)]
    pairs += [(neighbours_in, neighbours), (trace_map_in, trace_map)]
    for i in range(2):
        cut = pl.ds(i * part, part)
        pairs.append((state_in.at[cut], state.at[cut]))
    pairs.append((projection_in, projection))
    copies = [pltpu.make_async_copy(a, b, sems.at[i]) for i, (a, b) in enumerate(pairs)]
    for copy in copies:
        copy.start()
    for copy in copies[:5]:
        copy.wait()
    columns = record_columns(records, counts)
    column[...] = columns
    source_hot[...] = hot(columns[:, 0:1], elements)
    elements_column[...] = element_columns(velocity, levels, neighbours)
    copies[5].wait()
    for i in range(2):
        copies[6 + i].wait()
        cut = slice(i * part, i * part + part)
        traces[cut, :] = dot(state[cut, :].astype(bf16), trace_map[...]).astype(bf16)
    copies[8].wait()
    send(traces, source_hot[...], column, projection, first_out, own_out, own_out, blocks, True)


def element_columns(velocity, levels, neighbours):
    elements = velocity.shape[1]
    rim = elements // 8
    chip, core = place()
    raw = neighbours[...].astype(f32)
    local = raw - ((2 * chip + core) * elements).astype(f32)
    before = ((2 - core) * rim).astype(f32)
    after = (elements - core * rim).astype(f32)
    index = jnp.where(local < 0, local + before, jnp.where(local >= elements, local - after, -1.0))
    index = jnp.where(raw < 0, -1.0, index)
    scale = jnp.exp2(levels[...].astype(f32)) * 0.25
    gap = jnp.zeros((4, elements), f32)
    return transposed(jnp.concatenate([velocity[...], scale, gap, local, gap[0:2], index], axis=0))


def volume_term(column, lowered, stiffness, n, step):
    modes = stiffness.shape[0]
    volume = jnp.zeros((lowered.shape[0], step), f32)
    for d in range(3):
        volume += column[:, d : d + 1] * dot(lowered, stiffness[:, d * modes + n : d * modes + n + step])
    return column[:, 3:4] * volume


def own_part(column, traces, partial_out):
    elements = traces.shape[0]
    for t in range(3):
        tile = traces[:, 128 * t : 128 * t + 128]
        at = 8 + 2 * t
        picks = [hot(column[:, at + i : at + i + 1], elements) for i in range(2)]
        near = dot(jnp.concatenate(picks, axis=1), swapped(tile))
        partial_out[:, 128 * t : 128 * t + 128] = near - tile.astype(f32)


def own_kernel(column, traces, partial):
    own_part(column[...], traces, partial)


def local_kernel(stiffness_in, lift_in, column, state, got, stiffness, lift, base, inflow, picks, token, sems):
    token[...] = got[0:16, :]
    elements, modes = state.shape
    rim = elements // 8
    copies = [
        pltpu.make_async_copy(stiffness_in, stiffness, sems.at[0]),
        pltpu.make_async_copy(lift_in, lift, sems.at[1]),
    ]
    copies[0].start()
    columns = column[...]
    low = lanes((elements, 128)) < 64
    for t in range(3):
        speed = columns[:, t : t + 1]
        inflow[:, 128 * t : 128 * t + 128] = columns[:, 3:4] * jnp.maximum(jnp.where(low, speed, -speed), 0.0)
    for i in range(6):
        picks[:, 2 * rim * i : 2 * rim * i + 2 * rim] = hot(columns[:, 16 + i : 17 + i], 2 * rim)
    lowered = state[...].astype(bf16)
    step = 256
    copies[0].wait()
    copies[1].start()
    for n in range(0, modes, step):
        base[:, n : n + step] = state[:, n : n + step] + time_step * volume_term(columns, lowered, stiffness, n, step)
    copies[1].wait()


def second_local_kernel(column, state, field, stiffness, traces, got, base, partial, token):
    token[...] = got[0:16, :]
    modes = state.shape[1]
    columns = column[...]
    lowered = field[...].astype(bf16)
    step = 256
    for n in range(0, modes, step):
        volume = volume_term(columns, lowered, stiffness, n, step)
        base[:, n : n + step] = 0.5 * (state[:, n : n + step] + field[:, n : n + step]) + 0.5 * time_step * volume
    own_part(columns, traces, partial)


def direct_pieces(got, near, far, arrived):
    capacity = arrived.shape[0] // 5
    at = 6 * capacity
    core = lax.axis_index("pair")

    def mine(ref, start):
        return ref[pl.ds(pl.multiple_of(start + core * capacity, capacity), capacity), :]

    blocks = [
        got[at : at + capacity, :],
        mine(near, at),
        mine(near, at + 2 * capacity),
        mine(far, 0),
        far[2 * capacity : 3 * capacity, :],
    ]
    for i, block in enumerate(blocks):
        arrived[capacity * i : capacity * i + capacity, :] = block
    return arrived[...]


def in_both(pieces, which):
    half = jnp.where(lanes(pieces.shape) < 64, 0, 1)
    kept = jnp.where(half == which, pieces.astype(f32), 0.0)
    return kept + pltpu.roll(kept, 64, 1)


def direct_pairs(got, near, far, arrived):
    capacity = arrived.shape[0] // 5
    at = 6 * capacity
    core = lax.axis_index("pair")
    blocks = [
        (got[at : at + capacity, :], 0),
        (near[0:capacity, :], core),
        (near[capacity : 2 * capacity, :], core),
        (far[0:capacity, :], core),
        (far[capacity : 2 * capacity, :], 1),
    ]
    for i, (block, which) in enumerate(blocks):
        arrived[capacity * i : capacity * i + capacity, :] = in_both(block, which)
    return arrived[...]


def targets(pieces, elements):
    face_of = jnp.where(rows_of((128, 128)) == 66, 1.0, 0.0).astype(bf16)
    face = dot(pieces, face_of) - 1.0
    lane = lanes((8, 128))
    element_of = jnp.where(lane == 64, 16.0, jnp.where(lane == 65, 1.0, 0.0)).astype(bf16)
    target = lax.dot_general(element_of, pieces, (((1,), (1,)), ((), ())), preferred_element_type=f32)[0:1, :]
    match = rows_of((elements, pieces.shape[0])) == target.astype(jnp.int32)
    return face, jnp.where(match, 1.0, 0.0).astype(bf16)


def mortar_sum(both, face, element_hot):
    half = jnp.where(lanes(both.shape) < 64, 0.0, 1.0)
    placed = [jnp.where(half + 2 * t == face, both, 0.0).astype(bf16) for t in range(3)]
    return dot(element_hot, jnp.concatenate(placed, axis=1))


def add_direct(picks, partial, got, near, both, face, element_hot, total):
    rim = picks.shape[1] // 12
    mortar = mortar_sum(both, face, element_hot)
    for t in range(3):
        cut = slice(128 * t, 128 * t + 128)
        rows = slice(rim * t, rim * t + rim)
        window = jnp.concatenate([got[rows, :], near[rows, :]], axis=0)
        conforming = dot(picks[:, 4 * rim * t : 4 * rim * t + 4 * rim], swapped(window))
        total[:, cut] = partial[:, cut] + conforming + mortar[:, cut]


def direct_kernel(picks, partial, got, near, far, last, total, face_out, element_hot_out, arrived):
    pieces = direct_pieces(got, near, far, arrived)
    face, element_hot = targets(pieces, partial.shape[0])
    face_out[...] = face
    element_hot_out[...] = element_hot
    add_direct(picks, partial, got, near, in_both(pieces, 0), face, element_hot, total)


def second_direct_kernel(picks, partial, face, element_hot, got, rim, near, far, last, total, arrived):
    both = direct_pairs(got, near, far, arrived)
    add_direct(picks, partial, got, rim, both, face[...], element_hot[...], total)


def fluxes(both, face, element_hot, partial, inflow):
    return (inflow[...] * (partial[...] + mortar_sum(both, face, element_hot))).astype(bf16)


def middle_kernel(
    lift, base, partial, inflow, last, trace_map, projection, source_hot, column,
    field, traces, first_out, rim_out, own_out, face_out, element_hot_out, blocks
):
    elements = base.shape[0]
    pieces = last[0 : face_out.shape[0], :]
    face, element_hot = targets(pieces, elements)
    face_out[...] = face
    element_hot_out[...] = element_hot
    flux = fluxes(in_both(pieces, 0), face, element_hot, partial, inflow)
    new = base[...] + time_step * dot(flux, lift[...])
    field[...] = new
    traces[...] = dot(new.astype(bf16), trace_map[...]).astype(bf16)
    send(traces, source_hot[...], column, projection, first_out, rim_out, own_out, blocks, False)


def end_kernel(lift, base, partial, inflow, last, face, element_hot, field, result, sems):
    elements = base.shape[0]
    both = in_both(last[0 : face.shape[0], :], lax.axis_index("pair"))
    flux = fluxes(both, face[...], element_hot[...], partial, inflow)
    part = elements // 4
    copies = []
    for i in range(4):
        cut = slice(part * i, part * i + part)
        result[cut, :] = base[cut, :] + 0.5 * time_step * dot(flux[cut, :], lift[...])
        rows = pl.ds(part * i, part)
        copies.append(pltpu.make_async_copy(result.at[rows], field.at[rows], sems.at[i]))
        copies[i].start()
    for copy in copies:
        copy.wait()


def paired(groups, count, step, lower):
    partner = {}
    for s in range(count):
        if lower(s) and s + step < count:
            partner[s] = s + step
            partner[s + step] = s
    pairs = []
    for g in range(groups):
        for s in range(count):
            if s in partner:
                pairs.append((g * count + s, g * count + partner[s]))
            elif g ^ 1 < groups:
                pairs.append((g * count + s, (g ^ 1) * count + s))
    return pairs


def call(kernel, out_shape, scratch, flops, far, near, out_space=pltpu.VMEM):
    operands = [pltpu.with_memory_space_constraint(x, pltpu.HBM) for x in far] + list(near)
    read = sum(x.size * x.dtype.itemsize for x in operands) if flops > 10**8 else 10**5
    specs = [pl.BlockSpec(memory_space=pl.ANY)] * len(far) + [pl.BlockSpec(memory_space=pltpu.VMEM)] * len(near)
    return pl.pallas_call(
        kernel,
        out_shape=out_shape,
        in_specs=specs,
        out_specs=[pl.BlockSpec(memory_space=out_space)] * len(out_shape),
        scratch_shapes=scratch,
        compiler_params=pltpu.CompilerParams(vmem_limit_bytes=16 * 1024 * 1024),
        cost_estimate=pl.CostEstimate(flops=flops, bytes_accessed=read, transcendentals=0),
    )(*operands)


def exchange(first, rim, own, core, capacity, local, direct):
    axes = ("groups",) + CURVE
    groups, count = lax.axis_size("groups"), lax.axis_size(CURVE)
    cores = paired(groups, count, 1, lambda s: s % 2 == 0)
    chips = paired(groups, count, 1, lambda s: s % 2 == 1)
    far_chips = paired(groups, count, 3, lambda s: s % 2 == 1)
    got = lax.ppermute(first, axes, cores)
    with_codes = rim is None
    at = own.shape[0] - 4 * capacity if with_codes else 0

    def either(x, at_first, at_second):
        return jnp.where(core == 0, x[at_first : at_first + capacity], x[at_second : at_second + capacity])

    if with_codes:
        near = jnp.concatenate([own[: at + 2 * capacity], got[at + capacity : at + 3 * capacity]], axis=0)
        far = jnp.concatenate([own[at + 2 * capacity :], got[at + 3 * capacity :]], axis=0)
    else:
        rim = lax.ppermute(rim, axes, chips)
        theirs = got.shape[0] - 2 * capacity
        near = jnp.concatenate([own[:capacity], got[theirs + capacity :]], axis=0)
        far = jnp.concatenate([own[capacity:], got[theirs : theirs + capacity]], axis=0)
    near = lax.ppermute(near, axes, chips)
    far = lax.ppermute(far, axes, far_chips)
    *results, token = local(got)
    if with_codes:
        parts = [either(near, at + capacity, at + 2 * capacity), either(near, at + 3 * capacity, at)]
        parts += [either(far, capacity, 0), either(far, 0, capacity)]
    else:
        parts = [either(near, at, at + capacity), either(near, at + capacity, at), far[:capacity]]
    last = jnp.concatenate(parts + [token], axis=0)
    arrived = (got, near, far) if with_codes else (got, rim, near, far)
    totals = direct(results, *arrived, last)
    return lax.ppermute(last, axes, cores), totals, results


def body(
    state, velocity, levels, neighbours, records, counts, stiffness, trace_map, lift, projection
):
    elements, modes = state.shape
    width = trace_map.shape[1]
    slots = records.shape[1]
    capacity = slots // counts.shape[1]
    rim = elements // 8
    core = lax.axis_index("pair")

    def array(shape, dtype):
        return jax.ShapeDtypeStruct(shape, dtype)

    def like(x):
        return array(x.shape, x.dtype)

    message = array((3 * rim + 4 * capacity, 128), bf16)
    sent = [array((elements, width), bf16), message, message]
    second_sent = [
        array((elements, width), bf16),
        array((3 * rim + 2 * capacity, 128), bf16),
        array((3 * rim, 128), bf16),
        array((2 * capacity, 128), bf16),
    ]
    whole = array((elements, modes), f32)
    faces = array((elements, width), f32)
    blocks = pltpu.VMEM((slots, 128), bf16)
    column_shape = array((slots, 128), f32)
    mark = array((16, 128), bf16)

    levels = levels.reshape(1, elements)
    vmem = pltpu.VMEM
    wide = (elements, 128)
    near_state, trace_map, projection, traces, first, own, source_hot, column, element_column = call(
        start_kernel,
        [like(state), like(trace_map), like(projection)]
        + sent
        + [array((slots, elements), bf16), column_shape, array(wide, f32)],
        [vmem(x.shape, x.dtype) for x in (records, counts, velocity, levels, neighbours)]
        + [blocks, pltpu.SemaphoreType.DMA((9,))],
        2 * 10**8,
        (state, trace_map, records, counts, velocity, levels, neighbours, projection),
        (),
    )

    partial = call(own_kernel, [faces], [], 10**8, (), (element_column, traces))[0]

    def local(got):
        return call(
            local_kernel,
            [like(stiffness), like(lift), whole, faces, array((elements, 12 * rim), bf16), mark],
            [pltpu.SemaphoreType.DMA((2,))],
            10**8,
            (stiffness, lift),
            (element_column, near_state, got),
        )

    def direct(results, *arrived):
        return call(
            direct_kernel,
            [faces, array((5 * capacity, 128), f32), array((elements, 5 * capacity), bf16)],
            [vmem((5 * capacity, 128), bf16)],
            10**9,
            (),
            (results[4], partial, *arrived),
        )

    last, (partial, *direct_targets), (stiffness, lift, base, inflow, picks) = exchange(
        first, None, own, core, capacity, local, direct
    )
    field, traces, first, rims, own, face, element_hot = call(
        middle_kernel,
        [whole] + second_sent + [array((3 * capacity, 128), f32), array((elements, 3 * capacity), bf16)],
        [blocks],
        10**9,
        (),
        (lift, base, partial, inflow, last, trace_map, projection, source_hot, column),
    )

    def second_local(got):
        return call(
            second_local_kernel,
            [whole, faces, mark],
            [],
            10**8,
            (),
            (element_column, state, field, stiffness, traces, got),
        )

    def second_direct(results, *arrived):
        return call(
            second_direct_kernel,
            [faces],
            [vmem((5 * capacity, 128), f32)],
            10**9,
            (),
            (picks, results[1], *direct_targets, *arrived),
        )

    last, (partial,), (base, _) = exchange(
        first, rims, own, core, capacity, second_local, second_direct
    )
    return call(
        end_kernel,
        [whole],
        [vmem((elements, modes), f32), pltpu.SemaphoreType.DMA((4,))],
        10**9,
        (),
        (lift, base, partial, inflow, last, face, element_hot),
        out_space=pl.ANY,
    )[0]


def solution(mesh):
    placed = (
        P(("groups", "curve", "sub", "pair"), None),
        P(None, ("groups", "curve", "sub", "pair")),
        P(("groups", "curve", "sub", "pair")),
        P(None, ("groups", "curve", "sub", "pair")),
        P(None, ("groups", "curve", "sub", "pair")),
        P(("groups", "curve", "sub", "pair"), None),
        P(),
        P(),
        P(),
        P(),
    )
    return jax.shard_map(
        body,
        mesh=mesh,
        in_specs=placed,
        out_specs=P(("groups", "curve", "sub", "pair"), None),
        check_vma=False,
    )
```

```python
import jax
import jax.numpy as jnp
from jax import lax
from jax.experimental import pallas as pl
from jax.experimental.pallas import tpu as pltpu
from jax.sharding import PartitionSpec as P

time_step = 0.3
bf16 = jnp.bfloat16
f32 = jnp.float32
CURVE = ("curve", "sub", "pair")


def dot(a, b):
    return jnp.dot(a, b, preferred_element_type=f32)


def transposed(rows):
    pad = jnp.zeros((128 - rows.shape[0], rows.shape[1]), f32)
    return jnp.concatenate([rows, pad], axis=0).T


def lanes(shape):
    return lax.broadcasted_iota(jnp.int32, shape, 1)


def rows_of(shape):
    return lax.broadcasted_iota(jnp.int32, shape, 0)


def swapped(tile):
    turned = pltpu.roll(tile.astype(f32), 64, 1)
    low = lanes(turned.shape) < 64
    top = jnp.where(low, turned, 0.0).astype(bf16)
    bottom = jnp.where(low, 0.0, turned).astype(bf16)
    return jnp.concatenate([top, bottom], axis=0)


def hot(column, width):
    rows = column.shape[0]
    picked = column.astype(jnp.int32) == lanes((rows, width))
    return jnp.where(picked, 1.0, 0.0).astype(bf16)


def place():
    return lax.axis_index("curve") * lax.axis_size("sub") + lax.axis_index("sub"), lax.axis_index("pair")


def record_columns(records, counts):
    slots = records.shape[1]
    capacity = slots // 8
    source, face, kind, target = (records[i : i + 1, :] for i in range(4))
    slot = lanes((1, slots))
    allowed = jnp.zeros((1, slots), jnp.int32)
    for j in range(8):
        inside = (slot >= j * capacity) & (slot < (j + 1) * capacity)
        allowed = jnp.where(inside, counts[:, j : j + 1] + j * capacity, allowed)
    facing = jnp.where(slot < allowed, jnp.bitwise_xor(face, 1) + 1, 0)
    digits = [lax.shift_right_logical(target, 4), jnp.bitwise_and(target, 15), facing]
    gap = jnp.zeros((61, slots), f32)
    rows = [x.astype(f32) for x in (source, face, kind)] + [gap] + [x.astype(f32) for x in digits]
    return transposed(jnp.concatenate(rows, axis=0))


def send(traces, source_hot, column, projection, first_out, rim_out, own_out, blocks, with_codes):
    elements, width = traces.shape
    slots = column.shape[0]
    capacity = slots // 8
    rim = elements // 8
    core = lax.axis_index("pair")
    shape = (slots, 128)
    lane = lanes(shape)
    half = jnp.where(lane < 64, 0.0, 1.0)
    picked = dot(source_hot, traces[...])
    face = column[:, 1:2]
    row = jnp.zeros(shape, f32)
    for t in range(3):
        row = jnp.where(half + 2 * t == face, picked[:, 128 * t : 128 * t + 128], row)
    every = dot(row.astype(bf16), jnp.concatenate([projection[...]] * 2, axis=0))
    kind = column[:, 2:3]
    folded = jnp.zeros(shape, f32)
    for t in range(4):
        folded = jnp.where(half + 2 * t == kind, every[:, 128 * t : 128 * t + 128], folded)
    piece = folded + pltpu.roll(folded, 64, 1)
    if with_codes:
        piece = jnp.where(lane < 64, piece, column[...])
    blocks[...] = piece.astype(bf16)

    def block(at_first, at_second):
        index = at_first + core * (at_second - at_first)
        return blocks[pl.ds(pl.multiple_of(index * capacity, capacity), capacity), :]

    final_at = pl.multiple_of((1 - core) * (elements - rim), rim)
    other_at = pl.multiple_of(core * (elements - rim), rim)
    for t in range(3):
        cut = slice(128 * t, 128 * t + 128)
        rows = slice(rim * t, rim * t + rim)
        first_out[rows, :] = traces[pl.ds(final_at, rim), cut]
        rim_out[rows, :] = traces[pl.ds(other_at, rim), cut]
    at = 3 * rim
    there = [(4, 3), (5, 1), (6, 2), (7, 0)]
    here = [(2, 4), (3, 5), (0, 6), (1, 7)]
    if with_codes:
        for i in range(4):
            rows = slice(at + capacity * i, at + capacity * i + capacity)
            first_out[rows, :] = block(*there[i])
            own_out[rows, :] = block(*here[i])
        return
    low = lanes((capacity, 128)) < 64

    def pair(a, b):
        return jnp.where(low, block(*a), block(*b))

    first_out[at : at + capacity, :] = pair(there[0], there[3])
    first_out[at + capacity :, :] = pair(there[1], there[2])
    own_out[0:capacity, :] = pair(here[0], here[1])
    own_out[capacity:, :] = pair(here[2], here[3])


def start_kernel(
    state_in, trace_map_in, records_in, counts_in, velocity_in, levels_in, neighbours_in, projection_in,
    state, trace_map, projection, traces, first_out, own_out, source_hot, column, elements_column, local,
    records, counts, velocity, levels, neighbours, blocks, sems
):
    elements = state.shape[0]
    part = elements // 2
    pairs = [(records_in, records), (counts_in, counts), (velocity_in, velocity), (levels_in, levels)]
    pairs += [(neighbours_in, neighbours), (trace_map_in, trace_map)]
    for i in range(2):
        cut = pl.ds(i * part, part)
        pairs.append((state_in.at[cut], state.at[cut]))
    pairs.append((projection_in, projection))
    copies = [pltpu.make_async_copy(a, b, sems.at[i]) for i, (a, b) in enumerate(pairs)]
    for copy in copies:
        copy.start()
    for copy in copies[:5]:
        copy.wait()
    columns = record_columns(records, counts)
    column[...] = columns
    source_hot[...] = hot(columns[:, 0:1], elements)
    elements_column[...] = element_columns(velocity, levels, neighbours, local)
    copies[5].wait()
    for i in range(2):
        copies[6 + i].wait()
        cut = slice(i * part, i * part + part)
        traces[cut, :] = dot(state[cut, :].astype(bf16), trace_map[...]).astype(bf16)
    copies[8].wait()
    send(traces, source_hot[...], column, projection, first_out, own_out, own_out, blocks, True)


def element_columns(velocity, levels, neighbours, local_out):
    elements = velocity.shape[1]
    rim = elements // 8
    chip, core = place()
    raw = neighbours[...].astype(f32)
    local = raw - ((2 * chip + core) * elements).astype(f32)
    local_out[0:6, :] = local
    local_out[6:, :] = jnp.zeros((2, elements), f32)
    before = ((2 - core) * rim).astype(f32)
    after = (elements - core * rim).astype(f32)
    index = jnp.where(local < 0, local + before, jnp.where(local >= elements, local - after, -1.0))
    index = jnp.where(raw < 0, -1.0, index)
    scale = jnp.exp2(levels[...].astype(f32)) * 0.25
    gap = jnp.zeros((4, elements), f32)
    return transposed(jnp.concatenate([velocity[...], scale, gap, local, gap[0:2], index], axis=0))


def volume_term(column, lowered, stiffness, n, step):
    modes = stiffness.shape[0]
    volume = jnp.zeros((lowered.shape[0], step), f32)
    for d in range(3):
        volume += column[:, d : d + 1] * dot(lowered, stiffness[:, d * modes + n : d * modes + n + step])
    return column[:, 3:4] * volume


def own_part(local, traces, partial):
    elements = traces.shape[0]
    element = rows_of((elements, elements))
    for t in range(3):
        tile = traces[:, 128 * t : 128 * t + 128].astype(f32)
        turned = tile.T.astype(bf16)
        parts = []
        for i in range(2):
            face = 2 * t + i
            picked = jnp.where(element == local[face : face + 1, :].astype(jnp.int32), 1.0, 0.0).astype(bf16)
            parts.append(dot(turned[64 - 64 * i : 128 - 64 * i, :], picked))
        near = jnp.concatenate(parts, axis=0).astype(bf16).T
        partial[:, 128 * t : 128 * t + 128] = near.astype(f32) - tile


def own_kernel(local, traces, partial):
    own_part(local, traces, partial)


def local_kernel(stiffness_in, lift_in, column, state, got, stiffness, lift, base, inflow, picks, token, sems):
    token[...] = got[0:16, :]
    elements, modes = state.shape
    rim = elements // 8
    copies = [
        pltpu.make_async_copy(stiffness_in, stiffness, sems.at[0]),
        pltpu.make_async_copy(lift_in, lift, sems.at[1]),
    ]
    copies[0].start()
    columns = column[...]
    low = lanes((elements, 128)) < 64
    for t in range(3):
        speed = columns[:, t : t + 1]
        inflow[:, 128 * t : 128 * t + 128] = columns[:, 3:4] * jnp.maximum(jnp.where(low, speed, -speed), 0.0)
    for i in range(6):
        picks[:, 2 * rim * i : 2 * rim * i + 2 * rim] = hot(columns[:, 16 + i : 17 + i], 2 * rim)
    lowered = state[...].astype(bf16)
    step = 256
    copies[0].wait()
    copies[1].start()
    for n in range(0, modes, step):
        base[:, n : n + step] = state[:, n : n + step] + time_step * volume_term(columns, lowered, stiffness, n, step)
    copies[1].wait()


def second_local_kernel(column, local, state, field, stiffness, traces, got, base, partial, token):
    token[...] = got[0:16, :]
    modes = state.shape[1]
    columns = column[...]
    lowered = field[...].astype(bf16)
    step = 256
    for n in range(0, modes, step):
        volume = volume_term(columns, lowered, stiffness, n, step)
        base[:, n : n + step] = 0.5 * (state[:, n : n + step] + field[:, n : n + step]) + 0.5 * time_step * volume
    own_part(local, traces, partial)


def direct_pieces(got, near, far, arrived):
    capacity = arrived.shape[0] // 5
    at = 6 * capacity
    core = lax.axis_index("pair")

    def mine(ref, start):
        return ref[pl.ds(pl.multiple_of(start + core * capacity, capacity), capacity), :]

    blocks = [
        got[at : at + capacity, :],
        mine(near, at),
        mine(near, at + 2 * capacity),
        mine(far, 0),
        far[2 * capacity : 3 * capacity, :],
    ]
    for i, block in enumerate(blocks):
        arrived[capacity * i : capacity * i + capacity, :] = block
    return arrived[...]


def in_both(pieces, which):
    half = jnp.where(lanes(pieces.shape) < 64, 0, 1)
    kept = jnp.where(half == which, pieces.astype(f32), 0.0)
    return kept + pltpu.roll(kept, 64, 1)


def direct_pairs(got, near, far, arrived):
    capacity = arrived.shape[0] // 5
    at = 6 * capacity
    core = lax.axis_index("pair")
    blocks = [
        (got[at : at + capacity, :], 0),
        (near[0:capacity, :], core),
        (near[capacity : 2 * capacity, :], core),
        (far[0:capacity, :], core),
        (far[capacity : 2 * capacity, :], 1),
    ]
    for i, (block, which) in enumerate(blocks):
        arrived[capacity * i : capacity * i + capacity, :] = in_both(block, which)
    return arrived[...]


def targets(pieces, elements):
    face_of = jnp.where(rows_of((128, 128)) == 66, 1.0, 0.0).astype(bf16)
    face = dot(pieces, face_of) - 1.0
    lane = lanes((8, 128))
    element_of = jnp.where(lane == 64, 16.0, jnp.where(lane == 65, 1.0, 0.0)).astype(bf16)
    target = lax.dot_general(element_of, pieces, (((1,), (1,)), ((), ())), preferred_element_type=f32)[0:1, :]
    match = rows_of((elements, pieces.shape[0])) == target.astype(jnp.int32)
    return face, jnp.where(match, 1.0, 0.0).astype(bf16)


def mortar_sum(both, face, element_hot):
    half = jnp.where(lanes(both.shape) < 64, 0.0, 1.0)
    placed = [jnp.where(half + 2 * t == face, both, 0.0).astype(bf16) for t in range(3)]
    return dot(element_hot, jnp.concatenate(placed, axis=1))


def add_direct(picks, partial, got, near, both, face, element_hot, total):
    rim = picks.shape[1] // 12
    mortar = mortar_sum(both, face, element_hot)
    for t in range(3):
        cut = slice(128 * t, 128 * t + 128)
        rows = slice(rim * t, rim * t + rim)
        window = jnp.concatenate([got[rows, :], near[rows, :]], axis=0)
        conforming = dot(picks[:, 4 * rim * t : 4 * rim * t + 4 * rim], swapped(window))
        total[:, cut] = partial[:, cut] + conforming + mortar[:, cut]


def direct_kernel(picks, partial, got, near, far, last, total, face_out, element_hot_out, arrived):
    pieces = direct_pieces(got, near, far, arrived)
    face, element_hot = targets(pieces, partial.shape[0])
    face_out[...] = face
    element_hot_out[...] = element_hot
    add_direct(picks, partial, got, near, in_both(pieces, 0), face, element_hot, total)


def second_direct_kernel(picks, partial, face, element_hot, got, rim, near, far, last, total, arrived):
    both = direct_pairs(got, near, far, arrived)
    add_direct(picks, partial, got, rim, both, face[...], element_hot[...], total)


def fluxes(both, face, element_hot, partial, inflow):
    return (inflow[...] * (partial[...] + mortar_sum(both, face, element_hot))).astype(bf16)


def middle_kernel(
    lift, base, partial, inflow, last, trace_map, projection, source_hot, column,
    field, traces, first_out, rim_out, own_out, face_out, element_hot_out, blocks
):
    elements = base.shape[0]
    pieces = last[0 : face_out.shape[0], :]
    face, element_hot = targets(pieces, elements)
    face_out[...] = face
    element_hot_out[...] = element_hot
    flux = fluxes(in_both(pieces, 0), face, element_hot, partial, inflow)
    new = base[...] + time_step * dot(flux, lift[...])
    field[...] = new
    traces[...] = dot(new.astype(bf16), trace_map[...]).astype(bf16)
    send(traces, source_hot[...], column, projection, first_out, rim_out, own_out, blocks, False)


def end_kernel(lift, base, partial, inflow, last, face, element_hot, field, result, sems):
    elements = base.shape[0]
    both = in_both(last[0 : face.shape[0], :], lax.axis_index("pair"))
    flux = fluxes(both, face[...], element_hot[...], partial, inflow)
    part = elements // 4
    copies = []
    for i in range(4):
        cut = slice(part * i, part * i + part)
        result[cut, :] = base[cut, :] + 0.5 * time_step * dot(flux[cut, :], lift[...])
        rows = pl.ds(part * i, part)
        copies.append(pltpu.make_async_copy(result.at[rows], field.at[rows], sems.at[i]))
        copies[i].start()
    for copy in copies:
        copy.wait()


def paired(groups, count, step, lower):
    partner = {}
    for s in range(count):
        if lower(s) and s + step < count:
            partner[s] = s + step
            partner[s + step] = s
    pairs = []
    for g in range(groups):
        for s in range(count):
            if s in partner:
                pairs.append((g * count + s, g * count + partner[s]))
            elif g ^ 1 < groups:
                pairs.append((g * count + s, (g ^ 1) * count + s))
    return pairs


def call(kernel, out_shape, scratch, flops, far, near, out_space=pltpu.VMEM):
    operands = [pltpu.with_memory_space_constraint(x, pltpu.HBM) for x in far] + list(near)
    read = sum(x.size * x.dtype.itemsize for x in operands) if flops > 10**8 else 10**5
    specs = [pl.BlockSpec(memory_space=pl.ANY)] * len(far) + [pl.BlockSpec(memory_space=pltpu.VMEM)] * len(near)
    return pl.pallas_call(
        kernel,
        out_shape=out_shape,
        in_specs=specs,
        out_specs=[pl.BlockSpec(memory_space=out_space)] * len(out_shape),
        scratch_shapes=scratch,
        compiler_params=pltpu.CompilerParams(vmem_limit_bytes=16 * 1024 * 1024),
        cost_estimate=pl.CostEstimate(flops=flops, bytes_accessed=read, transcendentals=0),
    )(*operands)


def exchange(first, rim, own, core, capacity, local, direct):
    axes = ("groups",) + CURVE
    groups, count = lax.axis_size("groups"), lax.axis_size(CURVE)
    cores = paired(groups, count, 1, lambda s: s % 2 == 0)
    chips = paired(groups, count, 1, lambda s: s % 2 == 1)
    far_chips = paired(groups, count, 3, lambda s: s % 2 == 1)
    got = lax.ppermute(first, axes, cores)
    with_codes = rim is None
    at = own.shape[0] - 4 * capacity if with_codes else 0

    def either(x, at_first, at_second):
        return jnp.where(core == 0, x[at_first : at_first + capacity], x[at_second : at_second + capacity])

    if with_codes:
        near = jnp.concatenate([own[: at + 2 * capacity], got[at + capacity : at + 3 * capacity]], axis=0)
        far = jnp.concatenate([own[at + 2 * capacity :], got[at + 3 * capacity :]], axis=0)
    else:
        rim = lax.ppermute(rim, axes, chips)
        theirs = got.shape[0] - 2 * capacity
        near = jnp.concatenate([own[:capacity], got[theirs + capacity :]], axis=0)
        far = jnp.concatenate([own[capacity:], got[theirs : theirs + capacity]], axis=0)
    near = lax.ppermute(near, axes, chips)
    far = lax.ppermute(far, axes, far_chips)
    *results, token = local(got)
    if with_codes:
        parts = [either(near, at + capacity, at + 2 * capacity), either(near, at + 3 * capacity, at)]
        parts += [either(far, capacity, 0), either(far, 0, capacity)]
    else:
        parts = [either(near, at, at + capacity), either(near, at + capacity, at), far[:capacity]]
    last = jnp.concatenate(parts + [token], axis=0)
    arrived = (got, near, far) if with_codes else (got, rim, near, far)
    totals = direct(results, *arrived, last)
    return lax.ppermute(last, axes, cores), totals, results


def body(
    state, velocity, levels, neighbours, records, counts, stiffness, trace_map, lift, projection
):
    elements, modes = state.shape
    width = trace_map.shape[1]
    slots = records.shape[1]
    capacity = slots // counts.shape[1]
    rim = elements // 8
    core = lax.axis_index("pair")

    def array(shape, dtype):
        return jax.ShapeDtypeStruct(shape, dtype)

    def like(x):
        return array(x.shape, x.dtype)

    message = array((3 * rim + 4 * capacity, 128), bf16)
    sent = [array((elements, width), bf16), message, message]
    second_sent = [
        array((elements, width), bf16),
        array((3 * rim + 2 * capacity, 128), bf16),
        array((3 * rim, 128), bf16),
        array((2 * capacity, 128), bf16),
    ]
    whole = array((elements, modes), f32)
    faces = array((elements, width), f32)
    blocks = pltpu.VMEM((slots, 128), bf16)
    column_shape = array((slots, 128), f32)
    mark = array((16, 128), bf16)

    levels = levels.reshape(1, elements)
    vmem = pltpu.VMEM
    wide = (elements, 128)
    near_state, trace_map, projection, traces, first, own, source_hot, column, element_column, local_rows = call(
        start_kernel,
        [like(state), like(trace_map), like(projection)]
        + sent
        + [array((slots, elements), bf16), column_shape, array(wide, f32), array((8, elements), f32)],
        [vmem(x.shape, x.dtype) for x in (records, counts, velocity, levels, neighbours)]
        + [blocks, pltpu.SemaphoreType.DMA((9,))],
        2 * 10**8,
        (state, trace_map, records, counts, velocity, levels, neighbours, projection),
        (),
    )

    partial = call(own_kernel, [faces], [], 10**8, (), (local_rows, traces))[0]

    def local(got):
        return call(
            local_kernel,
            [like(stiffness), like(lift), whole, faces, array((elements, 12 * rim), bf16), mark],
            [pltpu.SemaphoreType.DMA((2,))],
            10**8,
            (stiffness, lift),
            (element_column, near_state, got),
        )

    def direct(results, *arrived):
        return call(
            direct_kernel,
            [faces, array((5 * capacity, 128), f32), array((elements, 5 * capacity), bf16)],
            [vmem((5 * capacity, 128), bf16)],
            10**9,
            (),
            (results[4], partial, *arrived),
        )

    last, (partial, *direct_targets), (stiffness, lift, base, inflow, picks) = exchange(
        first, None, own, core, capacity, local, direct
    )
    field, traces, first, rims, own, face, element_hot = call(
        middle_kernel,
        [whole] + second_sent + [array((3 * capacity, 128), f32), array((elements, 3 * capacity), bf16)],
        [blocks],
        10**9,
        (),
        (lift, base, partial, inflow, last, trace_map, projection, source_hot, column),
    )

    def second_local(got):
        return call(
            second_local_kernel,
            [whole, faces, mark],
            [],
            10**8,
            (),
            (element_column, local_rows, state, field, stiffness, traces, got),
        )

    def second_direct(results, *arrived):
        return call(
            second_direct_kernel,
            [faces],
            [vmem((5 * capacity, 128), f32)],
            10**9,
            (),
            (picks, results[1], *direct_targets, *arrived),
        )

    last, (partial,), (base, _) = exchange(
        first, rims, own, core, capacity, second_local, second_direct
    )
    return call(
        end_kernel,
        [whole],
        [vmem((elements, modes), f32), pltpu.SemaphoreType.DMA((4,))],
        10**9,
        (),
        (lift, base, partial, inflow, last, face, element_hot),
        out_space=pl.ANY,
    )[0]


def solution(mesh):
    placed = (
        P(("groups", "curve", "sub", "pair"), None),
        P(None, ("groups", "curve", "sub", "pair")),
        P(("groups", "curve", "sub", "pair")),
        P(None, ("groups", "curve", "sub", "pair")),
        P(None, ("groups", "curve", "sub", "pair")),
        P(("groups", "curve", "sub", "pair"), None),
        P(),
        P(),
        P(),
        P(),
    )
    return jax.shard_map(
        body,
        mesh=mesh,
        in_specs=placed,
        out_specs=P(("groups", "curve", "sub", "pair"), None),
        check_vma=False,
    )
```
